32 devices in a mesh: group: 4 (over y, core), dev: 8 (over z, x).
Axes of the slice: x: 2, y: 2, z: 4, core: 2. Of those that a mesh axis runs over, the one named last changes fastest.
Arguments:
- primary_q: bfloat16 [64, 3584, 1024], P(('group', 'dev')), may hold values from -0.09375 to 0.09375
- primary_scales: bfloat16 [64, 28, 8], P(('group', 'dev')), may hold values from 0.5 to 2
- new_place: int32 [32], P(('group', 'dev')), may hold values from 0 to 63, as said below
- tokens: bfloat16 [512, 3584], P(('group', 'dev')), may hold values from -6 to 6
- experts: int32 [512, 8], P(('group', 'dev')), may hold values from 0 to 63, all different within a row
- replica: int32 [512, 8], P(('group', 'dev')), may hold values from 0 to 1
- route_num: int32 [512, 8], P(('group', 'dev')), may hold values from 1 to 16
Outputs:
- new_weights: bfloat16 [32, 3584, 1024], P(('group', 'dev'))
- new_scales: bfloat16 [32, 28, 8], P(('group', 'dev'))
- hidden_out: bfloat16 [512, 8, 1024], P(('group', 'dev'))
- slot_load: int32 [32, 3], P(('group', 'dev'))
The draws below stay inside these ranges and needn't reach their ends.
Inputs may be any that keep to these rules, and one draw needn't show every extreme that they name: `new_place`: the redundant slots of the 8 devices of one group hold 8 different experts, each with its primary copy on a device of that group.
All inputs are finite; a program needn't handle non-finite values.
Results may differ from the reference program's by a relative error of at most 0.0057.
Values may be sent and summed in bfloat16 or wider, within the bound.
No kernel may reach another device: no remote copies, remote signals or barrier semaphores. Data moves between devices by JAX's collectives and lax.ppermute only.
A program may use at most 192 MiB of HBM per device.

```python
import math
import jax
import jax.numpy as jnp
from jax import lax

D = 3584
FF = 1024
TILE = 128
EXP_DEV = 2
TOPK = 8
CAP = 2
ROWS_DEV = 16
EXPERTS = 64
ROWS = 512
N_GROUP = 4
N_DEV = 8


def draw_new_place(key, part):
    group_keys = jax.random.split(jax.random.fold_in(key, 17), N_GROUP)

    def one_group(group_key, group_id):
        chosen = jax.random.permutation(group_key, EXP_DEV * N_DEV)[:N_DEV]
        return chosen + group_id * EXP_DEV * N_DEV
    placed = jax.vmap(one_group)(group_keys, jnp.arange(N_GROUP, dtype=jnp.int32))
    return placed.reshape(N_GROUP * N_DEV).astype(jnp.int32)


def plant(array, stream_key, low, high):
    longest = array.shape.index(max(array.shape))
    spots = []
    for shift in (0, 1):
        where = [jax.random.randint(jax.random.fold_in(stream_key, axis), (), 0, length) for axis, length in enumerate(array.shape)]
        where[longest] = (where[longest] + shift) % array.shape[longest]
        spots.append(tuple(where))
    return array.at[spots[0]].set(low).at[spots[1]].set(high)


def levels(own_key, shape, shards, smallest, largest):
    gain, own = 1.0, jax.random.fold_in(own_key, 6)
    for dim, blocks in shards:
        steps = jnp.exp(jax.random.uniform(jax.random.fold_in(own, dim), (blocks,), jnp.float32, smallest / len(shards), largest / len(shards)))
        gain = gain * jnp.repeat(steps, shape[dim] // blocks).reshape([-1 if axis == dim else 1 for axis in range(len(shape))])
    return gain


def distinct(key, rows, number_of, top, lift):
    ranking = jax.random.permutation(jax.random.fold_in(key, 1), number_of)
    favour = ranking
    for power in range(3):
        favour = favour * favour // number_of
    favour = favour * lift // number_of
    chance = jax.random.randint(jax.random.fold_in(key, 2), (rows, number_of), 0, 4096) + favour
    holders = jax.random.permutation(jax.random.fold_in(key, 3), rows)[jnp.arange(number_of) % rows]
    chance = jnp.where(jnp.arange(rows)[:, None] == holders[None, :], 1 << 14, chance)
    merit = chance * number_of + jnp.arange(number_of)
    return lax.top_k(merit.astype(jnp.int32), top)[1].astype(jnp.int32)


def bell_draw(rng, shape, deviation, most, cuts=(), kind=jnp.bfloat16):
    result = jax.random.normal(rng, shape, jnp.float32) * deviation
    if len(cuts) > 0:
        result = levels(rng, shape, cuts, -0.22, 0.18) * result
    return jnp.clip(result, min=-most, max=most).astype(kind)


def setup_inputs(seed: int = 0) -> dict:
    arg_keys = jax.random.split(jax.random.key(seed), 8)
    return {
        "primary_q": bell_draw(arg_keys[0], (EXPERTS, D, FF), D ** -0.5, 0.09375, ((0, 32),)),
        "primary_scales": jnp.clip(jnp.exp(math.log(2.0) - 1.3862944 * jax.random.uniform(arg_keys[1], (EXPERTS, D // TILE, FF // TILE), jnp.float32) ** levels(arg_keys[1], (EXPERTS, D // TILE, FF // TILE), ((0, 32),), -0.2, 0.2)), 0.5, 2.0).astype(jnp.bfloat16),
        "new_place": draw_new_place(jax.random.fold_in(arg_keys[7], 71), 0),
        "tokens": bell_draw(arg_keys[3], (ROWS, D), 1.0, 6.0, ((0, 32),)),
        "experts": distinct(arg_keys[4], ROWS, EXPERTS, TOPK, 2048),
        "replica": plant(jax.random.randint(arg_keys[5], (ROWS, TOPK), 0, 2), jax.random.fold_in(arg_keys[5], 1), 0, 1).astype(jnp.int32),
        "route_num": plant(jax.random.randint(arg_keys[6], (ROWS, TOPK), 1, 17), jax.random.fold_in(arg_keys[6], 1), 1, 16).astype(jnp.int32),
    }


def dequantize(values, scales):
    tile_grid = values.astype(jnp.float32).reshape(D // TILE, TILE, FF // TILE, TILE)
    scaled = tile_grid * scales.astype(jnp.float32)[:, None, :, None]
    return scaled.reshape(D, FF).astype(jnp.bfloat16)


def reference(primary_q, primary_scales, new_place, tokens, experts, replica, route_num):
    device_count = N_GROUP * N_DEV
    pairs_dev = ROWS_DEV * TOPK
    expert_flat = experts.reshape(-1).astype(jnp.int32)
    pair_total = expert_flat.shape[0]
    holder = jnp.full((EXPERTS,), -1, jnp.int32).at[new_place].set(jnp.arange(device_count, dtype=jnp.int32))
    holder_of = holder[expert_flat]
    use_copy = (replica.reshape(-1) == 1) & (holder_of >= 0)
    target = jnp.where(use_copy, holder_of, expert_flat // EXP_DEV).astype(jnp.int32)
    slot_id = jnp.where(use_copy, EXP_DEV, expert_flat % EXP_DEV).astype(jnp.int32)
    grouped = target.reshape(device_count, pairs_dev)
    is_earlier = jnp.arange(pairs_dev)[None, :] < jnp.arange(pairs_dev)[:, None]
    same_dest = grouped[:, :, None] == grouped[:, None, :]
    position = jnp.sum(same_dest & is_earlier[None], axis=2).astype(jnp.int32).reshape(-1)
    served = position < CAP
    source_dev = (jnp.arange(pair_total, dtype=jnp.int32) // pairs_dev).astype(jnp.int32)
    cell_count = device_count * CAP
    flat_index = (target * cell_count + source_dev * CAP + position).astype(jnp.int32)
    dump_cell = device_count * cell_count
    cell_table = jnp.full((dump_cell + 1,), -1, jnp.int32)
    cell_table = cell_table.at[jnp.where(served, flat_index, dump_cell)].set(jnp.arange(pair_total, dtype=jnp.int32))
    cell_table = cell_table[:dump_cell].reshape(device_count, cell_count)

    def serve_rows(operands):
        device, pair_ids = operands
        is_valid = pair_ids >= 0
        safe_ids = jnp.maximum(pair_ids, 0)
        row_block = jnp.where(is_valid[:, None], tokens[safe_ids // TOPK], jnp.zeros((), tokens.dtype))
        slot_code = jnp.where(is_valid, slot_id[safe_ids], -1)
        matrices = [dequantize(primary_q[device * EXP_DEV + member], primary_scales[device * EXP_DEV + member]) for member in range(EXP_DEV)]
        matrices.append(dequantize(primary_q[new_place[device]], primary_scales[new_place[device]]))
        joined = jnp.concatenate(matrices, axis=1)
        product = jnp.dot(row_block, joined, preferred_element_type=jnp.float32)
        picked = jnp.zeros_like(product[:, :FF])
        for member in range(EXP_DEV + 1):
            picked = picked + jnp.where((slot_code == member)[:, None], product[:, member * FF:(member + 1) * FF], jnp.zeros_like(picked))
        return jax.nn.silu(picked).astype(jnp.bfloat16)

    results = lax.map(serve_rows, (jnp.arange(device_count, dtype=jnp.int32), cell_table))
    gathered = results.reshape(device_count * cell_count, FF)[jnp.where(served, flat_index, 0)]
    selected = jnp.where(served[:, None], gathered.astype(jnp.float32), jnp.zeros((), jnp.float32))
    weight = route_num.reshape(-1).astype(jnp.float32) / 16.0
    hidden_out = (selected * weight[:, None]).astype(jnp.bfloat16).reshape(experts.shape[0], TOPK, FF)
    load_table = jnp.zeros((device_count * (EXP_DEV + 1),), jnp.int32)
    load_table = load_table.at[target * (EXP_DEV + 1) + slot_id].add(served.astype(jnp.int32))
    load_table = load_table.reshape(device_count, EXP_DEV + 1)
    return primary_q[new_place], primary_scales[new_place], hidden_out, load_table
```

```python
import functools

import jax
import jax.numpy as jnp
from jax import lax
from jax.experimental import pallas as pl
from jax.experimental.pallas import tpu as pltpu
from jax.sharding import PartitionSpec as P

TILE = 128
CAP = 2
POOL = 16
AXES = ("group", "dev")
PARTS = (128, 96)


def expert_kernel(x_ref, q_ref, s_ref, o_ref, acc_ref):
    step = pl.program_id(0)

    @pl.when(step == 0)
    def _():
        acc_ref[...] = jnp.zeros_like(acc_ref)

    holding, depth, _ = q_ref.shape
    cells = 2 * CAP
    rows = x_ref.shape[0]
    member_of = lax.broadcasted_iota(jnp.int32, (rows, TILE), 0) // cells % holding
    total = acc_ref[...]
    for member in range(holding):
        for block in range(depth // TILE):
            span = slice(block * TILE, (block + 1) * TILE)
            scale = s_ref[member, 0, block : block + 1, :]
            weights = (q_ref[member, span, :].astype(jnp.float32) * scale).astype(jnp.bfloat16)
            rows_in = jnp.where(member_of == member, x_ref[:, span], jnp.zeros((), jnp.bfloat16))
            total = total + jnp.dot(rows_in, weights, preferred_element_type=jnp.float32)
    acc_ref[...] = total

    @pl.when(step == pl.num_programs(0) - 1)
    def _():
        value = acc_ref[...]
        o_ref[...] = (value / (1.0 + jnp.exp(-value))).astype(jnp.bfloat16)


def serve(rows, values, scales):
    holding, width_in, hidden = values.shape
    depth = 512
    steps = width_in // depth
    count = rows.shape[0]
    wide = jnp.repeat(scales.astype(jnp.float32), TILE, axis=2)
    wide = wide.reshape(holding, steps, depth // TILE, hidden)
    return pl.pallas_call(
        expert_kernel,
        grid=(steps,),
        in_specs=[
            pl.BlockSpec((count, depth), lambda k: (0, k)),
            pl.BlockSpec((holding, depth, hidden), lambda k: (0, k, 0)),
            pl.BlockSpec((holding, 1, depth // TILE, hidden), lambda k: (0, k, 0, 0)),
        ],
        out_specs=pl.BlockSpec((count, hidden), lambda k: (0, 0)),
        out_shape=jax.ShapeDtypeStruct((count, hidden), jnp.bfloat16),
        scratch_shapes=[pltpu.VMEM((count, hidden), jnp.float32)],
        compiler_params=pltpu.CompilerParams(vmem_limit_bytes=48 * 1024 * 1024),
        cost_estimate=pl.CostEstimate(
            flops=2 * count * width_in * hidden * holding,
            bytes_accessed=2 * (values.size + rows.size + count * hidden),
            transcendentals=count * hidden,
        ),
    )(rows, values, wide)


def gather_kernel(count, index_ref, near_ref, far_ref, out_ref, sem):
    near_count = near_ref.shape[0]

    def step(spot, carry):
        index = index_ref[spot]

        @pl.when(index < near_count)
        def _():
            pltpu.make_async_copy(
                near_ref.at[jnp.minimum(index, near_count - 1)], out_ref.at[spot], sem
            ).start()

        @pl.when(index >= near_count)
        def _():
            far_index = jnp.maximum(index - near_count, 0)
            pltpu.make_async_copy(far_ref.at[far_index], out_ref.at[spot], sem).start()

        return carry

    lax.fori_loop(0, count, step, 0)
    pltpu.make_async_copy(out_ref, out_ref, sem).wait()


def gather(indices, near, far):
    count = indices.shape[0]
    anywhere = pl.BlockSpec(memory_space=pl.ANY)
    return pl.pallas_call(
        functools.partial(gather_kernel, count),
        in_specs=[pl.BlockSpec(memory_space=pltpu.SMEM), anywhere, anywhere],
        out_specs=anywhere,
        out_shape=jax.ShapeDtypeStruct((count,) + near.shape[1:], near.dtype),
        scratch_shapes=[pltpu.SemaphoreType.DMA],
    )(indices, near, far)


def cross_over(count, blocks, pairs):
    most = blocks.shape[0]

    def branch_of(size):
        def branch(held):
            if size == 0:
                return jnp.zeros_like(held)
            got = lax.ppermute(held[:size], AXES, pairs)
            return jnp.pad(got, ((0, most - size), (0, 0), (0, 0)))

        return branch

    return lax.switch(count, [branch_of(size) for size in range(most + 1)], blocks)


def per_device(primary_q, primary_scales, new_place, tokens, experts, replica, route_num):
    holding, width_in, hidden = primary_q.shape
    dev_count = lax.axis_size("dev")
    group_count = lax.axis_size("group")
    device_count = dev_count * group_count
    half = dev_count // 2
    pooled = POOL // half
    my_dev = lax.axis_index("dev")
    my_group = lax.axis_index("group")
    first_dev = my_group * dev_count
    pools = [
        [(base + group) * dev_count + side * half + spot for group in range(pooled) for spot in range(half)]
        for base in range(0, group_count, pooled)
        for side in range(2)
    ]
    over = [
        (group * dev_count + spot, group * dev_count + (spot + half) % dev_count)
        for group in range(group_count)
        for spot in range(dev_count)
    ]

    scale_count = primary_scales.size
    notice = jnp.concatenate(
        [primary_scales.reshape(scale_count), new_place.astype(jnp.bfloat16)]
    )
    notice = jnp.pad(notice, (0, -notice.size % TILE))
    notices = lax.all_to_all(
        jnp.broadcast_to(notice[None], (device_count, notice.size)),
        AXES,
        split_axis=0,
        concat_axis=0,
        tiled=True,
    )

    spread = []
    start = 0
    for height in PARTS:
        block = primary_q[:, start : start + POOL * height]
        block = block.reshape(holding, POOL, height, hidden).transpose(1, 0, 2, 3)
        block = lax.all_to_all(
            block, AXES, split_axis=0, concat_axis=0, tiled=True, axis_index_groups=pools
        )
        spread.append(block.reshape(POOL * holding, height, hidden))
        start += POOL * height

    place_all = notices[:, scale_count].astype(jnp.int32)
    nearby = lax.dynamic_slice_in_dim(notices, first_dev, dev_count)
    wanted = lax.dynamic_slice_in_dim(place_all, first_dev, dev_count)
    owner = wanted // holding - first_dev
    member = wanted % holding
    own_scales = lax.dynamic_slice(
        nearby[:, :scale_count].reshape(dev_count * holding, scale_count // holding),
        (owner[my_dev] * holding + member[my_dev], 0),
        (1, scale_count // holding),
    )
    new_scales = own_scales.reshape((1,) + primary_scales.shape[1:])

    row_count, top_count = experts.shape
    pair_count = row_count * top_count
    expert_flat = experts.reshape(pair_count)
    device_ids = jnp.arange(device_count, dtype=jnp.int32)
    matched = expert_flat[:, None] == place_all[None, :]
    has_copy = jnp.any(matched, axis=1)
    holder = jnp.sum(jnp.where(matched, device_ids[None, :], 0), axis=1)
    use_copy = (replica.reshape(pair_count) == 1) & has_copy
    target = jnp.where(use_copy, holder, expert_flat // holding)
    slot_id = jnp.where(use_copy, holding, expert_flat % holding)
    pair_order = jnp.arange(pair_count)
    before = pair_order[None, :] < pair_order[:, None]
    position = jnp.sum((target[:, None] == target[None, :]) & before, axis=1)
    served = position < CAP
    cells = 2 * CAP
    same_expert = (expert_flat[:, None] == expert_flat[None, :]) & before & served[None, :]
    cell_index = expert_flat * cells + jnp.sum(same_expert, axis=1)
    cell_count = device_count * holding * cells
    placed = (cell_index[None, :] == jnp.arange(cell_count)[:, None]) & served[None, :]
    row_hits = jnp.any(placed.reshape(cell_count, row_count, top_count), axis=2)
    row_buffer = jnp.dot(row_hits.astype(jnp.bfloat16), tokens, preferred_element_type=jnp.float32)
    row_buffer = row_buffer.astype(jnp.bfloat16).reshape(device_count, holding * cells, width_in)
    row_block = lax.all_to_all(row_buffer, AXES, split_axis=0, concat_axis=0, tiled=True)

    dest_hit = (target[None, :] == device_ids[:, None]) & served[None, :]
    slot_hit = slot_id[:, None] == jnp.arange(holding + 1)[None, :]
    counted = jnp.dot(
        dest_hit.astype(jnp.bfloat16),
        slot_hit.astype(jnp.bfloat16),
        preferred_element_type=jnp.float32,
    )
    counts = lax.all_to_all(
        counted.astype(jnp.bfloat16), AXES, split_axis=0, concat_axis=0, tiled=True
    )
    slot_load = jnp.sum(counts.astype(jnp.float32), axis=0, keepdims=True).astype(jnp.int32)

    activated = serve(row_block.reshape(cell_count, width_in), primary_q, primary_scales)
    returned = lax.all_to_all(
        activated.reshape(device_count, holding * cells, hidden),
        AXES,
        split_axis=0,
        concat_axis=0,
        tiled=True,
    )
    selected = jnp.dot(
        placed.T.astype(jnp.bfloat16),
        returned.reshape(cell_count, hidden),
        preferred_element_type=jnp.float32,
    )
    weight = route_num.reshape(pair_count).astype(jnp.float32) / 16.0
    hidden_out = (selected * weight[:, None]).astype(jnp.bfloat16)
    hidden_out = hidden_out.reshape(row_count, top_count, hidden)

    source = place_all // holding
    dest_side = device_ids % dev_count // half
    source_side = source % dev_count // half
    crossing = source_side != dest_side
    row_at = (source // dev_count % pooled * half + source % half) * holding + place_all % holding
    pool_of = device_ids // dev_count // pooled
    peers = (pool_of[:, None] == pool_of[None, :]) & (dest_side[:, None] == dest_side[None, :])
    ahead = peers & crossing[None, :] & (device_ids[None, :] < device_ids[:, None])
    rank = jnp.sum(ahead, axis=1)
    cross_count = jnp.max(jnp.where(crossing, rank + 1, 0))
    my_side = my_dev // half
    my_pool = my_group // pooled
    leaving = (pool_of == my_pool) & (dest_side != my_side) & crossing
    slots = jnp.arange(POOL)
    leave_rows = jnp.sum(
        jnp.where(leaving[None, :] & (rank[None, :] == slots[:, None]), row_at[None, :], 0), axis=1
    )
    staying = (pool_of == my_pool) & (dest_side == my_side)
    place_in_pool = device_ids // dev_count % pooled * half + device_ids % half
    give_rows = jnp.sum(
        jnp.where(
            staying[None, :] & (place_in_pool[None, :] == slots[:, None]),
            jnp.where(crossing, POOL * holding + rank, row_at)[None, :],
            0,
        ),
        axis=1,
    )
    pieces = []
    for block in spread:
        arrived = cross_over(cross_count, gather(leave_rows, block, block), over)
        given = gather(give_rows, block, arrived)
        given = lax.all_to_all(
            given, AXES, split_axis=0, concat_axis=0, tiled=True, axis_index_groups=pools
        )
        pieces.append(given.reshape(1, -1, hidden))
    new_weights = jnp.concatenate(pieces, axis=1)
    return (new_weights, new_scales, hidden_out, slot_load)


def solution(mesh):
    in_specs = (
        P(AXES, None, None),
        P(AXES, None, None),
        P(AXES),
        P(AXES, None),
        P(AXES, None),
        P(AXES, None),
        P(AXES, None),
    )
    out_specs = (
        P(AXES, None, None),
        P(AXES, None, None),
        P(AXES, None, None),
        P(AXES, None),
    )
    return jax.shard_map(
        per_device, mesh=mesh, in_specs=in_specs, out_specs=out_specs, check_vma=False
    )
```

```python
import functools

import jax
import jax.numpy as jnp
from jax import lax
from jax.experimental import pallas as pl
from jax.experimental.pallas import tpu as pltpu
from jax.sharding import PartitionSpec as P

TILE = 128
CAP = 2
POOL = 16
AXES = ("group", "dev")
PARTS = (112, 112)


def expert_kernel(x_ref, q_ref, s_ref, o_ref, acc_ref):
    step = pl.program_id(0)

    @pl.when(step == 0)
    def _():
        acc_ref[...] = jnp.zeros_like(acc_ref)

    holding, depth, _ = q_ref.shape
    cells = 2 * CAP
    rows = x_ref.shape[0]
    member_of = lax.broadcasted_iota(jnp.int32, (rows, TILE), 0) // cells % holding
    total = acc_ref[...]
    for member in range(holding):
        for block in range(depth // TILE):
            span = slice(block * TILE, (block + 1) * TILE)
            scale = s_ref[member, 0, block : block + 1, :]
            weights = (q_ref[member, span, :].astype(jnp.float32) * scale).astype(jnp.bfloat16)
            rows_in = jnp.where(member_of == member, x_ref[:, span], jnp.zeros((), jnp.bfloat16))
            total = total + jnp.dot(rows_in, weights, preferred_element_type=jnp.float32)
    acc_ref[...] = total

    @pl.when(step == pl.num_programs(0) - 1)
    def _():
        value = acc_ref[...]
        o_ref[...] = (value / (1.0 + jnp.exp(-value))).astype(jnp.bfloat16)


def serve(rows, values, scales):
    holding, width_in, hidden = values.shape
    depth = 512
    steps = width_in // depth
    count = rows.shape[0]
    wide = jnp.repeat(scales.astype(jnp.float32), TILE, axis=2)
    wide = wide.reshape(holding, steps, depth // TILE, hidden)
    return pl.pallas_call(
        expert_kernel,
        grid=(steps,),
        in_specs=[
            pl.BlockSpec((count, depth), lambda k: (0, k)),
            pl.BlockSpec((holding, depth, hidden), lambda k: (0, k, 0)),
            pl.BlockSpec((holding, 1, depth // TILE, hidden), lambda k: (0, k, 0, 0)),
        ],
        out_specs=pl.BlockSpec((count, hidden), lambda k: (0, 0)),
        out_shape=jax.ShapeDtypeStruct((count, hidden), jnp.bfloat16),
        scratch_shapes=[pltpu.VMEM((count, hidden), jnp.float32)],
        compiler_params=pltpu.CompilerParams(vmem_limit_bytes=48 * 1024 * 1024),
        cost_estimate=pl.CostEstimate(
            flops=2 * count * width_in * hidden * holding,
            bytes_accessed=2 * (values.size + count * (width_in + hidden)),
            transcendentals=count * hidden,
        ),
    )(rows, values, wide)


def gather_kernel(count, index_ref, near_ref, far_ref, out_ref, sem):
    near_count = near_ref.shape[0]

    def step(spot, carry):
        index = index_ref[spot]

        @pl.when(index < near_count)
        def _():
            pltpu.make_async_copy(
                near_ref.at[jnp.minimum(index, near_count - 1)], out_ref.at[spot], sem
            ).start()

        @pl.when(index >= near_count)
        def _():
            far_index = jnp.maximum(index - near_count, 0)
            pltpu.make_async_copy(far_ref.at[far_index], out_ref.at[spot], sem).start()

        return carry

    lax.fori_loop(0, count, step, 0)
    pltpu.make_async_copy(out_ref, out_ref, sem).wait()


def gather(indices, near, far):
    count = indices.shape[0]
    anywhere = pl.BlockSpec(memory_space=pl.ANY)
    return pl.pallas_call(
        functools.partial(gather_kernel, count),
        in_specs=[pl.BlockSpec(memory_space=pltpu.SMEM), anywhere, anywhere],
        out_specs=pl.BlockSpec(memory_space=pltpu.VMEM),
        out_shape=jax.ShapeDtypeStruct((count,) + near.shape[1:], near.dtype),
        scratch_shapes=[pltpu.SemaphoreType.DMA],
    )(indices, near, far)


def copy_kernel(in_ref, out_ref):
    out_ref[0] = in_ref[...]


def by_chunk(values, first, height):
    holding, _, hidden = values.shape
    return pl.pallas_call(
        copy_kernel,
        grid=(POOL,),
        in_specs=[pl.BlockSpec((holding, height, hidden), lambda k: (0, first // height + k, 0))],
        out_specs=pl.BlockSpec((1, holding, height, hidden), lambda k: (k, 0, 0, 0)),
        out_shape=jax.ShapeDtypeStruct((POOL, holding, height, hidden), values.dtype),
    )(values)


def cross_over(count, blocks, pairs):
    most = blocks.shape[0]

    def branch_of(size):
        def branch(held):
            if size == 0:
                return jnp.zeros_like(held)
            got = lax.ppermute(held[:size], AXES, pairs)
            return jnp.pad(got, ((0, most - size), (0, 0), (0, 0)))

        return branch

    return lax.switch(count, [branch_of(size) for size in range(most + 1)], blocks)


def per_device(primary_q, primary_scales, new_place, tokens, experts, replica, route_num):
    holding, width_in, hidden = primary_q.shape
    dev_count = lax.axis_size("dev")
    group_count = lax.axis_size("group")
    device_count = dev_count * group_count
    half = dev_count // 2
    pooled = POOL // half
    my_dev = lax.axis_index("dev")
    my_group = lax.axis_index("group")
    first_dev = my_group * dev_count
    pools = [
        [(base + group) * dev_count + side * half + spot for group in range(pooled) for spot in range(half)]
        for base in range(0, group_count, pooled)
        for side in range(2)
    ]
    over = [
        (group * dev_count + spot, group * dev_count + (spot + half) % dev_count)
        for group in range(group_count)
        for spot in range(dev_count)
    ]

    spread = []
    start = 0
    for height in PARTS:
        block = lax.all_to_all(
            by_chunk(primary_q, start, height), AXES, split_axis=0, concat_axis=0, tiled=True, axis_index_groups=pools
        )
        spread.append(block.reshape(POOL * holding, height, hidden))
        start += POOL * height

    row_count, top_count = experts.shape
    pair_count = row_count * top_count
    scale_cols = primary_scales.size // row_count
    notice = jnp.concatenate(
        [
            experts.astype(jnp.bfloat16),
            replica.astype(jnp.bfloat16),
            jnp.broadcast_to(new_place.astype(jnp.bfloat16)[None], (row_count, 1)),
            primary_scales.reshape(row_count, scale_cols),
        ],
        axis=1,
    )
    notice = jnp.pad(notice, ((0, 0), (0, -notice.shape[1] % TILE)))
    held = jnp.concatenate([tokens, notice], axis=1)
    dev_bits = dev_count.bit_length() - 1
    all_bits = device_count.bit_length() - 1
    order = list(range(dev_bits))[::-1] + list(range(dev_bits, all_bits))[::-1]
    for bit in order:
        pairs = [(device, device ^ 1 << bit) for device in range(device_count)]
        held = jnp.concatenate([held, lax.ppermute(held, AXES, pairs)], axis=0)
    device_ids = jnp.arange(device_count, dtype=jnp.int32)
    my_id = first_dev + my_dev
    apart = device_ids ^ my_id
    spot_of = sum((apart >> bit & 1) << step for step, bit in enumerate(order))

    notices = held[:, width_in:].reshape(device_count, row_count, -1)[spot_of]
    experts_all = notices[:, :, :top_count].astype(jnp.int32).reshape(device_count, pair_count)
    replica_all = notices[:, :, top_count : 2 * top_count].astype(jnp.int32)
    replica_all = replica_all.reshape(device_count, pair_count)
    place_all = notices[:, 0, 2 * top_count].astype(jnp.int32)
    my_place = new_place[0]
    owner_notice = lax.dynamic_index_in_dim(notices, my_place // holding, 0, keepdims=False)
    owner_scales = owner_notice[:, 2 * top_count + 1 : 2 * top_count + 1 + scale_cols]
    new_scales = lax.dynamic_index_in_dim(
        owner_scales.reshape(primary_scales.shape), my_place % holding, 0
    )

    matched = experts_all[:, :, None] == place_all[None, None, :]
    has_copy = jnp.any(matched, axis=2)
    holder = jnp.sum(jnp.where(matched, device_ids[None, None, :], 0), axis=2)
    use_copy = (replica_all == 1) & has_copy
    target = jnp.where(use_copy, holder, experts_all // holding)
    slot_id = jnp.where(use_copy, holding, experts_all % holding)
    pair_order = jnp.arange(pair_count)
    before = pair_order[:, None] < pair_order[None, :]
    position = jnp.sum((target[:, :, None] == target[:, None, :]) & before[None], axis=1)
    served = position < CAP
    arriving = served & (target == my_id)
    slot_load = jnp.stack(
        [jnp.sum((arriving & (slot_id == slot)).astype(jnp.int32)) for slot in range(holding + 1)]
    )[None]

    cells = 2 * CAP
    cell_count = device_count * holding * cells
    cell = experts_all % holding * cells + use_copy * CAP + position
    mine = served & (experts_all // holding == my_id)
    cell_ids = jnp.arange(holding * cells)
    hit = mine[:, None, :] & (cell[:, None, :] == cell_ids[None, :, None])
    row_at = spot_of[:, None] * row_count + jnp.sum(
        jnp.where(hit, pair_order // top_count, 0), axis=2
    )
    row_at = jnp.where(jnp.any(hit, axis=2), row_at, -1).reshape(cell_count)
    row_hits = row_at[:, None] == jnp.arange(device_count * row_count)[None, :]
    row_block = jnp.dot(row_hits.astype(jnp.bfloat16), held, preferred_element_type=jnp.float32)
    activated = serve(row_block.astype(jnp.bfloat16), primary_q, primary_scales)
    returned = lax.all_to_all(
        activated.reshape(device_count, holding * cells, hidden),
        AXES,
        split_axis=0,
        concat_axis=0,
        tiled=True,
    )
    my_cell = (experts_all // holding * (holding * cells) + cell)[my_id]
    placed = (my_cell[:, None] == jnp.arange(cell_count)[None, :]) & served[my_id][:, None]
    selected = jnp.dot(
        placed.astype(jnp.bfloat16),
        returned.reshape(cell_count, hidden),
        preferred_element_type=jnp.float32,
    )
    weight = route_num.reshape(pair_count).astype(jnp.float32) / 16.0
    hidden_out = (selected * weight[:, None]).astype(jnp.bfloat16)
    hidden_out = hidden_out.reshape(row_count, top_count, hidden)

    source = place_all // holding
    dest_side = device_ids % dev_count // half
    source_side = source % dev_count // half
    crossing = source_side != dest_side
    source_row = (source // dev_count % pooled * half + source % half) * holding + place_all % holding
    pool_of = device_ids // dev_count // pooled
    peers = (pool_of[:, None] == pool_of[None, :]) & (dest_side[:, None] == dest_side[None, :])
    ahead = peers & crossing[None, :] & (device_ids[None, :] < device_ids[:, None])
    rank = jnp.sum(ahead, axis=1)
    cross_count = jnp.max(jnp.where(crossing, rank + 1, 0))
    my_side = my_dev // half
    my_pool = my_group // pooled
    leaving = (pool_of == my_pool) & (dest_side != my_side) & crossing
    slots = jnp.arange(POOL)
    leave_rows = jnp.sum(
        jnp.where(leaving[None, :] & (rank[None, :] == slots[:, None]), source_row[None, :], 0), axis=1
    )
    staying = (pool_of == my_pool) & (dest_side == my_side)
    place_in_pool = device_ids // dev_count % pooled * half + device_ids % half
    give_rows = jnp.sum(
        jnp.where(
            staying[None, :] & (place_in_pool[None, :] == slots[:, None]),
            jnp.where(crossing, POOL * holding + rank, source_row)[None, :],
            0,
        ),
        axis=1,
    )
    new_weights = None
    start = 0
    for block in spread:
        arrived = cross_over(cross_count, gather(leave_rows, block, block), over)
        given = gather(give_rows, block, arrived)
        given = lax.all_to_all(
            given, AXES, split_axis=0, concat_axis=0, tiled=True, axis_index_groups=pools
        ).reshape(1, -1, hidden)
        if new_weights is None:
            new_weights = jnp.pad(given, ((0, 0), (0, width_in - given.shape[1]), (0, 0)))
        else:
            new_weights = lax.dynamic_update_slice(new_weights, given, (0, start, 0))
        start += given.shape[1]
    return (new_weights, new_scales, hidden_out, slot_load)


def solution(mesh):
    in_specs = (
        P(AXES, None, None),
        P(AXES, None, None),
        P(AXES),
        P(AXES, None),
        P(AXES, None),
        P(AXES, None),
        P(AXES, None),
    )
    out_specs = (
        P(AXES, None, None),
        P(AXES, None, None),
        P(AXES, None, None),
        P(AXES, None),
    )
    return jax.shard_map(
        per_device, mesh=mesh, in_specs=in_specs, out_specs=out_specs, check_vma=False
    )
```

```python
import functools

import jax
import jax.numpy as jnp
from jax import lax
from jax.experimental import pallas as pl
from jax.experimental.pallas import tpu as pltpu
from jax.sharding import PartitionSpec as P

TILE = 128
CAP = 2
POOL = 16
VMEM_LIMIT = 60 * 1024 * 1024
AXES = ("group", "dev")
PARTS = (112, 112)


def expert_kernel(x_ref, q_ref, s_ref, o_ref, acc_ref):
    step = pl.program_id(0)

    @pl.when(step == 0)
    def _():
        acc_ref[...] = jnp.zeros_like(acc_ref)

    holding, depth, _ = q_ref.shape
    cells = 2 * CAP
    rows = x_ref.shape[0]
    member_of = lax.broadcasted_iota(jnp.int32, (rows, TILE), 0) // cells % holding
    total = acc_ref[...]
    for member in range(holding):
        for block in range(depth // TILE):
            span = slice(block * TILE, (block + 1) * TILE)
            scale = s_ref[member, 0, block : block + 1, :]
            weights = (q_ref[member, span, :].astype(jnp.float32) * scale).astype(jnp.bfloat16)
            rows_in = jnp.where(member_of == member, x_ref[:, span], jnp.zeros((), jnp.bfloat16))
            total = total + jnp.dot(rows_in, weights, preferred_element_type=jnp.float32)
    acc_ref[...] = total

    @pl.when(step == pl.num_programs(0) - 1)
    def _():
        value = acc_ref[...]
        o_ref[...] = (value / (1.0 + jnp.exp(-value))).astype(jnp.bfloat16)


def serve(rows, values, scales):
    holding, width_in, hidden = values.shape
    depth = 512
    steps = width_in // depth
    count = rows.shape[0]
    wide = jnp.repeat(scales.astype(jnp.float32), TILE, axis=2)
    wide = wide.reshape(holding, steps, depth // TILE, hidden)
    return pl.pallas_call(
        expert_kernel,
        grid=(steps,),
        in_specs=[
            pl.BlockSpec((count, depth), lambda k: (0, k)),
            pl.BlockSpec((holding, depth, hidden), lambda k: (0, k, 0)),
            pl.BlockSpec((holding, 1, depth // TILE, hidden), lambda k: (0, k, 0, 0)),
        ],
        out_specs=pl.BlockSpec((count, hidden), lambda k: (0, 0)),
        out_shape=jax.ShapeDtypeStruct((count, hidden), jnp.bfloat16),
        scratch_shapes=[pltpu.VMEM((count, hidden), jnp.float32)],
        compiler_params=pltpu.CompilerParams(vmem_limit_bytes=VMEM_LIMIT),
        cost_estimate=pl.CostEstimate(
            flops=2 * count * width_in * hidden * holding,
            bytes_accessed=2 * (values.size + count * (width_in + hidden)),
            transcendentals=count * hidden,
        ),
    )(rows, values, wide)


def through_vmem(count, sources, out_at, held, in_sem, out_sem):
    def leave(spot):
        pltpu.make_async_copy(held.at[spot], held.at[spot], in_sem.at[spot]).wait()
        pltpu.make_async_copy(held.at[spot], out_at(spot), out_sem.at[spot]).start()

    def finish(spot):
        pltpu.make_async_copy(held.at[spot], out_at(spot), out_sem.at[spot]).wait()

    for stage in (sources, leave, finish):
        pl.loop(0, count)(stage)


def gather_kernel(index_ref, near_ref, far_ref, out_ref, held, in_sem, out_sem):
    near_count = near_ref.shape[0]

    def start(spot):
        index = index_ref[spot]

        @pl.when(index < near_count)
        def _():
            near_index = jnp.minimum(index, near_count - 1)
            pltpu.make_async_copy(near_ref.at[near_index], held.at[spot], in_sem.at[spot]).start()

        @pl.when(index >= near_count)
        def _():
            far_index = jnp.clip(index - near_count, 0, far_ref.shape[0] - 1)
            pltpu.make_async_copy(far_ref.at[far_index], held.at[spot], in_sem.at[spot]).start()

    through_vmem(out_ref.shape[0], start, lambda spot: out_ref.at[spot], held, in_sem, out_sem)


def gather(indices, near, far):
    count = indices.shape[0]
    anywhere = pl.BlockSpec(memory_space=pl.ANY)
    out = jax.ShapeDtypeStruct((count,) + near.shape[1:], near.dtype)
    return pl.pallas_call(
        gather_kernel,
        in_specs=[pl.BlockSpec(memory_space=pltpu.SMEM), anywhere, anywhere],
        out_specs=anywhere,
        out_shape=out,
        scratch_shapes=[
            pltpu.VMEM(out.shape, out.dtype),
            pltpu.SemaphoreType.DMA((count,)),
            pltpu.SemaphoreType.DMA((count,)),
        ],
        compiler_params=pltpu.CompilerParams(vmem_limit_bytes=VMEM_LIMIT),
        cost_estimate=pl.CostEstimate(
            flops=0, bytes_accessed=4 * out.size, transcendentals=0
        ),
    )(indices, near, far)


def chunk_kernel(first, in_ref, out_ref, held, in_sem, out_sem):
    height = out_ref.shape[2]

    def start(spot):
        pltpu.make_async_copy(
            in_ref.at[:, pl.ds(first + spot * height, height), :], held.at[spot], in_sem.at[spot]
        ).start()

    through_vmem(POOL, start, lambda spot: out_ref.at[spot], held, in_sem, out_sem)


def by_chunk(values, first, height):
    holding, _, hidden = values.shape
    anywhere = pl.BlockSpec(memory_space=pl.ANY)
    out = jax.ShapeDtypeStruct((POOL, holding, height, hidden), values.dtype)
    return pl.pallas_call(
        functools.partial(chunk_kernel, first),
        in_specs=[anywhere],
        out_specs=anywhere,
        out_shape=out,
        scratch_shapes=[
            pltpu.VMEM(out.shape, out.dtype),
            pltpu.SemaphoreType.DMA((POOL,)),
            pltpu.SemaphoreType.DMA((POOL,)),
        ],
        compiler_params=pltpu.CompilerParams(vmem_limit_bytes=VMEM_LIMIT),
        cost_estimate=pl.CostEstimate(
            flops=0, bytes_accessed=4 * out.size, transcendentals=0
        ),
    )(values)


def join_kernel(first, blocks_ref, *refs):
    out_ref, held, in_sem, out_sem = refs[-4:]
    count, height, _ = blocks_ref.shape

    def start(spot):
        pltpu.make_async_copy(blocks_ref.at[spot], held.at[spot], in_sem.at[spot]).start()

    def out_at(spot):
        return out_ref.at[0, pl.ds(first + spot * height, height), :]

    through_vmem(count, start, out_at, held, in_sem, out_sem)


def join(weights, blocks, first, width_in):
    count, _, hidden = blocks.shape
    anywhere = pl.BlockSpec(memory_space=pl.ANY)
    operands = (blocks,) if weights is None else (blocks, weights)
    return pl.pallas_call(
        functools.partial(join_kernel, first),
        in_specs=[anywhere] * len(operands),
        out_specs=anywhere,
        out_shape=jax.ShapeDtypeStruct((1, width_in, hidden), blocks.dtype),
        input_output_aliases={} if weights is None else {1: 0},
        scratch_shapes=[
            pltpu.VMEM(blocks.shape, blocks.dtype),
            pltpu.SemaphoreType.DMA((count,)),
            pltpu.SemaphoreType.DMA((count,)),
        ],
        compiler_params=pltpu.CompilerParams(vmem_limit_bytes=VMEM_LIMIT),
        cost_estimate=pl.CostEstimate(flops=0, bytes_accessed=4 * blocks.size, transcendentals=0),
    )(*operands)


def cross_over(count, leave_rows, give_rows, block, pairs):
    def branch_of(size):
        def branch(leave_rows, give_rows, block):
            if size == 0:
                return gather(give_rows, block, block)
            arrived = lax.ppermute(gather(leave_rows[:size], block, block), AXES, pairs)
            return gather(give_rows, block, arrived)

        return branch

    branches = [branch_of(size) for size in range(POOL + 1)]
    return lax.switch(count, branches, leave_rows, give_rows, block)


def per_device(primary_q, primary_scales, new_place, tokens, experts, replica, route_num):
    holding, width_in, hidden = primary_q.shape
    dev_count = lax.axis_size("dev")
    group_count = lax.axis_size("group")
    device_count = dev_count * group_count
    half = dev_count // 2
    pooled = POOL // half
    my_dev = lax.axis_index("dev")
    my_group = lax.axis_index("group")
    first_dev = my_group * dev_count
    pools = [
        [(base + group) * dev_count + side * half + spot for group in range(pooled) for spot in range(half)]
        for base in range(0, group_count, pooled)
        for side in range(2)
    ]
    over = [
        (group * dev_count + spot, group * dev_count + (spot + half) % dev_count)
        for group in range(group_count)
        for spot in range(dev_count)
    ]

    spread = []
    start = 0
    for height in PARTS:
        block = lax.all_to_all(
            by_chunk(primary_q, start, height), AXES, split_axis=0, concat_axis=0, tiled=True, axis_index_groups=pools
        )
        spread.append(block.reshape(POOL * holding, height, hidden))
        start += POOL * height

    row_count, top_count = experts.shape
    pair_count = row_count * top_count
    scale_cols = primary_scales.size // row_count
    notice = jnp.concatenate(
        [
            experts.astype(jnp.bfloat16),
            replica.astype(jnp.bfloat16),
            jnp.broadcast_to(new_place.astype(jnp.bfloat16)[None], (row_count, 1)),
            primary_scales.reshape(row_count, scale_cols),
        ],
        axis=1,
    )
    notice = jnp.pad(notice, ((0, 0), (0, -notice.shape[1] % TILE)))
    held = jnp.concatenate([tokens, notice], axis=1)
    dev_bits = dev_count.bit_length() - 1
    all_bits = device_count.bit_length() - 1
    order = list(range(dev_bits))[::-1] + list(range(dev_bits, all_bits))[::-1]
    for bit in order:
        pairs = [(device, device ^ 1 << bit) for device in range(device_count)]
        held = jnp.concatenate([held, lax.ppermute(held, AXES, pairs)], axis=0)
    device_ids = jnp.arange(device_count, dtype=jnp.int32)
    my_id = first_dev + my_dev
    apart = device_ids ^ my_id
    spot_of = sum((apart >> bit & 1) << step for step, bit in enumerate(order))

    notices = held[:, width_in:].reshape(device_count, row_count, -1)[spot_of]
    experts_all = notices[:, :, :top_count].astype(jnp.int32).reshape(device_count, pair_count)
    replica_all = notices[:, :, top_count : 2 * top_count].astype(jnp.int32)
    replica_all = replica_all.reshape(device_count, pair_count)
    place_all = notices[:, 0, 2 * top_count].astype(jnp.int32)
    my_place = new_place[0]
    owner_notice = lax.dynamic_index_in_dim(notices, my_place // holding, 0, keepdims=False)
    owner_scales = owner_notice[:, 2 * top_count + 1 : 2 * top_count + 1 + scale_cols]
    new_scales = lax.dynamic_index_in_dim(
        owner_scales.reshape(primary_scales.shape), my_place % holding, 0
    )

    matched = experts_all[:, :, None] == place_all[None, None, :]
    has_copy = jnp.any(matched, axis=2)
    holder = jnp.sum(jnp.where(matched, device_ids[None, None, :], 0), axis=2)
    use_copy = (replica_all == 1) & has_copy
    target = jnp.where(use_copy, holder, experts_all // holding)
    slot_id = jnp.where(use_copy, holding, experts_all % holding)
    pair_order = jnp.arange(pair_count)
    before = pair_order[:, None] < pair_order[None, :]
    position = jnp.sum((target[:, :, None] == target[:, None, :]) & before[None], axis=1)
    served = position < CAP
    arriving = served & (target == my_id)
    slot_load = jnp.stack(
        [jnp.sum((arriving & (slot_id == slot)).astype(jnp.int32)) for slot in range(holding + 1)]
    )[None]

    cells = 2 * CAP
    cell_count = device_count * holding * cells
    cell = experts_all % holding * cells + use_copy * CAP + position
    mine = served & (experts_all // holding == my_id)
    cell_ids = jnp.arange(holding * cells)
    hit = mine[:, None, :] & (cell[:, None, :] == cell_ids[None, :, None])
    row_at = spot_of[:, None] * row_count + jnp.sum(
        jnp.where(hit, pair_order // top_count, 0), axis=2
    )
    row_at = jnp.where(jnp.any(hit, axis=2), row_at, -1).reshape(cell_count)
    row_hits = row_at[:, None] == jnp.arange(device_count * row_count)[None, :]
    row_block = jnp.dot(row_hits.astype(jnp.bfloat16), held, preferred_element_type=jnp.float32)
    activated = serve(row_block.astype(jnp.bfloat16), primary_q, primary_scales)

    def send_back(*after):
        blocks, *_ = lax.optimization_barrier((activated, *after))
        return lax.all_to_all(
            blocks.reshape(device_count, holding * cells, hidden),
            AXES,
            split_axis=0,
            concat_axis=0,
            tiled=True,
        )

    my_cell = (experts_all // holding * (holding * cells) + cell)[my_id]
    placed = (my_cell[:, None] == jnp.arange(cell_count)[None, :]) & served[my_id][:, None]
    source = place_all // holding
    dest_side = device_ids % dev_count // half
    source_side = source % dev_count // half
    crossing = source_side != dest_side
    source_row = (source // dev_count % pooled * half + source % half) * holding + place_all % holding
    pool_of = device_ids // dev_count // pooled
    peers = (pool_of[:, None] == pool_of[None, :]) & (dest_side[:, None] == dest_side[None, :])
    ahead = peers & crossing[None, :] & (device_ids[None, :] < device_ids[:, None])
    rank = jnp.sum(ahead, axis=1)
    cross_count = jnp.max(jnp.where(crossing, rank + 1, 0))
    my_side = my_dev // half
    my_pool = my_group // pooled
    leaving = (pool_of == my_pool) & (dest_side != my_side) & crossing
    slots = jnp.arange(POOL)
    leave_rows = jnp.sum(
        jnp.where(leaving[None, :] & (rank[None, :] == slots[:, None]), source_row[None, :], 0), axis=1
    )
    staying = (pool_of == my_pool) & (dest_side == my_side)
    place_in_pool = device_ids // dev_count % pooled * half + device_ids % half
    give_rows = jnp.sum(
        jnp.where(
            staying[None, :] & (place_in_pool[None, :] == slots[:, None]),
            jnp.where(crossing, POOL * holding + rank, source_row)[None, :],
            0,
        ),
        axis=1,
    )
    given = []
    for block in spread:
        given.append(cross_over(cross_count, leave_rows, give_rows, block, over))
        if len(given) == 1:
            returned = send_back(given[0], spread[-1])
            given[0], returned = lax.optimization_barrier((given[0], returned))
    new_weights = None
    start = 0
    for block in given:
        block = lax.all_to_all(
            block, AXES, split_axis=0, concat_axis=0, tiled=True, axis_index_groups=pools
        )
        new_weights = join(new_weights, block, start, width_in)
        start += block.shape[0] * block.shape[1]

    selected = jnp.dot(
        placed.astype(jnp.bfloat16),
        returned.reshape(cell_count, hidden),
        preferred_element_type=jnp.float32,
    )
    weight = route_num.reshape(pair_count).astype(jnp.float32) / 16.0
    hidden_out = (selected * weight[:, None]).astype(jnp.bfloat16)
    hidden_out = hidden_out.reshape(row_count, top_count, hidden)
    return (new_weights, new_scales, hidden_out, slot_load)


def solution(mesh):
    in_specs = (
        P(AXES, None, None),
        P(AXES, None, None),
        P(AXES),
        P(AXES, None),
        P(AXES, None),
        P(AXES, None),
        P(AXES, None),
    )
    out_specs = (
        P(AXES, None, None),
        P(AXES, None, None),
        P(AXES, None, None),
        P(AXES, None),
    )
    return jax.shard_map(
        per_device, mesh=mesh, in_specs=in_specs, out_specs=out_specs, check_vma=False
    )
```

```python
import functools

import jax
import jax.numpy as jnp
from jax import lax
from jax.experimental import pallas as pl
from jax.experimental.pallas import tpu as pltpu
from jax.sharding import PartitionSpec as P

TILE = 128
CAP = 2
POOL = 16
VMEM_LIMIT = 60 * 1024 * 1024
AXES = ("group", "dev")
PARTS = (112, 112)


def expert_kernel(x_ref, q_ref, s_ref, o_ref, acc_ref):
    step = pl.program_id(0)

    @pl.when(step == 0)
    def _():
        acc_ref[...] = jnp.zeros_like(acc_ref)

    holding, depth, _ = q_ref.shape
    cells = 2 * CAP
    rows = x_ref.shape[0]
    member_of = lax.broadcasted_iota(jnp.int32, (rows, TILE), 0) // cells % holding
    total = acc_ref[...]
    for member in range(holding):
        for block in range(depth // TILE):
            span = slice(block * TILE, (block + 1) * TILE)
            scale = s_ref[member, 0, block : block + 1, :]
            weights = (q_ref[member, span, :].astype(jnp.float32) * scale).astype(jnp.bfloat16)
            rows_in = jnp.where(member_of == member, x_ref[:, span], jnp.zeros((), jnp.bfloat16))
            total = total + jnp.dot(rows_in, weights, preferred_element_type=jnp.float32)
    acc_ref[...] = total

    @pl.when(step == pl.num_programs(0) - 1)
    def _():
        value = acc_ref[...]
        o_ref[...] = (value / (1.0 + jnp.exp(-value))).astype(jnp.bfloat16)


def serve(rows, values, scales):
    holding, width_in, hidden = values.shape
    depth = 512
    steps = width_in // depth
    count = rows.shape[0]
    wide = jnp.repeat(scales.astype(jnp.float32), TILE, axis=2)
    wide = wide.reshape(holding, steps, depth // TILE, hidden)
    return pl.pallas_call(
        expert_kernel,
        grid=(steps,),
        in_specs=[
            pl.BlockSpec((count, depth), lambda k: (0, k)),
            pl.BlockSpec((holding, depth, hidden), lambda k: (0, k, 0)),
            pl.BlockSpec((holding, 1, depth // TILE, hidden), lambda k: (0, k, 0, 0)),
        ],
        out_specs=pl.BlockSpec((count, hidden), lambda k: (0, 0)),
        out_shape=jax.ShapeDtypeStruct((count, hidden), jnp.bfloat16),
        scratch_shapes=[pltpu.VMEM((count, hidden), jnp.float32)],
        compiler_params=pltpu.CompilerParams(vmem_limit_bytes=VMEM_LIMIT),
        cost_estimate=pl.CostEstimate(
            flops=2 * count * width_in * hidden * holding,
            bytes_accessed=2 * (values.size + count * (width_in + hidden)),
            transcendentals=count * hidden,
        ),
    )(rows, values, wide)


def through_vmem(count, sources, out_at, held, in_sem, out_sem):
    def leave(spot):
        pltpu.make_async_copy(held.at[spot], held.at[spot], in_sem.at[spot]).wait()
        pltpu.make_async_copy(held.at[spot], out_at(spot), out_sem.at[spot]).start()

    def finish(spot):
        pltpu.make_async_copy(held.at[spot], out_at(spot), out_sem.at[spot]).wait()

    for stage in (sources, leave, finish):
        pl.loop(0, count)(stage)


def gather_kernel(index_ref, near_ref, far_ref, out_ref, held, in_sem, out_sem):
    near_count = near_ref.shape[0]

    def start(spot):
        index = index_ref[spot]

        @pl.when(index < near_count)
        def _():
            near_index = jnp.minimum(index, near_count - 1)
            pltpu.make_async_copy(near_ref.at[near_index], held.at[spot], in_sem.at[spot]).start()

        @pl.when(index >= near_count)
        def _():
            far_index = jnp.clip(index - near_count, 0, far_ref.shape[0] - 1)
            pltpu.make_async_copy(far_ref.at[far_index], held.at[spot], in_sem.at[spot]).start()

    through_vmem(out_ref.shape[0], start, lambda spot: out_ref.at[spot], held, in_sem, out_sem)


def gather(indices, near, far):
    count = indices.shape[0]
    anywhere = pl.BlockSpec(memory_space=pl.ANY)
    out = jax.ShapeDtypeStruct((count,) + near.shape[1:], near.dtype)
    return pl.pallas_call(
        gather_kernel,
        in_specs=[pl.BlockSpec(memory_space=pltpu.SMEM), anywhere, anywhere],
        out_specs=anywhere,
        out_shape=out,
        scratch_shapes=[
            pltpu.VMEM(out.shape, out.dtype),
            pltpu.SemaphoreType.DMA((count,)),
            pltpu.SemaphoreType.DMA((count,)),
        ],
        compiler_params=pltpu.CompilerParams(vmem_limit_bytes=VMEM_LIMIT),
        cost_estimate=pl.CostEstimate(
            flops=0, bytes_accessed=4 * out.size, transcendentals=0
        ),
    )(indices, near, far)


def chunk_kernel(first, in_ref, out_ref, held, in_sem, out_sem):
    height = out_ref.shape[2]

    def start(spot):
        pltpu.make_async_copy(
            in_ref.at[:, pl.ds(first + spot * height, height), :], held.at[spot], in_sem.at[spot]
        ).start()

    through_vmem(POOL, start, lambda spot: out_ref.at[spot], held, in_sem, out_sem)


def by_chunk(values, first, height):
    holding, _, hidden = values.shape
    anywhere = pl.BlockSpec(memory_space=pl.ANY)
    out = jax.ShapeDtypeStruct((POOL, holding, height, hidden), values.dtype)
    return pl.pallas_call(
        functools.partial(chunk_kernel, first),
        in_specs=[anywhere],
        out_specs=anywhere,
        out_shape=out,
        scratch_shapes=[
            pltpu.VMEM(out.shape, out.dtype),
            pltpu.SemaphoreType.DMA((POOL,)),
            pltpu.SemaphoreType.DMA((POOL,)),
        ],
        compiler_params=pltpu.CompilerParams(vmem_limit_bytes=VMEM_LIMIT),
        cost_estimate=pl.CostEstimate(
            flops=0, bytes_accessed=4 * out.size, transcendentals=0
        ),
    )(values)


def join_kernel(first, blocks_ref, *refs):
    out_ref, held, in_sem, out_sem = refs[-4:]
    count, height, _ = blocks_ref.shape

    def start(spot):
        pltpu.make_async_copy(blocks_ref.at[spot], held.at[spot], in_sem.at[spot]).start()

    def out_at(spot):
        return out_ref.at[0, pl.ds(first + spot * height, height), :]

    through_vmem(count, start, out_at, held, in_sem, out_sem)


def join(weights, blocks, first, width_in):
    count, _, hidden = blocks.shape
    anywhere = pl.BlockSpec(memory_space=pl.ANY)
    operands = (blocks,) if weights is None else (blocks, weights)
    return pl.pallas_call(
        functools.partial(join_kernel, first),
        in_specs=[anywhere] * len(operands),
        out_specs=anywhere,
        out_shape=jax.ShapeDtypeStruct((1, width_in, hidden), blocks.dtype),
        input_output_aliases={} if weights is None else {1: 0},
        scratch_shapes=[
            pltpu.VMEM(blocks.shape, blocks.dtype),
            pltpu.SemaphoreType.DMA((count,)),
            pltpu.SemaphoreType.DMA((count,)),
        ],
        compiler_params=pltpu.CompilerParams(vmem_limit_bytes=VMEM_LIMIT),
        cost_estimate=pl.CostEstimate(flops=0, bytes_accessed=4 * blocks.size, transcendentals=0),
    )(*operands)


def cross_over(count, leave_rows, give_rows, block, pairs):
    def branch_of(size):
        def branch(leave_rows, give_rows, block):
            if size == 0:
                return gather(give_rows, block, block)
            arrived = lax.ppermute(gather(leave_rows[:size], block, block), AXES, pairs)
            return gather(give_rows, block, arrived)

        return branch

    branches = [branch_of(size) for size in range(POOL + 1)]
    return lax.switch(count, branches, leave_rows, give_rows, block)


def per_device(primary_q, primary_scales, new_place, tokens, experts, replica, route_num):
    holding, width_in, hidden = primary_q.shape
    dev_count = lax.axis_size("dev")
    group_count = lax.axis_size("group")
    device_count = dev_count * group_count
    half = dev_count // 2
    pooled = POOL // half
    my_dev = lax.axis_index("dev")
    my_group = lax.axis_index("group")
    first_dev = my_group * dev_count
    pools = [
        [(base + group) * dev_count + side * half + spot for group in range(pooled) for spot in range(half)]
        for base in range(0, group_count, pooled)
        for side in range(2)
    ]
    over = [
        (group * dev_count + spot, group * dev_count + (spot + half) % dev_count)
        for group in range(group_count)
        for spot in range(dev_count)
    ]

    spread = []
    start = 0
    for height in PARTS:
        block = lax.all_to_all(
            by_chunk(primary_q, start, height), AXES, split_axis=0, concat_axis=0, tiled=True, axis_index_groups=pools
        )
        spread.append(block.reshape(POOL * holding, height, hidden))
        start += POOL * height

    row_count, top_count = experts.shape
    pair_count = row_count * top_count
    scale_cols = primary_scales.size // row_count
    notice = jnp.concatenate(
        [
            experts.astype(jnp.bfloat16),
            replica.astype(jnp.bfloat16),
            jnp.broadcast_to(new_place.astype(jnp.bfloat16)[None], (row_count, 1)),
            primary_scales.reshape(row_count, scale_cols),
        ],
        axis=1,
    )
    notice = jnp.pad(notice, ((0, 0), (0, -notice.shape[1] % TILE)))
    held = jnp.concatenate([tokens, notice], axis=1)
    held = lax.all_gather(held, AXES, axis=0, tiled=True)
    device_ids = jnp.arange(device_count, dtype=jnp.int32)
    my_id = first_dev + my_dev
    notices = held[:, width_in:].reshape(device_count, row_count, -1)
    experts_all = notices[:, :, :top_count].astype(jnp.int32).reshape(device_count, pair_count)
    replica_all = notices[:, :, top_count : 2 * top_count].astype(jnp.int32)
    replica_all = replica_all.reshape(device_count, pair_count)
    place_all = notices[:, 0, 2 * top_count].astype(jnp.int32)
    my_place = new_place[0]
    owner_notice = lax.dynamic_index_in_dim(notices, my_place // holding, 0, keepdims=False)
    owner_scales = owner_notice[:, 2 * top_count + 1 : 2 * top_count + 1 + scale_cols]
    new_scales = lax.dynamic_index_in_dim(
        owner_scales.reshape(primary_scales.shape), my_place % holding, 0
    )

    matched = experts_all[:, :, None] == place_all[None, None, :]
    has_copy = jnp.any(matched, axis=2)
    holder = jnp.sum(jnp.where(matched, device_ids[None, None, :], 0), axis=2)
    use_copy = (replica_all == 1) & has_copy
    target = jnp.where(use_copy, holder, experts_all // holding)
    slot_id = jnp.where(use_copy, holding, experts_all % holding)
    pair_order = jnp.arange(pair_count)
    before = pair_order[:, None] < pair_order[None, :]
    position = jnp.sum((target[:, :, None] == target[:, None, :]) & before[None], axis=1)
    served = position < CAP
    arriving = served & (target == my_id)
    slot_load = jnp.stack(
        [jnp.sum((arriving & (slot_id == slot)).astype(jnp.int32)) for slot in range(holding + 1)]
    )[None]

    cells = 2 * CAP
    cell_count = device_count * holding * cells
    cell = experts_all % holding * cells + use_copy * CAP + position
    mine = served & (experts_all // holding == my_id)
    cell_ids = jnp.arange(holding * cells)
    hit = mine[:, None, :] & (cell[:, None, :] == cell_ids[None, :, None])
    row_at = device_ids[:, None] * row_count + jnp.sum(
        jnp.where(hit, pair_order // top_count, 0), axis=2
    )
    row_at = jnp.where(jnp.any(hit, axis=2), row_at, -1).reshape(cell_count)
    row_hits = row_at[:, None] == jnp.arange(device_count * row_count)[None, :]
    row_block = jnp.dot(row_hits.astype(jnp.bfloat16), held, preferred_element_type=jnp.float32)
    activated = serve(row_block.astype(jnp.bfloat16), primary_q, primary_scales)

    def send_back(*after):
        blocks, *_ = lax.optimization_barrier((activated, *after))
        return lax.all_to_all(
            blocks.reshape(device_count, holding * cells, hidden),
            AXES,
            split_axis=0,
            concat_axis=0,
            tiled=True,
        )

    my_cell = (experts_all // holding * (holding * cells) + cell)[my_id]
    placed = (my_cell[:, None] == jnp.arange(cell_count)[None, :]) & served[my_id][:, None]
    source = place_all // holding
    dest_side = device_ids % dev_count // half
    source_side = source % dev_count // half
    crossing = source_side != dest_side
    source_row = (source // dev_count % pooled * half + source % half) * holding + place_all % holding
    pool_of = device_ids // dev_count // pooled
    peers = (pool_of[:, None] == pool_of[None, :]) & (dest_side[:, None] == dest_side[None, :])
    ahead = peers & crossing[None, :] & (device_ids[None, :] < device_ids[:, None])
    rank = jnp.sum(ahead, axis=1)
    cross_count = jnp.max(jnp.where(crossing, rank + 1, 0))
    my_side = my_dev // half
    my_pool = my_group // pooled
    leaving = (pool_of == my_pool) & (dest_side != my_side) & crossing
    slots = jnp.arange(POOL)
    leave_rows = jnp.sum(
        jnp.where(leaving[None, :] & (rank[None, :] == slots[:, None]), source_row[None, :], 0), axis=1
    )
    staying = (pool_of == my_pool) & (dest_side == my_side)
    place_in_pool = device_ids // dev_count % pooled * half + device_ids % half
    give_rows = jnp.sum(
        jnp.where(
            staying[None, :] & (place_in_pool[None, :] == slots[:, None]),
            jnp.where(crossing, POOL * holding + rank, source_row)[None, :],
            0,
        ),
        axis=1,
    )
    given = []
    for block in spread:
        given.append(cross_over(cross_count, leave_rows, give_rows, block, over))
        if len(given) == 1:
            returned = send_back(given[0], spread[-1])
            given[0], returned = lax.optimization_barrier((given[0], returned))
    new_weights = None
    start = 0
    for block in given:
        block = lax.all_to_all(
            block, AXES, split_axis=0, concat_axis=0, tiled=True, axis_index_groups=pools
        )
        new_weights = join(new_weights, block, start, width_in)
        start += block.shape[0] * block.shape[1]

    selected = jnp.dot(
        placed.astype(jnp.bfloat16),
        returned.reshape(cell_count, hidden),
        preferred_element_type=jnp.float32,
    )
    weight = route_num.reshape(pair_count).astype(jnp.float32) / 16.0
    hidden_out = (selected * weight[:, None]).astype(jnp.bfloat16)
    hidden_out = hidden_out.reshape(row_count, top_count, hidden)
    return (new_weights, new_scales, hidden_out, slot_load)


def solution(mesh):
    in_specs = (
        P(AXES, None, None),
        P(AXES, None, None),
        P(AXES),
        P(AXES, None),
        P(AXES, None),
        P(AXES, None),
        P(AXES, None),
    )
    out_specs = (
        P(AXES, None, None),
        P(AXES, None, None),
        P(AXES, None, None),
        P(AXES, None),
    )
    return jax.shard_map(
        per_device, mesh=mesh, in_specs=in_specs, out_specs=out_specs, check_vma=False
    )
```

```python
import functools

import jax
import jax.numpy as jnp
from jax import lax
from jax.experimental import pallas as pl
from jax.experimental.pallas import tpu as pltpu
from jax.sharding import PartitionSpec as P

TILE = 128
CAP = 2
POOL = 16
VMEM_LIMIT = 60 * 1024 * 1024
AXES = ("group", "dev")
PARTS = (112, 112)


def expert_kernel(x_ref, q_ref, s_ref, o_ref, acc_ref):
    step = pl.program_id(0)

    @pl.when(step == 0)
    def _():
        acc_ref[...] = jnp.zeros_like(acc_ref)

    holding, depth, _ = q_ref.shape
    cells = 2 * CAP
    rows = x_ref.shape[0]
    member_of = lax.broadcasted_iota(jnp.int32, (rows, TILE), 0) // cells % holding
    total = acc_ref[...]
    for member in range(holding):
        for block in range(depth // TILE):
            span = slice(block * TILE, (block + 1) * TILE)
            scale = s_ref[member, 0, block : block + 1, :]
            weights = (q_ref[member, span, :].astype(jnp.float32) * scale).astype(jnp.bfloat16)
            rows_in = jnp.where(member_of == member, x_ref[:, span], jnp.zeros((), jnp.bfloat16))
            total = total + jnp.dot(rows_in, weights, preferred_element_type=jnp.float32)
    acc_ref[...] = total

    @pl.when(step == pl.num_programs(0) - 1)
    def _():
        value = acc_ref[...]
        o_ref[...] = (value / (1.0 + jnp.exp(-value))).astype(jnp.bfloat16)


def serve(rows, values, scales):
    holding, width_in, hidden = values.shape
    depth = 512
    steps = width_in // depth
    count = rows.shape[0]
    wide = jnp.repeat(scales.astype(jnp.float32), TILE, axis=2)
    wide = wide.reshape(holding, steps, depth // TILE, hidden)
    return pl.pallas_call(
        expert_kernel,
        grid=(steps,),
        in_specs=[
            pl.BlockSpec((count, depth), lambda k: (0, k)),
            pl.BlockSpec((holding, depth, hidden), lambda k: (0, k, 0)),
            pl.BlockSpec((holding, 1, depth // TILE, hidden), lambda k: (0, k, 0, 0)),
        ],
        out_specs=pl.BlockSpec((count, hidden), lambda k: (0, 0)),
        out_shape=jax.ShapeDtypeStruct((count, hidden), jnp.bfloat16),
        scratch_shapes=[pltpu.VMEM((count, hidden), jnp.float32)],
        compiler_params=pltpu.CompilerParams(vmem_limit_bytes=VMEM_LIMIT),
        cost_estimate=pl.CostEstimate(
            flops=2 * count * width_in * hidden * holding,
            bytes_accessed=2 * (values.size + count * (width_in + hidden)),
            transcendentals=count * hidden,
        ),
    )(rows, values, wide)


def through_vmem(count, sources, out_at, held, in_sem, out_sem):
    def leave(spot):
        pltpu.make_async_copy(held.at[spot], held.at[spot], in_sem.at[spot]).wait()
        pltpu.make_async_copy(held.at[spot], out_at(spot), out_sem.at[spot]).start()

    def finish(spot):
        pltpu.make_async_copy(held.at[spot], out_at(spot), out_sem.at[spot]).wait()

    for stage in (sources, leave, finish):
        pl.loop(0, count)(stage)


def gather_kernel(index_ref, near_ref, far_ref, out_ref, held, in_sem, out_sem):
    near_count = near_ref.shape[0]

    def start(spot):
        index = index_ref[spot]

        @pl.when(index < near_count)
        def _():
            near_index = jnp.minimum(index, near_count - 1)
            pltpu.make_async_copy(near_ref.at[near_index], held.at[spot], in_sem.at[spot]).start()

        @pl.when(index >= near_count)
        def _():
            far_index = jnp.clip(index - near_count, 0, far_ref.shape[0] - 1)
            pltpu.make_async_copy(far_ref.at[far_index], held.at[spot], in_sem.at[spot]).start()

    through_vmem(out_ref.shape[0], start, lambda spot: out_ref.at[spot], held, in_sem, out_sem)


def gather(indices, near, far):
    count = indices.shape[0]
    anywhere = pl.BlockSpec(memory_space=pl.ANY)
    out = jax.ShapeDtypeStruct((count,) + near.shape[1:], near.dtype)
    return pl.pallas_call(
        gather_kernel,
        in_specs=[pl.BlockSpec(memory_space=pltpu.SMEM), anywhere, anywhere],
        out_specs=anywhere,
        out_shape=out,
        scratch_shapes=[
            pltpu.VMEM(out.shape, out.dtype),
            pltpu.SemaphoreType.DMA((count,)),
            pltpu.SemaphoreType.DMA((count,)),
        ],
        compiler_params=pltpu.CompilerParams(vmem_limit_bytes=VMEM_LIMIT),
        cost_estimate=pl.CostEstimate(
            flops=0, bytes_accessed=4 * out.size, transcendentals=0
        ),
    )(indices, near, far)


def chunk_kernel(first, in_ref, out_ref, held, in_sem, out_sem):
    height = out_ref.shape[2]

    def start(spot):
        pltpu.make_async_copy(
            in_ref.at[:, pl.ds(first + spot * height, height), :], held.at[spot], in_sem.at[spot]
        ).start()

    through_vmem(POOL, start, lambda spot: out_ref.at[spot], held, in_sem, out_sem)


def by_chunk(values, first, height):
    holding, _, hidden = values.shape
    anywhere = pl.BlockSpec(memory_space=pl.ANY)
    out = jax.ShapeDtypeStruct((POOL, holding, height, hidden), values.dtype)
    return pl.pallas_call(
        functools.partial(chunk_kernel, first),
        in_specs=[anywhere],
        out_specs=anywhere,
        out_shape=out,
        scratch_shapes=[
            pltpu.VMEM(out.shape, out.dtype),
            pltpu.SemaphoreType.DMA((POOL,)),
            pltpu.SemaphoreType.DMA((POOL,)),
        ],
        compiler_params=pltpu.CompilerParams(vmem_limit_bytes=VMEM_LIMIT),
        cost_estimate=pl.CostEstimate(
            flops=0, bytes_accessed=4 * out.size, transcendentals=0
        ),
    )(values)


def join_kernel(first, blocks_ref, *refs):
    out_ref, held, in_sem, out_sem = refs[-4:]
    count, height, _ = blocks_ref.shape

    def start(spot):
        pltpu.make_async_copy(blocks_ref.at[spot], held.at[spot], in_sem.at[spot]).start()

    def out_at(spot):
        return out_ref.at[0, pl.ds(first + spot * height, height), :]

    through_vmem(count, start, out_at, held, in_sem, out_sem)


def join(weights, blocks, first, width_in):
    count, _, hidden = blocks.shape
    anywhere = pl.BlockSpec(memory_space=pl.ANY)
    operands = (blocks,) if weights is None else (blocks, weights)
    return pl.pallas_call(
        functools.partial(join_kernel, first),
        in_specs=[anywhere] * len(operands),
        out_specs=anywhere,
        out_shape=jax.ShapeDtypeStruct((1, width_in, hidden), blocks.dtype),
        input_output_aliases={} if weights is None else {1: 0},
        scratch_shapes=[
            pltpu.VMEM(blocks.shape, blocks.dtype),
            pltpu.SemaphoreType.DMA((count,)),
            pltpu.SemaphoreType.DMA((count,)),
        ],
        compiler_params=pltpu.CompilerParams(vmem_limit_bytes=VMEM_LIMIT),
        cost_estimate=pl.CostEstimate(flops=0, bytes_accessed=4 * blocks.size, transcendentals=0),
    )(*operands)


def cross_over(count, leave_rows, give_rows, block, pairs):
    def branch_of(size):
        def branch(leave_rows, give_rows, block):
            if size == 0:
                return gather(give_rows, block, block)
            arrived = lax.ppermute(gather(leave_rows[:size], block, block), AXES, pairs)
            return gather(give_rows, block, arrived)

        return branch

    branches = [branch_of(size) for size in range(POOL + 1)]
    return lax.switch(count, branches, leave_rows, give_rows, block)


def per_device(primary_q, primary_scales, new_place, tokens, experts, replica, route_num):
    holding, width_in, hidden = primary_q.shape
    dev_count = lax.axis_size("dev")
    group_count = lax.axis_size("group")
    device_count = dev_count * group_count
    half = dev_count // 2
    pooled = POOL // half
    my_dev = lax.axis_index("dev")
    my_group = lax.axis_index("group")
    first_dev = my_group * dev_count
    pools = [
        [(base + group) * dev_count + side * half + spot for group in range(pooled) for spot in range(half)]
        for base in range(0, group_count, pooled)
        for side in range(2)
    ]
    over = [
        (group * dev_count + spot, group * dev_count + (spot + half) % dev_count)
        for group in range(group_count)
        for spot in range(dev_count)
    ]

    row_count, top_count = experts.shape
    pair_count = row_count * top_count
    scale_cols = primary_scales.size // row_count
    notice = jnp.concatenate(
        [
            experts.astype(jnp.bfloat16),
            replica.astype(jnp.bfloat16),
            jnp.broadcast_to(new_place.astype(jnp.bfloat16)[None], (row_count, 1)),
            primary_scales.reshape(row_count, scale_cols),
        ],
        axis=1,
    )
    notice = jnp.pad(notice, ((0, 0), (0, -notice.shape[1] % TILE)))
    held = jnp.concatenate([tokens, notice], axis=1)
    held = lax.all_gather(held, AXES, axis=0, tiled=True)
    spread = []
    start = 0
    for height in PARTS:
        block = by_chunk(primary_q, start, height)
        if spread:
            block, held = lax.optimization_barrier((block, held))
        block = lax.all_to_all(
            block, AXES, split_axis=0, concat_axis=0, tiled=True, axis_index_groups=pools
        )
        spread.append(block.reshape(POOL * holding, height, hidden))
        start += POOL * height

    device_ids = jnp.arange(device_count, dtype=jnp.int32)
    my_id = first_dev + my_dev
    notices = held[:, width_in:].reshape(device_count, row_count, -1)
    experts_all = notices[:, :, :top_count].astype(jnp.int32).reshape(device_count, pair_count)
    replica_all = notices[:, :, top_count : 2 * top_count].astype(jnp.int32)
    replica_all = replica_all.reshape(device_count, pair_count)
    place_all = notices[:, 0, 2 * top_count].astype(jnp.int32)
    my_place = new_place[0]
    owner_notice = lax.dynamic_index_in_dim(notices, my_place // holding, 0, keepdims=False)
    owner_scales = owner_notice[:, 2 * top_count + 1 : 2 * top_count + 1 + scale_cols]
    new_scales = lax.dynamic_index_in_dim(
        owner_scales.reshape(primary_scales.shape), my_place % holding, 0
    )

    matched = experts_all[:, :, None] == place_all[None, None, :]
    has_copy = jnp.any(matched, axis=2)
    holder = jnp.sum(jnp.where(matched, device_ids[None, None, :], 0), axis=2)
    use_copy = (replica_all == 1) & has_copy
    target = jnp.where(use_copy, holder, experts_all // holding)
    slot_id = jnp.where(use_copy, holding, experts_all % holding)
    pair_order = jnp.arange(pair_count)
    before = pair_order[:, None] < pair_order[None, :]
    position = jnp.sum((target[:, :, None] == target[:, None, :]) & before[None], axis=1)
    served = position < CAP
    arriving = served & (target == my_id)
    slot_load = jnp.stack(
        [jnp.sum((arriving & (slot_id == slot)).astype(jnp.int32)) for slot in range(holding + 1)]
    )[None]

    cells = 2 * CAP
    cell_count = device_count * holding * cells
    cell = experts_all % holding * cells + use_copy * CAP + position
    mine = served & (experts_all // holding == my_id)
    cell_ids = jnp.arange(holding * cells)
    hit = mine[:, None, :] & (cell[:, None, :] == cell_ids[None, :, None])
    row_at = device_ids[:, None] * row_count + jnp.sum(
        jnp.where(hit, pair_order // top_count, 0), axis=2
    )
    row_at = jnp.where(jnp.any(hit, axis=2), row_at, -1).reshape(cell_count)
    row_hits = row_at[:, None] == jnp.arange(device_count * row_count)[None, :]
    row_block = jnp.dot(row_hits.astype(jnp.bfloat16), held, preferred_element_type=jnp.float32)
    activated = serve(row_block.astype(jnp.bfloat16), primary_q, primary_scales)

    def send_back(*after):
        blocks, *_ = lax.optimization_barrier((activated, *after))
        return lax.all_to_all(
            blocks.reshape(device_count, holding * cells, hidden),
            AXES,
            split_axis=0,
            concat_axis=0,
            tiled=True,
        )

    my_cell = (experts_all // holding * (holding * cells) + cell)[my_id]
    placed = (my_cell[:, None] == jnp.arange(cell_count)[None, :]) & served[my_id][:, None]
    source = place_all // holding
    dest_side = device_ids % dev_count // half
    source_side = source % dev_count // half
    crossing = source_side != dest_side
    source_row = (source // dev_count % pooled * half + source % half) * holding + place_all % holding
    pool_of = device_ids // dev_count // pooled
    peers = (pool_of[:, None] == pool_of[None, :]) & (dest_side[:, None] == dest_side[None, :])
    ahead = peers & crossing[None, :] & (device_ids[None, :] < device_ids[:, None])
    rank = jnp.sum(ahead, axis=1)
    cross_count = jnp.max(jnp.where(crossing, rank + 1, 0))
    my_side = my_dev // half
    my_pool = my_group // pooled
    leaving = (pool_of == my_pool) & (dest_side != my_side) & crossing
    slots = jnp.arange(POOL)
    leave_rows = jnp.sum(
        jnp.where(leaving[None, :] & (rank[None, :] == slots[:, None]), source_row[None, :], 0), axis=1
    )
    staying = (pool_of == my_pool) & (dest_side == my_side)
    place_in_pool = device_ids // dev_count % pooled * half + device_ids % half
    give_rows = jnp.sum(
        jnp.where(
            staying[None, :] & (place_in_pool[None, :] == slots[:, None]),
            jnp.where(crossing, POOL * holding + rank, source_row)[None, :],
            0,
        ),
        axis=1,
    )
    given = []
    for block in spread:
        given.append(cross_over(cross_count, leave_rows, give_rows, block, over))
        if len(given) == 1:
            returned = send_back(given[0], spread[-1])
            given[0], returned = lax.optimization_barrier((given[0], returned))
    new_weights = None
    start = 0
    for block in given:
        block = lax.all_to_all(
            block, AXES, split_axis=0, concat_axis=0, tiled=True, axis_index_groups=pools
        )
        new_weights = join(new_weights, block, start, width_in)
        start += block.shape[0] * block.shape[1]

    selected = jnp.dot(
        placed.astype(jnp.bfloat16),
        returned.reshape(cell_count, hidden),
        preferred_element_type=jnp.float32,
    )
    weight = route_num.reshape(pair_count).astype(jnp.float32) / 16.0
    hidden_out = (selected * weight[:, None]).astype(jnp.bfloat16)
    hidden_out = hidden_out.reshape(row_count, top_count, hidden)
    return (new_weights, new_scales, hidden_out, slot_load)


def solution(mesh):
    in_specs = (
        P(AXES, None, None),
        P(AXES, None, None),
        P(AXES),
        P(AXES, None),
        P(AXES, None),
        P(AXES, None),
        P(AXES, None),
    )
    out_specs = (
        P(AXES, None, None),
        P(AXES, None, None),
        P(AXES, None, None),
        P(AXES, None),
    )
    return jax.shard_map(
        per_device, mesh=mesh, in_specs=in_specs, out_specs=out_specs, check_vma=False
    )
```

```python
import functools

import jax
import jax.numpy as jnp
from jax import lax
from jax.experimental import pallas as pl
from jax.experimental.pallas import tpu as pltpu
from jax.sharding import PartitionSpec as P

TILE = 128
CAP = 2
POOL = 16
VMEM_LIMIT = 60 * 1024 * 1024
AXES = ("group", "dev")
PARTS = (128, 96)


def expert_kernel(x_ref, q_ref, s_ref, o_ref, acc_ref):
    step = pl.program_id(0)

    @pl.when(step == 0)
    def _():
        acc_ref[...] = jnp.zeros_like(acc_ref)

    holding, depth, _ = q_ref.shape
    cells = 2 * CAP
    rows = x_ref.shape[0]
    member_of = lax.broadcasted_iota(jnp.int32, (rows, TILE), 0) // cells % holding
    total = acc_ref[...]
    for member in range(holding):
        for block in range(depth // TILE):
            span = slice(block * TILE, (block + 1) * TILE)
            scale = s_ref[member, 0, block : block + 1, :]
            weights = (q_ref[member, span, :].astype(jnp.float32) * scale).astype(jnp.bfloat16)
            rows_in = jnp.where(member_of == member, x_ref[:, span], jnp.zeros((), jnp.bfloat16))
            total = total + jnp.dot(rows_in, weights, preferred_element_type=jnp.float32)
    acc_ref[...] = total

    @pl.when(step == pl.num_programs(0) - 1)
    def _():
        value = acc_ref[...]
        o_ref[...] = (value / (1.0 + jnp.exp(-value))).astype(jnp.bfloat16)


def serve(rows, values, scales):
    holding, width_in, hidden = values.shape
    depth = 512
    steps = width_in // depth
    count = rows.shape[0]
    wide = jnp.repeat(scales.astype(jnp.float32), TILE, axis=2)
    wide = wide.reshape(holding, steps, depth // TILE, hidden)
    return pl.pallas_call(
        expert_kernel,
        grid=(steps,),
        in_specs=[
            pl.BlockSpec((count, depth), lambda k: (0, k)),
            pl.BlockSpec((holding, depth, hidden), lambda k: (0, k, 0)),
            pl.BlockSpec((holding, 1, depth // TILE, hidden), lambda k: (0, k, 0, 0)),
        ],
        out_specs=pl.BlockSpec((count, hidden), lambda k: (0, 0)),
        out_shape=jax.ShapeDtypeStruct((count, hidden), jnp.bfloat16),
        scratch_shapes=[pltpu.VMEM((count, hidden), jnp.float32)],
        compiler_params=pltpu.CompilerParams(vmem_limit_bytes=VMEM_LIMIT),
        cost_estimate=pl.CostEstimate(
            flops=2 * count * width_in * hidden * holding,
            bytes_accessed=2 * (values.size + count * (width_in + hidden)),
            transcendentals=count * hidden,
        ),
    )(rows, values, wide)


def through_vmem(count, sources, out_at, held, in_sem, out_sem):
    def leave(spot):
        pltpu.make_async_copy(held.at[spot], held.at[spot], in_sem.at[spot]).wait()
        pltpu.make_async_copy(held.at[spot], out_at(spot), out_sem.at[spot]).start()

    def finish(spot):
        pltpu.make_async_copy(held.at[spot], out_at(spot), out_sem.at[spot]).wait()

    for stage in (sources, leave, finish):
        pl.loop(0, count)(stage)


def gather_kernel(index_ref, near_ref, far_ref, out_ref, held, in_sem, out_sem):
    near_count = near_ref.shape[0]

    def start(spot):
        index = index_ref[spot]

        @pl.when(index < near_count)
        def _():
            near_index = jnp.minimum(index, near_count - 1)
            pltpu.make_async_copy(near_ref.at[near_index], held.at[spot], in_sem.at[spot]).start()

        @pl.when(index >= near_count)
        def _():
            far_index = jnp.clip(index - near_count, 0, far_ref.shape[0] - 1)
            pltpu.make_async_copy(far_ref.at[far_index], held.at[spot], in_sem.at[spot]).start()

    through_vmem(out_ref.shape[0], start, lambda spot: out_ref.at[spot], held, in_sem, out_sem)


def gather(indices, near, far):
    count = indices.shape[0]
    anywhere = pl.BlockSpec(memory_space=pl.ANY)
    out = jax.ShapeDtypeStruct((count,) + near.shape[1:], near.dtype)
    return pl.pallas_call(
        gather_kernel,
        in_specs=[pl.BlockSpec(memory_space=pltpu.SMEM), anywhere, anywhere],
        out_specs=anywhere,
        out_shape=out,
        scratch_shapes=[
            pltpu.VMEM(out.shape, out.dtype),
            pltpu.SemaphoreType.DMA((count,)),
            pltpu.SemaphoreType.DMA((count,)),
        ],
        compiler_params=pltpu.CompilerParams(vmem_limit_bytes=VMEM_LIMIT),
        cost_estimate=pl.CostEstimate(
            flops=0, bytes_accessed=4 * out.size, transcendentals=0
        ),
    )(indices, near, far)


def chunk_kernel(first, in_ref, out_ref, held, in_sem, out_sem):
    height = out_ref.shape[2]

    def start(spot):
        pltpu.make_async_copy(
            in_ref.at[:, pl.ds(first + spot * height, height), :], held.at[spot], in_sem.at[spot]
        ).start()

    through_vmem(POOL, start, lambda spot: out_ref.at[spot], held, in_sem, out_sem)


def by_chunk(values, first, height):
    holding, _, hidden = values.shape
    anywhere = pl.BlockSpec(memory_space=pl.ANY)
    out = jax.ShapeDtypeStruct((POOL, holding, height, hidden), values.dtype)
    return pl.pallas_call(
        functools.partial(chunk_kernel, first),
        in_specs=[anywhere],
        out_specs=anywhere,
        out_shape=out,
        scratch_shapes=[
            pltpu.VMEM(out.shape, out.dtype),
            pltpu.SemaphoreType.DMA((POOL,)),
            pltpu.SemaphoreType.DMA((POOL,)),
        ],
        compiler_params=pltpu.CompilerParams(vmem_limit_bytes=VMEM_LIMIT),
        cost_estimate=pl.CostEstimate(
            flops=0, bytes_accessed=4 * out.size, transcendentals=0
        ),
    )(values)


def join_kernel(first, blocks_ref, *refs):
    out_ref, held, in_sem, out_sem = refs[-4:]
    count, height, _ = blocks_ref.shape

    def start(spot):
        pltpu.make_async_copy(blocks_ref.at[spot], held.at[spot], in_sem.at[spot]).start()

    def out_at(spot):
        return out_ref.at[0, pl.ds(first + spot * height, height), :]

    through_vmem(count, start, out_at, held, in_sem, out_sem)


def join(weights, blocks, first, width_in):
    count, _, hidden = blocks.shape
    anywhere = pl.BlockSpec(memory_space=pl.ANY)
    operands = (blocks,) if weights is None else (blocks, weights)
    return pl.pallas_call(
        functools.partial(join_kernel, first),
        in_specs=[anywhere] * len(operands),
        out_specs=anywhere,
        out_shape=jax.ShapeDtypeStruct((1, width_in, hidden), blocks.dtype),
        input_output_aliases={} if weights is None else {1: 0},
        scratch_shapes=[
            pltpu.VMEM(blocks.shape, blocks.dtype),
            pltpu.SemaphoreType.DMA((count,)),
            pltpu.SemaphoreType.DMA((count,)),
        ],
        compiler_params=pltpu.CompilerParams(vmem_limit_bytes=VMEM_LIMIT),
        cost_estimate=pl.CostEstimate(flops=0, bytes_accessed=4 * blocks.size, transcendentals=0),
    )(*operands)


def cross_over(count, leave_rows, give_rows, block, pairs, beside=None, operands=()):
    def branch_of(size):
        def branch(leave_rows, give_rows, block, *operands):
            arrived = block
            if size > 0:
                arrived = lax.ppermute(gather(leave_rows[:size], block, block), AXES, pairs)
            extra = () if beside is None else (beside(*operands),)
            return (gather(give_rows, block, arrived),) + extra

        return branch

    branches = [branch_of(size) for size in range(POOL + 1)]
    return lax.switch(count, branches, leave_rows, give_rows, block, *operands)


def route(experts, replica, place_all, holding):
    pair_count = experts.shape[1]
    device_ids = jnp.arange(place_all.shape[0], dtype=jnp.int32)
    matched = experts[:, :, None] == place_all[None, None, :]
    has_copy = jnp.any(matched, axis=2)
    holder = jnp.sum(jnp.where(matched, device_ids[None, None, :], 0), axis=2)
    use_copy = (replica == 1) & has_copy
    target = jnp.where(use_copy, holder, experts // holding)
    slot_id = jnp.where(use_copy, holding, experts % holding)
    pair_order = jnp.arange(pair_count)
    before = pair_order[:, None] < pair_order[None, :]
    position = jnp.sum((target[:, :, None] == target[:, None, :]) & before[None], axis=1)
    cell = experts % holding * (2 * CAP) + use_copy * CAP + position
    return target, slot_id, position < CAP, cell


def per_device(primary_q, primary_scales, new_place, tokens, experts, replica, route_num):
    holding, width_in, hidden = primary_q.shape
    dev_count = lax.axis_size("dev")
    group_count = lax.axis_size("group")
    device_count = dev_count * group_count
    half = dev_count // 2
    pooled = POOL // half
    my_dev = lax.axis_index("dev")
    my_group = lax.axis_index("group")
    first_dev = my_group * dev_count
    pools = [
        [(base + group) * dev_count + side * half + spot for group in range(pooled) for spot in range(half)]
        for base in range(0, group_count, pooled)
        for side in range(2)
    ]
    over = [
        (group * dev_count + spot, group * dev_count + (spot + half) % dev_count)
        for group in range(group_count)
        for spot in range(dev_count)
    ]

    place_all = lax.all_to_all(
        jnp.broadcast_to(new_place.astype(jnp.bfloat16), (device_count, TILE)),
        AXES,
        split_axis=0,
        concat_axis=0,
        tiled=True,
    )

    spread = []
    start = 0
    for height in PARTS:
        block = by_chunk(primary_q, start, height)
        if not spread:
            block, place_all = lax.optimization_barrier((block, place_all))
        block = lax.all_to_all(
            block, AXES, split_axis=0, concat_axis=0, tiled=True, axis_index_groups=pools
        )
        spread.append(block.reshape(POOL * holding, height, hidden))
        start += POOL * height
    place_all = place_all[:, 0].astype(jnp.int32)
    device_ids = jnp.arange(device_count, dtype=jnp.int32)
    my_id = first_dev + my_dev

    row_count, top_count = experts.shape
    pair_count = row_count * top_count
    scale_cols = primary_scales.size // row_count
    notice = jnp.concatenate(
        [
            experts.astype(jnp.bfloat16),
            replica.astype(jnp.bfloat16),
            primary_scales.reshape(row_count, scale_cols),
        ],
        axis=1,
    )
    notice = jnp.pad(notice, ((0, 0), (0, -notice.shape[1] % TILE)))
    held = jnp.concatenate([tokens, notice], axis=1)
    held = lax.all_gather(held, AXES, axis=0, tiled=True)
    cells = 2 * CAP
    cell_count = device_count * holding * cells

    def pairs_of(held):
        notices = held[:, width_in:].reshape(device_count, row_count, -1)
        experts_all = notices[:, :, :top_count].astype(jnp.int32)
        replica_all = notices[:, :, top_count : 2 * top_count].astype(jnp.int32)
        return [each.reshape(device_count, pair_count) for each in (experts_all, replica_all)]

    def work(held, place_all, values, scales):
        experts_all, replica_all = pairs_of(held)
        _, _, served, cell = route(experts_all, replica_all, place_all, holding)
        mine = served & (experts_all // holding == my_id)
        cell_ids = jnp.arange(holding * cells)
        hit = mine[:, None, :] & (cell[:, None, :] == cell_ids[None, :, None])
        row_at = device_ids[:, None] * row_count + jnp.sum(
            jnp.where(hit, jnp.arange(pair_count) // top_count, 0), axis=2
        )
        row_at = jnp.where(jnp.any(hit, axis=2), row_at, -1).reshape(cell_count)
        row_hits = row_at[:, None] == jnp.arange(device_count * row_count)[None, :]
        rows = jnp.dot(row_hits.astype(jnp.bfloat16), held, preferred_element_type=jnp.float32)
        return serve(rows.astype(jnp.bfloat16), values, scales)

    source = place_all // holding
    dest_side = device_ids % dev_count // half
    source_side = source % dev_count // half
    crossing = source_side != dest_side
    source_row = (source // dev_count % pooled * half + source % half) * holding + place_all % holding
    pool_of = device_ids // dev_count // pooled
    peers = (pool_of[:, None] == pool_of[None, :]) & (dest_side[:, None] == dest_side[None, :])
    ahead = peers & crossing[None, :] & (device_ids[None, :] < device_ids[:, None])
    rank = jnp.sum(ahead, axis=1)
    cross_count = jnp.max(jnp.where(crossing, rank + 1, 0))
    my_side = my_dev // half
    my_pool = my_group // pooled
    leaving = (pool_of == my_pool) & (dest_side != my_side) & crossing
    slots = jnp.arange(POOL)
    leave_rows = jnp.sum(
        jnp.where(leaving[None, :] & (rank[None, :] == slots[:, None]), source_row[None, :], 0), axis=1
    )
    staying = (pool_of == my_pool) & (dest_side == my_side)
    place_in_pool = device_ids // dev_count % pooled * half + device_ids % half
    give_rows = jnp.sum(
        jnp.where(
            staying[None, :] & (place_in_pool[None, :] == slots[:, None]),
            jnp.where(crossing, POOL * holding + rank, source_row)[None, :],
            0,
        ),
        axis=1,
    )
    first, second = spread
    (first,) = cross_over(cross_count, leave_rows, give_rows, first, over)
    first = lax.all_to_all(
        first, AXES, split_axis=0, concat_axis=0, tiled=True, axis_index_groups=pools
    )
    second, activated = cross_over(
        cross_count,
        leave_rows,
        give_rows,
        second,
        over,
        work,
        (held, place_all, primary_q, primary_scales),
    )
    returned = lax.all_to_all(
        activated.reshape(device_count, holding * cells, hidden),
        AXES,
        split_axis=0,
        concat_axis=0,
        tiled=True,
    )
    second, returned, held = lax.optimization_barrier((second, returned, held))
    second = lax.all_to_all(
        second, AXES, split_axis=0, concat_axis=0, tiled=True, axis_index_groups=pools
    )
    new_weights = join(None, first, 0, width_in)
    new_weights = join(new_weights, second, first.shape[0] * first.shape[1], width_in)

    experts_all, replica_all = pairs_of(held)
    target, slot_id, served, _ = route(experts_all, replica_all, place_all, holding)
    arriving = served & (target == my_id)
    slot_load = jnp.stack(
        [jnp.sum((arriving & (slot_id == slot)).astype(jnp.int32)) for slot in range(holding + 1)]
    )[None]
    owner_notice = held[:, width_in:].reshape(device_count, row_count, -1)
    owner_notice = lax.dynamic_index_in_dim(
        owner_notice, new_place[0] // holding, 0, keepdims=False
    )
    owner_scales = owner_notice[:, 2 * top_count : 2 * top_count + scale_cols]
    new_scales = lax.dynamic_index_in_dim(
        owner_scales.reshape(primary_scales.shape), new_place[0] % holding, 0
    )

    my_experts = experts.reshape(1, pair_count)
    _, _, my_served, my_cell = route(
        my_experts, replica.reshape(1, pair_count), place_all, holding
    )
    my_cell = (my_experts // holding * (holding * cells) + my_cell)[0]
    placed = (my_cell[:, None] == jnp.arange(cell_count)[None, :]) & my_served[0][:, None]
    selected = jnp.dot(
        placed.astype(jnp.bfloat16),
        returned.reshape(cell_count, hidden),
        preferred_element_type=jnp.float32,
    )
    weight = route_num.reshape(pair_count).astype(jnp.float32) / 16.0
    hidden_out = (selected * weight[:, None]).astype(jnp.bfloat16)
    hidden_out = hidden_out.reshape(row_count, top_count, hidden)
    return (new_weights, new_scales, hidden_out, slot_load)


def solution(mesh):
    in_specs = (
        P(AXES, None, None),
        P(AXES, None, None),
        P(AXES),
        P(AXES, None),
        P(AXES, None),
        P(AXES, None),
        P(AXES, None),
    )
    out_specs = (
        P(AXES, None, None),
        P(AXES, None, None),
        P(AXES, None, None),
        P(AXES, None),
    )
    return jax.shard_map(
        per_device, mesh=mesh, in_specs=in_specs, out_specs=out_specs, check_vma=False
    )
```

```python
import functools

import jax
import jax.numpy as jnp
from jax import lax
from jax.experimental import pallas as pl
from jax.experimental.pallas import tpu as pltpu
from jax.sharding import PartitionSpec as P

TILE = 128
CAP = 2
POOL = 16
COMMON = 8
VMEM_LIMIT = 60 * 1024 * 1024
AXES = ("group", "dev")
PARTS = (128, 96)


def expert_kernel(x_ref, q_ref, s_ref, o_ref, acc_ref):
    step = pl.program_id(0)

    @pl.when(step == 0)
    def _():
        acc_ref[...] = jnp.zeros_like(acc_ref)

    holding, depth, _ = q_ref.shape
    cells = 2 * CAP
    rows = x_ref.shape[0]
    member_of = lax.broadcasted_iota(jnp.int32, (rows, TILE), 0) // cells % holding
    total = acc_ref[...]
    for member in range(holding):
        for block in range(depth // TILE):
            span = slice(block * TILE, (block + 1) * TILE)
            scale = s_ref[member, 0, block : block + 1, :]
            weights = (q_ref[member, span, :].astype(jnp.float32) * scale).astype(jnp.bfloat16)
            rows_in = jnp.where(member_of == member, x_ref[:, span], jnp.zeros((), jnp.bfloat16))
            total = total + jnp.dot(rows_in, weights, preferred_element_type=jnp.float32)
    acc_ref[...] = total

    @pl.when(step == pl.num_programs(0) - 1)
    def _():
        value = acc_ref[...]
        o_ref[...] = (value / (1.0 + jnp.exp(-value))).astype(jnp.bfloat16)


def serve(rows, values, scales):
    holding, width_in, hidden = values.shape
    depth = 512
    steps = width_in // depth
    count = rows.shape[0]
    wide = jnp.repeat(scales.astype(jnp.float32), TILE, axis=2)
    wide = wide.reshape(holding, steps, depth // TILE, hidden)
    return pl.pallas_call(
        expert_kernel,
        grid=(steps,),
        in_specs=[
            pl.BlockSpec((count, depth), lambda k: (0, k)),
            pl.BlockSpec((holding, depth, hidden), lambda k: (0, k, 0)),
            pl.BlockSpec((holding, 1, depth // TILE, hidden), lambda k: (0, k, 0, 0)),
        ],
        out_specs=pl.BlockSpec((count, hidden), lambda k: (0, 0)),
        out_shape=jax.ShapeDtypeStruct((count, hidden), jnp.bfloat16),
        scratch_shapes=[pltpu.VMEM((count, hidden), jnp.float32)],
        compiler_params=pltpu.CompilerParams(vmem_limit_bytes=VMEM_LIMIT),
        cost_estimate=pl.CostEstimate(
            flops=2 * count * width_in * hidden * holding,
            bytes_accessed=2 * (values.size + count * (width_in + hidden)),
            transcendentals=count * hidden,
        ),
    )(rows, values, wide)


def through_vmem(count, sources, out_at, held, in_sem, out_sem):
    def leave(spot):
        pltpu.make_async_copy(held.at[spot], held.at[spot], in_sem.at[spot]).wait()
        pltpu.make_async_copy(held.at[spot], out_at(spot), out_sem.at[spot]).start()

    def finish(spot):
        pltpu.make_async_copy(held.at[spot], out_at(spot), out_sem.at[spot]).wait()

    for stage in (sources, leave, finish):
        pl.loop(0, count)(stage)


def gather_kernel(index_ref, *refs):
    *source_refs, out_ref, held, in_sem, out_sem = refs

    def start(spot):
        index = index_ref[spot]
        base = 0
        for source_ref in source_refs:
            count = source_ref.shape[0]
            inside = (index >= base) & (index < base + count)
            at = jnp.clip(index - base, 0, count - 1)

            @pl.when(inside)
            def _():
                pltpu.make_async_copy(
                    source_ref.at[at], held.at[spot], in_sem.at[spot]
                ).start()

            base += count

    through_vmem(out_ref.shape[0], start, lambda spot: out_ref.at[spot], held, in_sem, out_sem)


def gather(indices, *sources):
    count = indices.shape[0]
    indices = jnp.clip(indices, 0, sum(source.shape[0] for source in sources) - 1)
    anywhere = pl.BlockSpec(memory_space=pl.ANY)
    out = jax.ShapeDtypeStruct((count,) + sources[0].shape[1:], sources[0].dtype)
    return pl.pallas_call(
        gather_kernel,
        in_specs=[pl.BlockSpec(memory_space=pltpu.SMEM)] + [anywhere] * len(sources),
        out_specs=anywhere,
        out_shape=out,
        scratch_shapes=[
            pltpu.VMEM(out.shape, out.dtype),
            pltpu.SemaphoreType.DMA((count,)),
            pltpu.SemaphoreType.DMA((count,)),
        ],
        compiler_params=pltpu.CompilerParams(vmem_limit_bytes=VMEM_LIMIT),
        cost_estimate=pl.CostEstimate(flops=0, bytes_accessed=4 * out.size, transcendentals=0),
    )(indices, *sources)


def chunk_kernel(first, in_ref, out_ref, held, in_sem, out_sem):
    height = out_ref.shape[2]

    def start(spot):
        pltpu.make_async_copy(
            in_ref.at[:, pl.ds(first + spot * height, height), :], held.at[spot], in_sem.at[spot]
        ).start()

    through_vmem(POOL, start, lambda spot: out_ref.at[spot], held, in_sem, out_sem)


def by_chunk(values, first, height):
    holding, _, hidden = values.shape
    anywhere = pl.BlockSpec(memory_space=pl.ANY)
    out = jax.ShapeDtypeStruct((POOL, holding, height, hidden), values.dtype)
    return pl.pallas_call(
        functools.partial(chunk_kernel, first),
        in_specs=[anywhere],
        out_specs=anywhere,
        out_shape=out,
        scratch_shapes=[
            pltpu.VMEM(out.shape, out.dtype),
            pltpu.SemaphoreType.DMA((POOL,)),
            pltpu.SemaphoreType.DMA((POOL,)),
        ],
        compiler_params=pltpu.CompilerParams(vmem_limit_bytes=VMEM_LIMIT),
        cost_estimate=pl.CostEstimate(
            flops=0, bytes_accessed=4 * out.size, transcendentals=0
        ),
    )(values)


def join_kernel(first, blocks_ref, *refs):
    out_ref, held, in_sem, out_sem = refs[-4:]
    count, height, _ = blocks_ref.shape

    def start(spot):
        pltpu.make_async_copy(blocks_ref.at[spot], held.at[spot], in_sem.at[spot]).start()

    def out_at(spot):
        return out_ref.at[0, pl.ds(first + spot * height, height), :]

    through_vmem(count, start, out_at, held, in_sem, out_sem)


def join(weights, blocks, first, width_in):
    count, _, hidden = blocks.shape
    anywhere = pl.BlockSpec(memory_space=pl.ANY)
    operands = (blocks,) if weights is None else (blocks, weights)
    return pl.pallas_call(
        functools.partial(join_kernel, first),
        in_specs=[anywhere] * len(operands),
        out_specs=anywhere,
        out_shape=jax.ShapeDtypeStruct((1, width_in, hidden), blocks.dtype),
        input_output_aliases={} if weights is None else {1: 0},
        scratch_shapes=[
            pltpu.VMEM(blocks.shape, blocks.dtype),
            pltpu.SemaphoreType.DMA((count,)),
            pltpu.SemaphoreType.DMA((count,)),
        ],
        compiler_params=pltpu.CompilerParams(vmem_limit_bytes=VMEM_LIMIT),
        cost_estimate=pl.CostEstimate(flops=0, bytes_accessed=4 * blocks.size, transcendentals=0),
    )(*operands)


def start_over(leave_rows, block, pairs):
    return lax.ppermute(gather(leave_rows[:COMMON], block), AXES, pairs)


def cross_over(count, leave_rows, give_rows, block, common, pairs):
    def branch_of(size):
        def branch(leave_rows, give_rows, block, common):
            if size == 0:
                return gather(give_rows, block, common)
            late = gather(leave_rows[COMMON : COMMON + size], block)
            return gather(give_rows, block, common, lax.ppermute(late, AXES, pairs))

        return branch

    branches = [branch_of(size) for size in range(POOL - COMMON + 1)]
    size = jnp.maximum(count - COMMON, 0)
    return lax.switch(size, branches, leave_rows, give_rows, block, common)


def route(experts, replica, place_all, holding):
    pair_count = experts.shape[1]
    device_ids = jnp.arange(place_all.shape[0], dtype=jnp.int32)
    matched = experts[:, :, None] == place_all[None, None, :]
    has_copy = jnp.any(matched, axis=2)
    holder = jnp.sum(jnp.where(matched, device_ids[None, None, :], 0), axis=2)
    use_copy = (replica == 1) & has_copy
    target = jnp.where(use_copy, holder, experts // holding)
    slot_id = jnp.where(use_copy, holding, experts % holding)
    pair_order = jnp.arange(pair_count)
    before = pair_order[:, None] < pair_order[None, :]
    position = jnp.sum((target[:, :, None] == target[:, None, :]) & before[None], axis=1)
    cell = experts % holding * (2 * CAP) + use_copy * CAP + position
    return target, slot_id, position < CAP, cell


def per_device(primary_q, primary_scales, new_place, tokens, experts, replica, route_num):
    holding, width_in, hidden = primary_q.shape
    dev_count = lax.axis_size("dev")
    group_count = lax.axis_size("group")
    device_count = dev_count * group_count
    half = dev_count // 2
    pooled = POOL // half
    my_dev = lax.axis_index("dev")
    my_group = lax.axis_index("group")
    first_dev = my_group * dev_count
    pools = [
        [(base + group) * dev_count + side * half + spot for group in range(pooled) for spot in range(half)]
        for base in range(0, group_count, pooled)
        for side in range(2)
    ]
    over = [
        (group * dev_count + spot, group * dev_count + (spot + half) % dev_count)
        for group in range(group_count)
        for spot in range(dev_count)
    ]

    place_all = lax.all_to_all(
        jnp.broadcast_to(new_place.astype(jnp.bfloat16), (device_count, TILE)),
        AXES,
        split_axis=0,
        concat_axis=0,
        tiled=True,
    )

    spread = []
    start = 0
    for height in PARTS:
        block = by_chunk(primary_q, start, height)
        if not spread:
            block, place_all = lax.optimization_barrier((block, place_all))
        block = lax.all_to_all(
            block, AXES, split_axis=0, concat_axis=0, tiled=True, axis_index_groups=pools
        )
        spread.append(block.reshape(POOL * holding, height, hidden))
        start += POOL * height
    place_all = place_all[:, 0].astype(jnp.int32)
    device_ids = jnp.arange(device_count, dtype=jnp.int32)
    my_id = first_dev + my_dev

    row_count, top_count = experts.shape
    pair_count = row_count * top_count
    scale_cols = primary_scales.size // row_count
    notice = jnp.concatenate(
        [
            experts.astype(jnp.bfloat16),
            replica.astype(jnp.bfloat16),
            primary_scales.reshape(row_count, scale_cols),
        ],
        axis=1,
    )
    notice = jnp.pad(notice, ((0, 0), (0, -notice.shape[1] % TILE)))
    held = jnp.concatenate([tokens, notice], axis=1)
    held = lax.all_gather(held, AXES, axis=0, tiled=True)
    cells = 2 * CAP
    cell_count = device_count * holding * cells

    def pairs_of(held):
        notices = held[:, width_in:].reshape(device_count, row_count, -1)
        experts_all = notices[:, :, :top_count].astype(jnp.int32)
        replica_all = notices[:, :, top_count : 2 * top_count].astype(jnp.int32)
        return [each.reshape(device_count, pair_count) for each in (experts_all, replica_all)]

    def work(held, place_all, values, scales):
        experts_all, replica_all = pairs_of(held)
        _, _, served, cell = route(experts_all, replica_all, place_all, holding)
        mine = served & (experts_all // holding == my_id)
        cell_ids = jnp.arange(holding * cells)
        hit = mine[:, None, :] & (cell[:, None, :] == cell_ids[None, :, None])
        row_at = device_ids[:, None] * row_count + jnp.sum(
            jnp.where(hit, jnp.arange(pair_count) // top_count, 0), axis=2
        )
        row_at = jnp.where(jnp.any(hit, axis=2), row_at, -1).reshape(cell_count)
        row_hits = row_at[:, None] == jnp.arange(device_count * row_count)[None, :]
        rows = jnp.dot(row_hits.astype(jnp.bfloat16), held, preferred_element_type=jnp.float32)
        return serve(rows.astype(jnp.bfloat16), values, scales)

    source = place_all // holding
    dest_side = device_ids % dev_count // half
    source_side = source % dev_count // half
    crossing = source_side != dest_side
    source_row = (source // dev_count % pooled * half + source % half) * holding + place_all % holding
    pool_of = device_ids // dev_count // pooled
    peers = (pool_of[:, None] == pool_of[None, :]) & (dest_side[:, None] == dest_side[None, :])
    ahead = peers & crossing[None, :] & (device_ids[None, :] < device_ids[:, None])
    rank = jnp.sum(ahead, axis=1)
    cross_count = jnp.max(jnp.where(crossing, rank + 1, 0))
    my_side = my_dev // half
    my_pool = my_group // pooled
    leaving = (pool_of == my_pool) & (dest_side != my_side) & crossing
    slots = jnp.arange(POOL)
    leave_rows = jnp.sum(
        jnp.where(leaving[None, :] & (rank[None, :] == slots[:, None]), source_row[None, :], 0), axis=1
    )
    staying = (pool_of == my_pool) & (dest_side == my_side)
    place_in_pool = device_ids // dev_count % pooled * half + device_ids % half
    give_rows = jnp.sum(
        jnp.where(
            staying[None, :] & (place_in_pool[None, :] == slots[:, None]),
            jnp.where(crossing, POOL * holding + rank, source_row)[None, :],
            0,
        ),
        axis=1,
    )
    first, second = spread
    common = start_over(leave_rows, first, over)
    first = cross_over(cross_count, leave_rows, give_rows, first, common, over)
    first, leave_rows, held = lax.optimization_barrier((first, leave_rows, held))
    first = lax.all_to_all(
        first, AXES, split_axis=0, concat_axis=0, tiled=True, axis_index_groups=pools
    )
    common = start_over(leave_rows, second, over)
    activated = work(held, place_all, primary_q, primary_scales)
    returned = lax.all_to_all(
        activated.reshape(device_count, holding * cells, hidden),
        AXES,
        split_axis=0,
        concat_axis=0,
        tiled=True,
    )
    common, returned = lax.optimization_barrier((common, returned))
    second = cross_over(cross_count, leave_rows, give_rows, second, common, over)
    second, held = lax.optimization_barrier((second, held))
    second = lax.all_to_all(
        second, AXES, split_axis=0, concat_axis=0, tiled=True, axis_index_groups=pools
    )
    new_weights = join(None, first, 0, width_in)
    new_weights = join(new_weights, second, first.shape[0] * first.shape[1], width_in)

    experts_all, replica_all = pairs_of(held)
    target, slot_id, served, _ = route(experts_all, replica_all, place_all, holding)
    arriving = served & (target == my_id)
    slot_load = jnp.stack(
        [jnp.sum((arriving & (slot_id == slot)).astype(jnp.int32)) for slot in range(holding + 1)]
    )[None]
    owner_notice = held[:, width_in:].reshape(device_count, row_count, -1)
    owner_notice = lax.dynamic_index_in_dim(
        owner_notice, new_place[0] // holding, 0, keepdims=False
    )
    owner_scales = owner_notice[:, 2 * top_count : 2 * top_count + scale_cols]
    new_scales = lax.dynamic_index_in_dim(
        owner_scales.reshape(primary_scales.shape), new_place[0] % holding, 0
    )

    my_experts = experts.reshape(1, pair_count)
    _, _, my_served, my_cell = route(
        my_experts, replica.reshape(1, pair_count), place_all, holding
    )
    my_cell = (my_experts // holding * (holding * cells) + my_cell)[0]
    placed = (my_cell[:, None] == jnp.arange(cell_count)[None, :]) & my_served[0][:, None]
    selected = jnp.dot(
        placed.astype(jnp.bfloat16),
        returned.reshape(cell_count, hidden),
        preferred_element_type=jnp.float32,
    )
    weight = route_num.reshape(pair_count).astype(jnp.float32) / 16.0
    hidden_out = (selected * weight[:, None]).astype(jnp.bfloat16)
    hidden_out = hidden_out.reshape(row_count, top_count, hidden)
    return (new_weights, new_scales, hidden_out, slot_load)


def solution(mesh):
    in_specs = (
        P(AXES, None, None),
        P(AXES, None, None),
        P(AXES),
        P(AXES, None),
        P(AXES, None),
        P(AXES, None),
        P(AXES, None),
    )
    out_specs = (
        P(AXES, None, None),
        P(AXES, None, None),
        P(AXES, None, None),
        P(AXES, None),
    )
    return jax.shard_map(
        per_device, mesh=mesh, in_specs=in_specs, out_specs=out_specs, check_vma=False
    )
```

```python
import functools

import jax
import jax.numpy as jnp
from jax import lax
from jax.experimental import pallas as pl
from jax.experimental.pallas import tpu as pltpu
from jax.sharding import PartitionSpec as P

TILE = 128
CAP = 2
POOL = 16
COMMON = 8
VMEM_LIMIT = 60 * 1024 * 1024
AXES = ("group", "dev")
PARTS = (128, 96)


def expert_kernel(x_ref, q_ref, s_ref, o_ref, acc_ref):
    step = pl.program_id(0)

    @pl.when(step == 0)
    def _():
        acc_ref[...] = jnp.zeros_like(acc_ref)

    holding, depth, _ = q_ref.shape
    cells = 2 * CAP
    rows = x_ref.shape[0]
    member_of = lax.broadcasted_iota(jnp.int32, (rows, TILE), 0) // cells % holding
    total = acc_ref[...]
    for member in range(holding):
        for block in range(depth // TILE):
            span = slice(block * TILE, (block + 1) * TILE)
            scale = s_ref[member, 0, block : block + 1, :]
            weights = (q_ref[member, span, :].astype(jnp.float32) * scale).astype(jnp.bfloat16)
            rows_in = jnp.where(member_of == member, x_ref[:, span], jnp.zeros((), jnp.bfloat16))
            total = total + jnp.dot(rows_in, weights, preferred_element_type=jnp.float32)
    acc_ref[...] = total

    @pl.when(step == pl.num_programs(0) - 1)
    def _():
        value = acc_ref[...]
        o_ref[...] = (value / (1.0 + jnp.exp(-value))).astype(jnp.bfloat16)


def serve(rows, values, scales):
    holding, width_in, hidden = values.shape
    depth = 512
    steps = width_in // depth
    count = rows.shape[0]
    wide = jnp.repeat(scales.astype(jnp.float32), TILE, axis=2)
    wide = wide.reshape(holding, steps, depth // TILE, hidden)
    return pl.pallas_call(
        expert_kernel,
        grid=(steps,),
        in_specs=[
            pl.BlockSpec((count, depth), lambda k: (0, k)),
            pl.BlockSpec((holding, depth, hidden), lambda k: (0, k, 0)),
            pl.BlockSpec((holding, 1, depth // TILE, hidden), lambda k: (0, k, 0, 0)),
        ],
        out_specs=pl.BlockSpec((count, hidden), lambda k: (0, 0)),
        out_shape=jax.ShapeDtypeStruct((count, hidden), jnp.bfloat16),
        scratch_shapes=[pltpu.VMEM((count, hidden), jnp.float32)],
        compiler_params=pltpu.CompilerParams(vmem_limit_bytes=VMEM_LIMIT),
        cost_estimate=pl.CostEstimate(
            flops=2 * count * width_in * hidden * holding,
            bytes_accessed=2 * (values.size + count * (width_in + hidden)),
            transcendentals=count * hidden,
        ),
    )(rows, values, wide)


def through_vmem(count, sources, out_at, held, in_sem, out_sem):
    def leave(spot):
        pltpu.make_async_copy(held.at[spot], held.at[spot], in_sem.at[spot]).wait()
        pltpu.make_async_copy(held.at[spot], out_at(spot), out_sem.at[spot]).start()

    def finish(spot):
        pltpu.make_async_copy(held.at[spot], out_at(spot), out_sem.at[spot]).wait()

    for stage in (sources, leave, finish):
        pl.loop(0, count)(stage)


def gather_kernel(index_ref, *refs):
    *source_refs, out_ref, held, in_sem, out_sem = refs

    def start(spot):
        index = index_ref[spot]
        base = 0
        for source_ref in source_refs:
            count = source_ref.shape[0]
            inside = (index >= base) & (index < base + count)
            at = jnp.clip(index - base, 0, count - 1)

            @pl.when(inside)
            def _():
                pltpu.make_async_copy(
                    source_ref.at[at], held.at[spot], in_sem.at[spot]
                ).start()

            base += count

    through_vmem(out_ref.shape[0], start, lambda spot: out_ref.at[spot], held, in_sem, out_sem)


def gather(indices, *sources):
    count = indices.shape[0]
    indices = jnp.clip(indices, 0, sum(source.shape[0] for source in sources) - 1)
    anywhere = pl.BlockSpec(memory_space=pl.ANY)
    out = jax.ShapeDtypeStruct((count,) + sources[0].shape[1:], sources[0].dtype)
    return pl.pallas_call(
        gather_kernel,
        in_specs=[pl.BlockSpec(memory_space=pltpu.SMEM)] + [anywhere] * len(sources),
        out_specs=anywhere,
        out_shape=out,
        scratch_shapes=[
            pltpu.VMEM(out.shape, out.dtype),
            pltpu.SemaphoreType.DMA((count,)),
            pltpu.SemaphoreType.DMA((count,)),
        ],
        compiler_params=pltpu.CompilerParams(vmem_limit_bytes=VMEM_LIMIT),
        cost_estimate=pl.CostEstimate(flops=0, bytes_accessed=4 * out.size, transcendentals=0),
    )(indices, *sources)


def chunk_kernel(first, in_ref, out_ref, held, in_sem, out_sem):
    height = out_ref.shape[2]

    def start(spot):
        pltpu.make_async_copy(
            in_ref.at[:, pl.ds(first + spot * height, height), :], held.at[spot], in_sem.at[spot]
        ).start()

    through_vmem(POOL, start, lambda spot: out_ref.at[spot], held, in_sem, out_sem)


def by_chunk(values, first, height):
    holding, _, hidden = values.shape
    anywhere = pl.BlockSpec(memory_space=pl.ANY)
    out = jax.ShapeDtypeStruct((POOL, holding, height, hidden), values.dtype)
    return pl.pallas_call(
        functools.partial(chunk_kernel, first),
        in_specs=[anywhere],
        out_specs=anywhere,
        out_shape=out,
        scratch_shapes=[
            pltpu.VMEM(out.shape, out.dtype),
            pltpu.SemaphoreType.DMA((POOL,)),
            pltpu.SemaphoreType.DMA((POOL,)),
        ],
        compiler_params=pltpu.CompilerParams(vmem_limit_bytes=VMEM_LIMIT),
        cost_estimate=pl.CostEstimate(
            flops=0, bytes_accessed=4 * out.size, transcendentals=0
        ),
    )(values)


def join_kernel(first, blocks_ref, *refs):
    out_ref, held, in_sem, out_sem = refs[-4:]
    count, height, _ = blocks_ref.shape

    def start(spot):
        pltpu.make_async_copy(blocks_ref.at[spot], held.at[spot], in_sem.at[spot]).start()

    def out_at(spot):
        return out_ref.at[0, pl.ds(first + spot * height, height), :]

    through_vmem(count, start, out_at, held, in_sem, out_sem)


def join(weights, blocks, first, width_in):
    count, _, hidden = blocks.shape
    anywhere = pl.BlockSpec(memory_space=pl.ANY)
    operands = (blocks,) if weights is None else (blocks, weights)
    return pl.pallas_call(
        functools.partial(join_kernel, first),
        in_specs=[anywhere] * len(operands),
        out_specs=anywhere,
        out_shape=jax.ShapeDtypeStruct((1, width_in, hidden), blocks.dtype),
        input_output_aliases={} if weights is None else {1: 0},
        scratch_shapes=[
            pltpu.VMEM(blocks.shape, blocks.dtype),
            pltpu.SemaphoreType.DMA((count,)),
            pltpu.SemaphoreType.DMA((count,)),
        ],
        compiler_params=pltpu.CompilerParams(vmem_limit_bytes=VMEM_LIMIT),
        cost_estimate=pl.CostEstimate(flops=0, bytes_accessed=4 * blocks.size, transcendentals=0),
    )(*operands)


def start_over(leave_rows, block, pairs):
    return lax.ppermute(gather(leave_rows[:COMMON], block), AXES, pairs)


def cross_over(count, leave_rows, give_rows, block, common, pairs):
    def branch_of(size):
        def branch(leave_rows, give_rows, block, common):
            if size == 0:
                return gather(give_rows, block, common)
            late = gather(leave_rows[COMMON : COMMON + size], block)
            return gather(give_rows, block, common, lax.ppermute(late, AXES, pairs))

        return branch

    branches = [branch_of(size) for size in range(POOL - COMMON + 1)]
    size = jnp.maximum(count - COMMON, 0)
    return lax.switch(size, branches, leave_rows, give_rows, block, common)


def route(experts, replica, place_all, holding):
    pair_count = experts.shape[1]
    device_ids = jnp.arange(place_all.shape[0], dtype=jnp.int32)
    matched = experts[:, :, None] == place_all[None, None, :]
    has_copy = jnp.any(matched, axis=2)
    holder = jnp.sum(jnp.where(matched, device_ids[None, None, :], 0), axis=2)
    use_copy = (replica == 1) & has_copy
    target = jnp.where(use_copy, holder, experts // holding)
    slot_id = jnp.where(use_copy, holding, experts % holding)
    pair_order = jnp.arange(pair_count)
    before = pair_order[:, None] < pair_order[None, :]
    position = jnp.sum((target[:, :, None] == target[:, None, :]) & before[None], axis=1)
    cell = experts % holding * (2 * CAP) + use_copy * CAP + position
    return target, slot_id, position < CAP, cell


def per_device(primary_q, primary_scales, new_place, tokens, experts, replica, route_num):
    holding, width_in, hidden = primary_q.shape
    dev_count = lax.axis_size("dev")
    group_count = lax.axis_size("group")
    device_count = dev_count * group_count
    half = dev_count // 2
    pooled = POOL // half
    my_dev = lax.axis_index("dev")
    my_group = lax.axis_index("group")
    first_dev = my_group * dev_count
    pools = [
        [(base + group) * dev_count + side * half + spot for group in range(pooled) for spot in range(half)]
        for base in range(0, group_count, pooled)
        for side in range(2)
    ]
    over = [
        (group * dev_count + spot, group * dev_count + (spot + half) % dev_count)
        for group in range(group_count)
        for spot in range(dev_count)
    ]

    place_all = lax.all_to_all(
        jnp.broadcast_to(new_place.astype(jnp.bfloat16), (device_count, TILE)),
        AXES,
        split_axis=0,
        concat_axis=0,
        tiled=True,
    )

    device_ids = jnp.arange(device_count, dtype=jnp.int32)
    my_id = first_dev + my_dev

    row_count, top_count = experts.shape
    pair_count = row_count * top_count
    scale_cols = primary_scales.size // row_count
    notice = jnp.concatenate(
        [
            experts.astype(jnp.bfloat16),
            replica.astype(jnp.bfloat16),
            primary_scales.reshape(row_count, scale_cols),
        ],
        axis=1,
    )
    notice = jnp.pad(notice, ((0, 0), (0, -notice.shape[1] % TILE)))
    held = jnp.concatenate([tokens, notice], axis=1)
    held = lax.all_gather(held, AXES, axis=0, tiled=True)

    def spread_over(block):
        block = lax.all_to_all(
            block, AXES, split_axis=0, concat_axis=0, tiled=True, axis_index_groups=pools
        )
        return block.reshape((POOL * holding,) + block.shape[2:])

    first_height, second_height = PARTS
    first, place_all = lax.optimization_barrier((by_chunk(primary_q, 0, first_height), place_all))
    first = spread_over(first)
    place_all = place_all[:, 0].astype(jnp.int32)
    second = by_chunk(primary_q, POOL * first_height, second_height)
    second, held = lax.optimization_barrier((second, held))
    second = spread_over(second)

    cells = 2 * CAP
    cell_count = device_count * holding * cells

    def pairs_of(held):
        notices = held[:, width_in:].reshape(device_count, row_count, -1)
        experts_all = notices[:, :, :top_count].astype(jnp.int32)
        replica_all = notices[:, :, top_count : 2 * top_count].astype(jnp.int32)
        return [each.reshape(device_count, pair_count) for each in (experts_all, replica_all)]

    def work(held, place_all, values, scales):
        experts_all, replica_all = pairs_of(held)
        _, _, served, cell = route(experts_all, replica_all, place_all, holding)
        mine = served & (experts_all // holding == my_id)
        cell_ids = jnp.arange(holding * cells)
        hit = mine[:, None, :] & (cell[:, None, :] == cell_ids[None, :, None])
        row_at = device_ids[:, None] * row_count + jnp.sum(
            jnp.where(hit, jnp.arange(pair_count) // top_count, 0), axis=2
        )
        row_at = jnp.where(jnp.any(hit, axis=2), row_at, -1).reshape(cell_count)
        row_hits = row_at[:, None] == jnp.arange(device_count * row_count)[None, :]
        rows = jnp.dot(row_hits.astype(jnp.bfloat16), held, preferred_element_type=jnp.float32)
        return serve(rows.astype(jnp.bfloat16), values, scales)

    source = place_all // holding
    dest_side = device_ids % dev_count // half
    source_side = source % dev_count // half
    crossing = source_side != dest_side
    source_row = (source // dev_count % pooled * half + source % half) * holding + place_all % holding
    pool_of = device_ids // dev_count // pooled
    peers = (pool_of[:, None] == pool_of[None, :]) & (dest_side[:, None] == dest_side[None, :])
    ahead = peers & crossing[None, :] & (device_ids[None, :] < device_ids[:, None])
    rank = jnp.sum(ahead, axis=1)
    cross_count = jnp.max(jnp.where(crossing, rank + 1, 0))
    my_side = my_dev // half
    my_pool = my_group // pooled
    leaving = (pool_of == my_pool) & (dest_side != my_side) & crossing
    slots = jnp.arange(POOL)
    leave_rows = jnp.sum(
        jnp.where(leaving[None, :] & (rank[None, :] == slots[:, None]), source_row[None, :], 0), axis=1
    )
    staying = (pool_of == my_pool) & (dest_side == my_side)
    place_in_pool = device_ids // dev_count % pooled * half + device_ids % half
    give_rows = jnp.sum(
        jnp.where(
            staying[None, :] & (place_in_pool[None, :] == slots[:, None]),
            jnp.where(crossing, POOL * holding + rank, source_row)[None, :],
            0,
        ),
        axis=1,
    )
    common = start_over(leave_rows, first, over)
    activated = work(held, place_all, primary_q, primary_scales)
    activated, second = lax.optimization_barrier((activated, second))
    returned = lax.all_to_all(
        activated.reshape(device_count, holding * cells, hidden),
        AXES,
        split_axis=0,
        concat_axis=0,
        tiled=True,
    )
    common, returned = lax.optimization_barrier((common, returned))
    first = cross_over(cross_count, leave_rows, give_rows, first, common, over)
    first, leave_rows = lax.optimization_barrier((first, leave_rows))
    first = lax.all_to_all(
        first, AXES, split_axis=0, concat_axis=0, tiled=True, axis_index_groups=pools
    )
    common = start_over(leave_rows, second, over)
    second = cross_over(cross_count, leave_rows, give_rows, second, common, over)
    second, held = lax.optimization_barrier((second, held))
    second = lax.all_to_all(
        second, AXES, split_axis=0, concat_axis=0, tiled=True, axis_index_groups=pools
    )
    new_weights = join(None, first, 0, width_in)
    new_weights = join(new_weights, second, first.shape[0] * first.shape[1], width_in)

    experts_all, replica_all = pairs_of(held)
    target, slot_id, served, _ = route(experts_all, replica_all, place_all, holding)
    arriving = served & (target == my_id)
    slot_load = jnp.stack(
        [jnp.sum((arriving & (slot_id == slot)).astype(jnp.int32)) for slot in range(holding + 1)]
    )[None]
    owner_notice = held[:, width_in:].reshape(device_count, row_count, -1)
    owner_notice = lax.dynamic_index_in_dim(
        owner_notice, new_place[0] // holding, 0, keepdims=False
    )
    owner_scales = owner_notice[:, 2 * top_count : 2 * top_count + scale_cols]
    new_scales = lax.dynamic_index_in_dim(
        owner_scales.reshape(primary_scales.shape), new_place[0] % holding, 0
    )

    my_experts = experts.reshape(1, pair_count)
    _, _, my_served, my_cell = route(
        my_experts, replica.reshape(1, pair_count), place_all, holding
    )
    my_cell = (my_experts // holding * (holding * cells) + my_cell)[0]
    placed = (my_cell[:, None] == jnp.arange(cell_count)[None, :]) & my_served[0][:, None]
    selected = jnp.dot(
        placed.astype(jnp.bfloat16),
        returned.reshape(cell_count, hidden),
        preferred_element_type=jnp.float32,
    )
    weight = route_num.reshape(pair_count).astype(jnp.float32) / 16.0
    hidden_out = (selected * weight[:, None]).astype(jnp.bfloat16)
    hidden_out = hidden_out.reshape(row_count, top_count, hidden)
    return (new_weights, new_scales, hidden_out, slot_load)


def solution(mesh):
    in_specs = (
        P(AXES, None, None),
        P(AXES, None, None),
        P(AXES),
        P(AXES, None),
        P(AXES, None),
        P(AXES, None),
        P(AXES, None),
    )
    out_specs = (
        P(AXES, None, None),
        P(AXES, None, None),
        P(AXES, None, None),
        P(AXES, None),
    )
    return jax.shard_map(
        per_device, mesh=mesh, in_specs=in_specs, out_specs=out_specs, check_vma=False
    )
```

```python
import functools

import jax
import jax.numpy as jnp
from jax import lax
from jax.experimental import pallas as pl
from jax.experimental.pallas import tpu as pltpu
from jax.sharding import PartitionSpec as P

TILE = 128
CAP = 2
POOL = 16
COMMON = 8
VMEM_LIMIT = 60 * 1024 * 1024
AXES = ("group", "dev")
PARTS = (128, 96)


def expert_kernel(x_ref, q_ref, s_ref, o_ref, acc_ref):
    step = pl.program_id(0)

    @pl.when(step == 0)
    def _():
        acc_ref[...] = jnp.zeros_like(acc_ref)

    holding, depth, _ = q_ref.shape
    cells = 2 * CAP
    rows = x_ref.shape[0]
    member_of = lax.broadcasted_iota(jnp.int32, (rows, TILE), 0) // cells % holding
    total = acc_ref[...]
    for member in range(holding):
        for block in range(depth // TILE):
            span = slice(block * TILE, (block + 1) * TILE)
            scale = s_ref[member, 0, block : block + 1, :]
            weights = (q_ref[member, span, :].astype(jnp.float32) * scale).astype(jnp.bfloat16)
            rows_in = jnp.where(member_of == member, x_ref[:, span], jnp.zeros((), jnp.bfloat16))
            total = total + jnp.dot(rows_in, weights, preferred_element_type=jnp.float32)
    acc_ref[...] = total

    @pl.when(step == pl.num_programs(0) - 1)
    def _():
        value = acc_ref[...]
        o_ref[...] = (value / (1.0 + jnp.exp(-value))).astype(jnp.bfloat16)


def serve(rows, values, scales):
    holding, width_in, hidden = values.shape
    depth = 512
    steps = width_in // depth
    count = rows.shape[0]
    wide = jnp.repeat(scales.astype(jnp.float32), TILE, axis=2)
    wide = wide.reshape(holding, steps, depth // TILE, hidden)
    return pl.pallas_call(
        expert_kernel,
        grid=(steps,),
        in_specs=[
            pl.BlockSpec((count, depth), lambda k: (0, k)),
            pl.BlockSpec((holding, depth, hidden), lambda k: (0, k, 0)),
            pl.BlockSpec((holding, 1, depth // TILE, hidden), lambda k: (0, k, 0, 0)),
        ],
        out_specs=pl.BlockSpec((count, hidden), lambda k: (0, 0)),
        out_shape=jax.ShapeDtypeStruct((count, hidden), jnp.bfloat16),
        scratch_shapes=[pltpu.VMEM((count, hidden), jnp.float32)],
        compiler_params=pltpu.CompilerParams(vmem_limit_bytes=VMEM_LIMIT),
        cost_estimate=pl.CostEstimate(
            flops=2 * count * width_in * hidden * holding,
            bytes_accessed=2 * (values.size + count * (width_in + hidden)),
            transcendentals=count * hidden,
        ),
    )(rows, values, wide)


def through_vmem(count, sources, out_at, held, in_sem, out_sem):
    def leave(spot):
        pltpu.make_async_copy(held.at[spot], held.at[spot], in_sem.at[spot]).wait()
        pltpu.make_async_copy(held.at[spot], out_at(spot), out_sem.at[spot]).start()

    def finish(spot):
        pltpu.make_async_copy(held.at[spot], out_at(spot), out_sem.at[spot]).wait()

    for stage in (sources, leave, finish):
        pl.loop(0, count)(stage)


def gather_kernel(index_ref, *refs):
    *source_refs, out_ref, held, in_sem, out_sem = refs

    def start(spot):
        index = index_ref[spot]
        base = 0
        for source_ref in source_refs:
            count = source_ref.shape[0]
            inside = (index >= base) & (index < base + count)
            at = jnp.clip(index - base, 0, count - 1)

            @pl.when(inside)
            def _():
                pltpu.make_async_copy(
                    source_ref.at[at], held.at[spot], in_sem.at[spot]
                ).start()

            base += count

    through_vmem(out_ref.shape[0], start, lambda spot: out_ref.at[spot], held, in_sem, out_sem)


def gather(indices, *sources):
    count = indices.shape[0]
    indices = jnp.clip(indices, 0, sum(source.shape[0] for source in sources) - 1)
    anywhere = pl.BlockSpec(memory_space=pl.ANY)
    out = jax.ShapeDtypeStruct((count,) + sources[0].shape[1:], sources[0].dtype)
    return pl.pallas_call(
        gather_kernel,
        in_specs=[pl.BlockSpec(memory_space=pltpu.SMEM)] + [anywhere] * len(sources),
        out_specs=anywhere,
        out_shape=out,
        scratch_shapes=[
            pltpu.VMEM(out.shape, out.dtype),
            pltpu.SemaphoreType.DMA((count,)),
            pltpu.SemaphoreType.DMA((count,)),
        ],
        compiler_params=pltpu.CompilerParams(vmem_limit_bytes=VMEM_LIMIT),
        cost_estimate=pl.CostEstimate(flops=0, bytes_accessed=4 * out.size, transcendentals=0),
    )(indices, *sources)


def chunk_kernel(first, in_ref, out_ref, held, in_sem, out_sem):
    height = out_ref.shape[2]

    def start(spot):
        pltpu.make_async_copy(
            in_ref.at[:, pl.ds(first + spot * height, height), :], held.at[spot], in_sem.at[spot]
        ).start()

    through_vmem(POOL, start, lambda spot: out_ref.at[spot], held, in_sem, out_sem)


def by_chunk(values, first, height):
    holding, _, hidden = values.shape
    anywhere = pl.BlockSpec(memory_space=pl.ANY)
    out = jax.ShapeDtypeStruct((POOL, holding, height, hidden), values.dtype)
    return pl.pallas_call(
        functools.partial(chunk_kernel, first),
        in_specs=[anywhere],
        out_specs=anywhere,
        out_shape=out,
        scratch_shapes=[
            pltpu.VMEM(out.shape, out.dtype),
            pltpu.SemaphoreType.DMA((POOL,)),
            pltpu.SemaphoreType.DMA((POOL,)),
        ],
        compiler_params=pltpu.CompilerParams(vmem_limit_bytes=VMEM_LIMIT),
        cost_estimate=pl.CostEstimate(
            flops=0, bytes_accessed=4 * out.size, transcendentals=0
        ),
    )(values)


def join_kernel(first, blocks_ref, *refs):
    out_ref, held, in_sem, out_sem = refs[-4:]
    count, height, _ = blocks_ref.shape

    def start(spot):
        pltpu.make_async_copy(blocks_ref.at[spot], held.at[spot], in_sem.at[spot]).start()

    def out_at(spot):
        return out_ref.at[0, pl.ds(first + spot * height, height), :]

    through_vmem(count, start, out_at, held, in_sem, out_sem)


def join(weights, blocks, first, width_in):
    count, _, hidden = blocks.shape
    anywhere = pl.BlockSpec(memory_space=pl.ANY)
    operands = (blocks,) if weights is None else (blocks, weights)
    return pl.pallas_call(
        functools.partial(join_kernel, first),
        in_specs=[anywhere] * len(operands),
        out_specs=anywhere,
        out_shape=jax.ShapeDtypeStruct((1, width_in, hidden), blocks.dtype),
        input_output_aliases={} if weights is None else {1: 0},
        scratch_shapes=[
            pltpu.VMEM(blocks.shape, blocks.dtype),
            pltpu.SemaphoreType.DMA((count,)),
            pltpu.SemaphoreType.DMA((count,)),
        ],
        compiler_params=pltpu.CompilerParams(vmem_limit_bytes=VMEM_LIMIT),
        cost_estimate=pl.CostEstimate(flops=0, bytes_accessed=4 * blocks.size, transcendentals=0),
    )(*operands)


def cross_over(count, leave_rows, give_rows, block, common, pairs):
    def branch_of(size):
        def branch(leave_rows, give_rows, block, common):
            if size == 0:
                return gather(give_rows, block, common)
            late = gather(leave_rows[COMMON : COMMON + size], block)
            return gather(give_rows, block, common, lax.ppermute(late, AXES, pairs))

        return branch

    branches = [branch_of(size) for size in range(POOL - COMMON + 1)]
    size = jnp.maximum(count - COMMON, 0)
    return lax.switch(size, branches, leave_rows, give_rows, block, common)


def route(experts, replica, place_all, holding):
    pair_count = experts.shape[1]
    device_ids = jnp.arange(place_all.shape[0], dtype=jnp.int32)
    matched = experts[:, :, None] == place_all[None, None, :]
    has_copy = jnp.any(matched, axis=2)
    holder = jnp.sum(jnp.where(matched, device_ids[None, None, :], 0), axis=2)
    use_copy = (replica == 1) & has_copy
    target = jnp.where(use_copy, holder, experts // holding)
    slot_id = jnp.where(use_copy, holding, experts % holding)
    pair_order = jnp.arange(pair_count)
    before = pair_order[:, None] < pair_order[None, :]
    position = jnp.sum((target[:, :, None] == target[:, None, :]) & before[None], axis=1)
    cell = experts % holding * (2 * CAP) + use_copy * CAP + position
    return target, slot_id, position < CAP, cell


def per_device(primary_q, primary_scales, new_place, tokens, experts, replica, route_num):
    holding, width_in, hidden = primary_q.shape
    dev_count = lax.axis_size("dev")
    group_count = lax.axis_size("group")
    device_count = dev_count * group_count
    half = dev_count // 2
    pooled = POOL // half
    my_dev = lax.axis_index("dev")
    my_group = lax.axis_index("group")
    first_dev = my_group * dev_count
    pools = [
        [(base + group) * dev_count + side * half + spot for group in range(pooled) for spot in range(half)]
        for base in range(0, group_count, pooled)
        for side in range(2)
    ]
    over = [
        (group * dev_count + spot, group * dev_count + (spot + half) % dev_count)
        for group in range(group_count)
        for spot in range(dev_count)
    ]

    device_ids = jnp.arange(device_count, dtype=jnp.int32)
    my_id = first_dev + my_dev

    place_all = lax.all_to_all(
        jnp.broadcast_to(new_place.astype(jnp.bfloat16), (device_count, TILE)),
        AXES,
        split_axis=0,
        concat_axis=0,
        tiled=True,
    )

    row_count, top_count = experts.shape
    pair_count = row_count * top_count
    scale_cols = primary_scales.size // row_count
    notice = jnp.concatenate(
        [
            experts.astype(jnp.bfloat16),
            replica.astype(jnp.bfloat16),
            primary_scales.reshape(row_count, scale_cols),
        ],
        axis=1,
    )
    notice = jnp.pad(notice, ((0, 0), (0, -notice.shape[1] % TILE)))
    held = jnp.concatenate([tokens, notice], axis=1)
    dev_bits = dev_count.bit_length() - 1
    all_bits = device_count.bit_length() - 1
    order = list(range(dev_bits))[::-1] + list(range(dev_bits, all_bits))[::-1]
    apart = device_ids ^ my_id
    spot_of = sum((apart >> bit & 1) << step for step, bit in enumerate(order))

    def double(held, bits):
        for bit in bits:
            pairs = [(device, device ^ 1 << bit) for device in range(device_count)]
            held = jnp.concatenate([held, lax.ppermute(held, AXES, pairs)], axis=0)
        return held

    held = double(held, order[:dev_bits])

    def spread_over(block):
        block = lax.all_to_all(
            block, AXES, split_axis=0, concat_axis=0, tiled=True, axis_index_groups=pools
        )
        return block.reshape((POOL * holding,) + block.shape[2:])

    first_height, second_height = PARTS
    first, place_all, held = lax.optimization_barrier(
        (by_chunk(primary_q, 0, first_height), place_all, held)
    )
    first = spread_over(first)
    place_all = place_all[:, 0].astype(jnp.int32)
    held = double(held, order[dev_bits:])
    second = by_chunk(primary_q, POOL * first_height, second_height)
    second, held = lax.optimization_barrier((second, held))
    second = spread_over(second)

    cells = 2 * CAP
    cell_count = device_count * holding * cells

    def pairs_of(held):
        notices = held[:, width_in:].reshape(device_count, row_count, -1)[spot_of]
        experts_all = notices[:, :, :top_count].astype(jnp.int32)
        replica_all = notices[:, :, top_count : 2 * top_count].astype(jnp.int32)
        return [each.reshape(device_count, pair_count) for each in (experts_all, replica_all)]

    def work(held, place_all, values, scales):
        experts_all, replica_all = pairs_of(held)
        _, _, served, cell = route(experts_all, replica_all, place_all, holding)
        mine = served & (experts_all // holding == my_id)
        cell_ids = jnp.arange(holding * cells)
        hit = mine[:, None, :] & (cell[:, None, :] == cell_ids[None, :, None])
        row_at = spot_of[:, None] * row_count + jnp.sum(
            jnp.where(hit, jnp.arange(pair_count) // top_count, 0), axis=2
        )
        row_at = jnp.where(jnp.any(hit, axis=2), row_at, -1).reshape(cell_count)
        row_hits = row_at[:, None] == jnp.arange(device_count * row_count)[None, :]
        rows = jnp.dot(row_hits.astype(jnp.bfloat16), held, preferred_element_type=jnp.float32)
        return serve(rows.astype(jnp.bfloat16), values, scales)

    source = place_all // holding
    dest_side = device_ids % dev_count // half
    source_side = source % dev_count // half
    crossing = source_side != dest_side
    source_row = (source // dev_count % pooled * half + source % half) * holding + place_all % holding
    pool_of = device_ids // dev_count // pooled
    peers = (pool_of[:, None] == pool_of[None, :]) & (dest_side[:, None] == dest_side[None, :])
    ahead = peers & crossing[None, :] & (device_ids[None, :] < device_ids[:, None])
    rank = jnp.sum(ahead, axis=1)
    cross_count = jnp.max(jnp.where(crossing, rank + 1, 0))
    my_side = my_dev // half
    my_pool = my_group // pooled
    leaving = (pool_of == my_pool) & (dest_side != my_side) & crossing
    slots = jnp.arange(POOL)
    leave_rows = jnp.sum(
        jnp.where(leaving[None, :] & (rank[None, :] == slots[:, None]), source_row[None, :], 0), axis=1
    )
    staying = (pool_of == my_pool) & (dest_side == my_side)
    place_in_pool = device_ids // dev_count % pooled * half + device_ids % half
    give_rows = jnp.sum(
        jnp.where(
            staying[None, :] & (place_in_pool[None, :] == slots[:, None]),
            jnp.where(crossing, POOL * holding + rank, source_row)[None, :],
            0,
        ),
        axis=1,
    )
    common = lax.ppermute(gather(leave_rows[:COMMON], first), AXES, over)
    activated = work(held, place_all, primary_q, primary_scales)
    common, activated = lax.optimization_barrier((common, activated))
    first = cross_over(cross_count, leave_rows, give_rows, first, common, over)
    first, leave_rows = lax.optimization_barrier((first, leave_rows))
    sent = gather(leave_rows[:COMMON], second)
    activated, sent = lax.optimization_barrier((activated, sent))
    common = lax.ppermute(sent, AXES, over)
    returned = lax.all_to_all(
        activated.reshape(device_count, holding * cells, hidden),
        AXES,
        split_axis=0,
        concat_axis=0,
        tiled=True,
    )
    first, returned = lax.optimization_barrier((first, returned))
    first = lax.all_to_all(
        first, AXES, split_axis=0, concat_axis=0, tiled=True, axis_index_groups=pools
    )
    second = cross_over(cross_count, leave_rows, give_rows, second, common, over)
    second, held = lax.optimization_barrier((second, held))
    second = lax.all_to_all(
        second, AXES, split_axis=0, concat_axis=0, tiled=True, axis_index_groups=pools
    )
    new_weights = join(None, first, 0, width_in)
    new_weights = join(new_weights, second, first.shape[0] * first.shape[1], width_in)

    experts_all, replica_all = pairs_of(held)
    target, slot_id, served, _ = route(experts_all, replica_all, place_all, holding)
    arriving = served & (target == my_id)
    slot_load = jnp.stack(
        [jnp.sum((arriving & (slot_id == slot)).astype(jnp.int32)) for slot in range(holding + 1)]
    )[None]
    owner_notice = held[:, width_in:].reshape(device_count, row_count, -1)
    owner_notice = lax.dynamic_index_in_dim(
        owner_notice, spot_of[new_place[0] // holding], 0, keepdims=False
    )
    owner_scales = owner_notice[:, 2 * top_count : 2 * top_count + scale_cols]
    new_scales = lax.dynamic_index_in_dim(
        owner_scales.reshape(primary_scales.shape), new_place[0] % holding, 0
    )

    my_experts = experts.reshape(1, pair_count)
    _, _, my_served, my_cell = route(
        my_experts, replica.reshape(1, pair_count), place_all, holding
    )
    my_cell = (my_experts // holding * (holding * cells) + my_cell)[0]
    placed = (my_cell[:, None] == jnp.arange(cell_count)[None, :]) & my_served[0][:, None]
    selected = jnp.dot(
        placed.astype(jnp.bfloat16),
        returned.reshape(cell_count, hidden),
        preferred_element_type=jnp.float32,
    )
    weight = route_num.reshape(pair_count).astype(jnp.float32) / 16.0
    hidden_out = (selected * weight[:, None]).astype(jnp.bfloat16)
    hidden_out = hidden_out.reshape(row_count, top_count, hidden)
    return (new_weights, new_scales, hidden_out, slot_load)


def solution(mesh):
    in_specs = (
        P(AXES, None, None),
        P(AXES, None, None),
        P(AXES),
        P(AXES, None),
        P(AXES, None),
        P(AXES, None),
        P(AXES, None),
    )
    out_specs = (
        P(AXES, None, None),
        P(AXES, None, None),
        P(AXES, None, None),
        P(AXES, None),
    )
    return jax.shard_map(
        per_device, mesh=mesh, in_specs=in_specs, out_specs=out_specs, check_vma=False
    )
```

```python
import functools

import jax
import jax.numpy as jnp
from jax import lax
from jax.experimental import pallas as pl
from jax.experimental.pallas import tpu as pltpu
from jax.sharding import PartitionSpec as P

TILE = 128
CAP = 2
POOL = 16
COMMON = 8
VMEM_LIMIT = 60 * 1024 * 1024
AXES = ("group", "dev")
PARTS = (128, 96)


def expert_kernel(x_ref, q_ref, s_ref, o_ref, acc_ref):
    step = pl.program_id(0)

    @pl.when(step == 0)
    def _():
        acc_ref[...] = jnp.zeros_like(acc_ref)

    holding, depth, _ = q_ref.shape
    cells = 2 * CAP
    rows = x_ref.shape[0]
    member_of = lax.broadcasted_iota(jnp.int32, (rows, TILE), 0) // cells % holding
    total = acc_ref[...]
    for member in range(holding):
        for block in range(depth // TILE):
            span = slice(block * TILE, (block + 1) * TILE)
            scale = s_ref[member, 0, block : block + 1, :]
            weights = (q_ref[member, span, :].astype(jnp.float32) * scale).astype(jnp.bfloat16)
            rows_in = jnp.where(member_of == member, x_ref[:, span], jnp.zeros((), jnp.bfloat16))
            total = total + jnp.dot(rows_in, weights, preferred_element_type=jnp.float32)
    acc_ref[...] = total

    @pl.when(step == pl.num_programs(0) - 1)
    def _():
        value = acc_ref[...]
        o_ref[...] = (value / (1.0 + jnp.exp(-value))).astype(jnp.bfloat16)


def serve(rows, values, scales):
    holding, width_in, hidden = values.shape
    depth = 512
    steps = width_in // depth
    count = rows.shape[0]
    wide = jnp.repeat(scales.astype(jnp.float32), TILE, axis=2)
    wide = wide.reshape(holding, steps, depth // TILE, hidden)
    return pl.pallas_call(
        expert_kernel,
        grid=(steps,),
        in_specs=[
            pl.BlockSpec((count, depth), lambda k: (0, k)),
            pl.BlockSpec((holding, depth, hidden), lambda k: (0, k, 0)),
            pl.BlockSpec((holding, 1, depth // TILE, hidden), lambda k: (0, k, 0, 0)),
        ],
        out_specs=pl.BlockSpec((count, hidden), lambda k: (0, 0)),
        out_shape=jax.ShapeDtypeStruct((count, hidden), jnp.bfloat16),
        scratch_shapes=[pltpu.VMEM((count, hidden), jnp.float32)],
        compiler_params=pltpu.CompilerParams(vmem_limit_bytes=VMEM_LIMIT),
        cost_estimate=pl.CostEstimate(
            flops=2 * count * width_in * hidden * holding,
            bytes_accessed=2 * (values.size + count * (width_in + hidden)),
            transcendentals=count * hidden,
        ),
    )(rows, values, wide)


def through_vmem(count, sources, out_at, held, in_sem, out_sem):
    def leave(spot):
        pltpu.make_async_copy(held.at[spot], held.at[spot], in_sem.at[spot]).wait()
        pltpu.make_async_copy(held.at[spot], out_at(spot), out_sem.at[spot]).start()

    def finish(spot):
        pltpu.make_async_copy(held.at[spot], out_at(spot), out_sem.at[spot]).wait()

    for stage in (sources, leave, finish):
        pl.loop(0, count)(stage)


def gather_kernel(index_ref, *refs):
    *source_refs, out_ref, held, in_sem, out_sem = refs

    def start(spot):
        index = index_ref[spot]
        base = 0
        for source_ref in source_refs:
            count = source_ref.shape[0]
            inside = (index >= base) & (index < base + count)
            at = jnp.clip(index - base, 0, count - 1)

            @pl.when(inside)
            def _():
                pltpu.make_async_copy(
                    source_ref.at[at], held.at[spot], in_sem.at[spot]
                ).start()

            base += count

    through_vmem(out_ref.shape[0], start, lambda spot: out_ref.at[spot], held, in_sem, out_sem)


def gather(indices, *sources):
    count = indices.shape[0]
    indices = jnp.clip(indices, 0, sum(source.shape[0] for source in sources) - 1)
    anywhere = pl.BlockSpec(memory_space=pl.ANY)
    out = jax.ShapeDtypeStruct((count,) + sources[0].shape[1:], sources[0].dtype)
    return pl.pallas_call(
        gather_kernel,
        in_specs=[pl.BlockSpec(memory_space=pltpu.SMEM)] + [anywhere] * len(sources),
        out_specs=anywhere,
        out_shape=out,
        scratch_shapes=[
            pltpu.VMEM(out.shape, out.dtype),
            pltpu.SemaphoreType.DMA((count,)),
            pltpu.SemaphoreType.DMA((count,)),
        ],
        compiler_params=pltpu.CompilerParams(vmem_limit_bytes=VMEM_LIMIT),
        cost_estimate=pl.CostEstimate(flops=0, bytes_accessed=4 * out.size, transcendentals=0),
    )(indices, *sources)


def chunk_kernel(first, in_ref, out_ref, held, in_sem, out_sem):
    height = out_ref.shape[2]

    def start(spot):
        pltpu.make_async_copy(
            in_ref.at[:, pl.ds(first + spot * height, height), :], held.at[spot], in_sem.at[spot]
        ).start()

    through_vmem(POOL, start, lambda spot: out_ref.at[spot], held, in_sem, out_sem)


def by_chunk(values, first, height):
    holding, _, hidden = values.shape
    anywhere = pl.BlockSpec(memory_space=pl.ANY)
    out = jax.ShapeDtypeStruct((POOL, holding, height, hidden), values.dtype)
    return pl.pallas_call(
        functools.partial(chunk_kernel, first),
        in_specs=[anywhere],
        out_specs=anywhere,
        out_shape=out,
        scratch_shapes=[
            pltpu.VMEM(out.shape, out.dtype),
            pltpu.SemaphoreType.DMA((POOL,)),
            pltpu.SemaphoreType.DMA((POOL,)),
        ],
        compiler_params=pltpu.CompilerParams(vmem_limit_bytes=VMEM_LIMIT),
        cost_estimate=pl.CostEstimate(
            flops=0, bytes_accessed=4 * out.size, transcendentals=0
        ),
    )(values)


def join_kernel(first, blocks_ref, *refs):
    out_ref, held, in_sem, out_sem = refs[-4:]
    count, height, _ = blocks_ref.shape

    def start(spot):
        pltpu.make_async_copy(blocks_ref.at[spot], held.at[spot], in_sem.at[spot]).start()

    def out_at(spot):
        return out_ref.at[0, pl.ds(first + spot * height, height), :]

    through_vmem(count, start, out_at, held, in_sem, out_sem)


def join(weights, blocks, first, width_in):
    count, _, hidden = blocks.shape
    anywhere = pl.BlockSpec(memory_space=pl.ANY)
    operands = (blocks,) if weights is None else (blocks, weights)
    return pl.pallas_call(
        functools.partial(join_kernel, first),
        in_specs=[anywhere] * len(operands),
        out_specs=anywhere,
        out_shape=jax.ShapeDtypeStruct((1, width_in, hidden), blocks.dtype),
        input_output_aliases={} if weights is None else {1: 0},
        scratch_shapes=[
            pltpu.VMEM(blocks.shape, blocks.dtype),
            pltpu.SemaphoreType.DMA((count,)),
            pltpu.SemaphoreType.DMA((count,)),
        ],
        compiler_params=pltpu.CompilerParams(vmem_limit_bytes=VMEM_LIMIT),
        cost_estimate=pl.CostEstimate(flops=0, bytes_accessed=4 * blocks.size, transcendentals=0),
    )(*operands)


def cross_over(count, leave_rows, give_rows, block, common, pairs):
    def branch_of(size):
        def branch(leave_rows, give_rows, block, common):
            if size == 0:
                return gather(give_rows, block, common)
            late = gather(leave_rows[COMMON : COMMON + size], block)
            return gather(give_rows, block, common, lax.ppermute(late, AXES, pairs))

        return branch

    branches = [branch_of(size) for size in range(POOL - COMMON + 1)]
    size = jnp.maximum(count - COMMON, 0)
    return lax.switch(size, branches, leave_rows, give_rows, block, common)


def route(experts, replica, place_all, holding):
    pair_count = experts.shape[1]
    device_ids = jnp.arange(place_all.shape[0], dtype=jnp.int32)
    matched = experts[:, :, None] == place_all[None, None, :]
    has_copy = jnp.any(matched, axis=2)
    holder = jnp.sum(jnp.where(matched, device_ids[None, None, :], 0), axis=2)
    use_copy = (replica == 1) & has_copy
    target = jnp.where(use_copy, holder, experts // holding)
    slot_id = jnp.where(use_copy, holding, experts % holding)
    pair_order = jnp.arange(pair_count)
    before = pair_order[:, None] < pair_order[None, :]
    position = jnp.sum((target[:, :, None] == target[:, None, :]) & before[None], axis=1)
    cell = experts % holding * (2 * CAP) + use_copy * CAP + position
    return target, slot_id, position < CAP, cell


def per_device(primary_q, primary_scales, new_place, tokens, experts, replica, route_num):
    holding, width_in, hidden = primary_q.shape
    dev_count = lax.axis_size("dev")
    group_count = lax.axis_size("group")
    device_count = dev_count * group_count
    half = dev_count // 2
    pooled = POOL // half
    my_dev = lax.axis_index("dev")
    my_group = lax.axis_index("group")
    first_dev = my_group * dev_count
    pools = [
        [(base + group) * dev_count + side * half + spot for group in range(pooled) for spot in range(half)]
        for base in range(0, group_count, pooled)
        for side in range(2)
    ]
    over = [
        (group * dev_count + spot, group * dev_count + (spot + half) % dev_count)
        for group in range(group_count)
        for spot in range(dev_count)
    ]

    device_ids = jnp.arange(device_count, dtype=jnp.int32)
    my_id = first_dev + my_dev

    place_all = lax.all_to_all(
        jnp.broadcast_to(new_place.astype(jnp.bfloat16), (device_count, TILE)),
        AXES,
        split_axis=0,
        concat_axis=0,
        tiled=True,
    )

    row_count, top_count = experts.shape
    pair_count = row_count * top_count
    scale_cols = primary_scales.size // row_count
    notice = jnp.concatenate(
        [
            experts.astype(jnp.bfloat16),
            replica.astype(jnp.bfloat16),
            primary_scales.reshape(row_count, scale_cols),
        ],
        axis=1,
    )
    notice = jnp.pad(notice, ((0, 0), (0, -notice.shape[1] % TILE)))
    held = jnp.concatenate([tokens, notice], axis=1)
    dev_bits = dev_count.bit_length() - 1
    all_bits = device_count.bit_length() - 1
    order = list(range(dev_bits))[::-1] + list(range(dev_bits, all_bits))[::-1]
    apart = device_ids ^ my_id
    spot_of = sum((apart >> bit & 1) << step for step, bit in enumerate(order))

    def double(held, bits):
        for bit in bits:
            pairs = [(device, device ^ 1 << bit) for device in range(device_count)]
            held = jnp.concatenate([held, lax.ppermute(held, AXES, pairs)], axis=0)
        return held

    held = double(held, order[:-1])

    place_all = place_all[:, 0].astype(jnp.int32)
    source = place_all // holding
    dest_side = device_ids % dev_count // half
    source_side = source % dev_count // half
    crossing = source_side != dest_side
    source_row = (source // dev_count % pooled * half + source % half) * holding + place_all % holding
    pool_of = device_ids // dev_count // pooled
    peers = (pool_of[:, None] == pool_of[None, :]) & (dest_side[:, None] == dest_side[None, :])
    ahead = peers & crossing[None, :] & (device_ids[None, :] < device_ids[:, None])
    rank = jnp.sum(ahead, axis=1)
    cross_count = jnp.max(jnp.where(crossing, rank + 1, 0))
    my_side = my_dev // half
    my_pool = my_group // pooled
    leaving = (pool_of == my_pool) & (dest_side != my_side) & crossing
    slots = jnp.arange(POOL)
    leave_rows = jnp.sum(
        jnp.where(leaving[None, :] & (rank[None, :] == slots[:, None]), source_row[None, :], 0), axis=1
    )
    staying = (pool_of == my_pool) & (dest_side == my_side)
    place_in_pool = device_ids // dev_count % pooled * half + device_ids % half
    give_rows = jnp.sum(
        jnp.where(
            staying[None, :] & (place_in_pool[None, :] == slots[:, None]),
            jnp.where(crossing, POOL * holding + rank, source_row)[None, :],
            0,
        ),
        axis=1,
    )

    def spread_over(block):
        block = lax.all_to_all(
            block, AXES, split_axis=0, concat_axis=0, tiled=True, axis_index_groups=pools
        )
        return block.reshape((POOL * holding,) + block.shape[2:])

    first_height, second_height = PARTS
    first = by_chunk(primary_q, 0, first_height)
    second = by_chunk(primary_q, POOL * first_height, second_height)
    first, second, held, place_all, leave_rows, give_rows, cross_count = lax.optimization_barrier(
        (first, second, held, place_all, leave_rows, give_rows, cross_count)
    )
    first = spread_over(first)
    held = double(held, order[-1:])
    second, held = lax.optimization_barrier((second, held))
    second = spread_over(second)

    cells = 2 * CAP
    cell_count = device_count * holding * cells

    def pairs_of(held):
        notices = held[:, width_in:].reshape(device_count, row_count, -1)[spot_of]
        experts_all = notices[:, :, :top_count].astype(jnp.int32)
        replica_all = notices[:, :, top_count : 2 * top_count].astype(jnp.int32)
        return [each.reshape(device_count, pair_count) for each in (experts_all, replica_all)]

    def work(held, place_all, values, scales):
        experts_all, replica_all = pairs_of(held)
        _, _, served, cell = route(experts_all, replica_all, place_all, holding)
        mine = served & (experts_all // holding == my_id)
        cell_ids = jnp.arange(holding * cells)
        hit = mine[:, None, :] & (cell[:, None, :] == cell_ids[None, :, None])
        row_at = spot_of[:, None] * row_count + jnp.sum(
            jnp.where(hit, jnp.arange(pair_count) // top_count, 0), axis=2
        )
        row_at = jnp.where(jnp.any(hit, axis=2), row_at, -1).reshape(cell_count)
        row_hits = row_at[:, None] == jnp.arange(device_count * row_count)[None, :]
        rows = jnp.dot(row_hits.astype(jnp.bfloat16), held, preferred_element_type=jnp.float32)
        return serve(rows.astype(jnp.bfloat16), values, scales)

    common = lax.ppermute(gather(leave_rows[:COMMON], first), AXES, over)
    activated = work(held, place_all, primary_q, primary_scales)
    blocks = activated.reshape(group_count, dev_count, holding * cells, hidden)
    along_dev = [lax.dynamic_index_in_dim(blocks, my_dev, 1, keepdims=False)]
    for step in range(1, dev_count):
        pairs = [
            (group * dev_count + spot, group * dev_count + (spot ^ step))
            for group in range(group_count)
            for spot in range(dev_count)
        ]
        block = lax.dynamic_index_in_dim(blocks, my_dev ^ step, 1, keepdims=False)
        along_dev.append(lax.ppermute(block, AXES, pairs))
    blocks = jnp.stack(along_dev, axis=1)
    common, blocks = lax.optimization_barrier((common, blocks))
    first = cross_over(cross_count, leave_rows, give_rows, first, common, over)
    first, leave_rows, blocks = lax.optimization_barrier((first, leave_rows, blocks))
    returned = [lax.dynamic_index_in_dim(blocks, my_group, 0, keepdims=False)]
    for step in range(1, group_count):
        pairs = [
            (group * dev_count + spot, (group ^ step) * dev_count + spot)
            for group in range(group_count)
            for spot in range(dev_count)
        ]
        block = lax.dynamic_index_in_dim(blocks, my_group ^ step, 0, keepdims=False)
        returned.append(lax.ppermute(block, AXES, pairs))
    returned = jnp.stack(returned)
    common = lax.ppermute(gather(leave_rows[:COMMON], second), AXES, over)
    first = lax.all_to_all(
        first, AXES, split_axis=0, concat_axis=0, tiled=True, axis_index_groups=pools
    )
    second = cross_over(cross_count, leave_rows, give_rows, second, common, over)
    second, held, returned = lax.optimization_barrier((second, held, returned))
    second = lax.all_to_all(
        second, AXES, split_axis=0, concat_axis=0, tiled=True, axis_index_groups=pools
    )
    new_weights = join(None, first, 0, width_in)
    new_weights = join(new_weights, second, first.shape[0] * first.shape[1], width_in)

    experts_all, replica_all = pairs_of(held)
    target, slot_id, served, _ = route(experts_all, replica_all, place_all, holding)
    arriving = served & (target == my_id)
    slot_load = jnp.stack(
        [jnp.sum((arriving & (slot_id == slot)).astype(jnp.int32)) for slot in range(holding + 1)]
    )[None]
    owner_notice = held[:, width_in:].reshape(device_count, row_count, -1)
    owner_notice = lax.dynamic_index_in_dim(
        owner_notice, spot_of[new_place[0] // holding], 0, keepdims=False
    )
    owner_scales = owner_notice[:, 2 * top_count : 2 * top_count + scale_cols]
    new_scales = lax.dynamic_index_in_dim(
        owner_scales.reshape(primary_scales.shape), new_place[0] % holding, 0
    )

    my_experts = experts.reshape(1, pair_count)
    _, _, my_served, my_cell = route(
        my_experts, replica.reshape(1, pair_count), place_all, holding
    )
    their_id = my_experts // holding
    block_at = (their_id // dev_count ^ my_group) * dev_count + (their_id % dev_count ^ my_dev)
    my_cell = (block_at * (holding * cells) + my_cell)[0]
    placed = (my_cell[:, None] == jnp.arange(cell_count)[None, :]) & my_served[0][:, None]
    selected = jnp.dot(
        placed.astype(jnp.bfloat16),
        returned.reshape(cell_count, hidden),
        preferred_element_type=jnp.float32,
    )
    weight = route_num.reshape(pair_count).astype(jnp.float32) / 16.0
    hidden_out = (selected * weight[:, None]).astype(jnp.bfloat16)
    hidden_out = hidden_out.reshape(row_count, top_count, hidden)
    return (new_weights, new_scales, hidden_out, slot_load)


def solution(mesh):
    in_specs = (
        P(AXES, None, None),
        P(AXES, None, None),
        P(AXES),
        P(AXES, None),
        P(AXES, None),
        P(AXES, None),
        P(AXES, None),
    )
    out_specs = (
        P(AXES, None, None),
        P(AXES, None, None),
        P(AXES, None, None),
        P(AXES, None),
    )
    return jax.shard_map(
        per_device, mesh=mesh, in_specs=in_specs, out_specs=out_specs, check_vma=False
    )
```

```python
import functools

import jax
import jax.numpy as jnp
from jax import lax
from jax.experimental import pallas as pl
from jax.experimental.pallas import tpu as pltpu
from jax.sharding import PartitionSpec as P

TILE = 128
CAP = 2
POOL = 16
ROW_CHIPS = 4
COMMON = 8
VMEM_LIMIT = 60 * 1024 * 1024
AXES = ("group", "dev")
PARTS = (128, 96)


def expert_kernel(x_ref, q_ref, s_ref, o_ref, acc_ref):
    step = pl.program_id(0)

    @pl.when(step == 0)
    def _():
        acc_ref[...] = jnp.zeros_like(acc_ref)

    holding, depth, _ = q_ref.shape
    cells = 2 * CAP
    rows = x_ref.shape[0]
    member_of = lax.broadcasted_iota(jnp.int32, (rows, TILE), 0) // cells % holding
    total = acc_ref[...]
    for member in range(holding):
        for block in range(depth // TILE):
            span = slice(block * TILE, (block + 1) * TILE)
            scale = s_ref[member, 0, block : block + 1, :]
            weights = (q_ref[member, span, :].astype(jnp.float32) * scale).astype(jnp.bfloat16)
            rows_in = jnp.where(member_of == member, x_ref[:, span], jnp.zeros((), jnp.bfloat16))
            total = total + jnp.dot(rows_in, weights, preferred_element_type=jnp.float32)
    acc_ref[...] = total

    @pl.when(step == pl.num_programs(0) - 1)
    def _():
        value = acc_ref[...]
        o_ref[...] = (value / (1.0 + jnp.exp(-value))).astype(jnp.bfloat16)


def serve(rows, values, scales):
    holding, width_in, hidden = values.shape
    depth = 512
    steps = width_in // depth
    count = rows.shape[0]
    wide = jnp.repeat(scales.astype(jnp.float32), TILE, axis=2)
    wide = wide.reshape(holding, steps, depth // TILE, hidden)
    return pl.pallas_call(
        expert_kernel,
        grid=(steps,),
        in_specs=[
            pl.BlockSpec((count, depth), lambda k: (0, k)),
            pl.BlockSpec((holding, depth, hidden), lambda k: (0, k, 0)),
            pl.BlockSpec((holding, 1, depth // TILE, hidden), lambda k: (0, k, 0, 0)),
        ],
        out_specs=pl.BlockSpec((count, hidden), lambda k: (0, 0)),
        out_shape=jax.ShapeDtypeStruct((count, hidden), jnp.bfloat16),
        scratch_shapes=[pltpu.VMEM((count, hidden), jnp.float32)],
        compiler_params=pltpu.CompilerParams(vmem_limit_bytes=VMEM_LIMIT),
        cost_estimate=pl.CostEstimate(
            flops=2 * count * width_in * hidden * holding,
            bytes_accessed=2 * (values.size + count * (width_in + hidden)),
            transcendentals=count * hidden,
        ),
    )(rows, values, wide)


def through_vmem(count, sources, out_at, held, in_sem, out_sem):
    def leave(spot):
        pltpu.make_async_copy(held.at[spot], held.at[spot], in_sem.at[spot]).wait()
        pltpu.make_async_copy(held.at[spot], out_at(spot), out_sem.at[spot]).start()

    def finish(spot):
        pltpu.make_async_copy(held.at[spot], out_at(spot), out_sem.at[spot]).wait()

    for stage in (sources, leave, finish):
        pl.loop(0, count)(stage)


def gather_kernel(index_ref, *refs):
    *source_refs, out_ref, held, in_sem, out_sem = refs

    def start(spot):
        index = index_ref[spot]
        base = 0
        for source_ref in source_refs:
            count = source_ref.shape[0]
            inside = (index >= base) & (index < base + count)
            at = jnp.clip(index - base, 0, count - 1)

            @pl.when(inside)
            def _():
                pltpu.make_async_copy(
                    source_ref.at[at], held.at[spot], in_sem.at[spot]
                ).start()

            base += count

    through_vmem(out_ref.shape[0], start, lambda spot: out_ref.at[spot], held, in_sem, out_sem)


def gather(indices, *sources):
    count = indices.shape[0]
    indices = jnp.clip(indices, 0, sum(source.shape[0] for source in sources) - 1)
    anywhere = pl.BlockSpec(memory_space=pl.ANY)
    out = jax.ShapeDtypeStruct((count,) + sources[0].shape[1:], sources[0].dtype)
    return pl.pallas_call(
        gather_kernel,
        in_specs=[pl.BlockSpec(memory_space=pltpu.SMEM)] + [anywhere] * len(sources),
        out_specs=anywhere,
        out_shape=out,
        scratch_shapes=[
            pltpu.VMEM(out.shape, out.dtype),
            pltpu.SemaphoreType.DMA((count,)),
            pltpu.SemaphoreType.DMA((count,)),
        ],
        compiler_params=pltpu.CompilerParams(vmem_limit_bytes=VMEM_LIMIT),
        cost_estimate=pl.CostEstimate(flops=0, bytes_accessed=4 * out.size, transcendentals=0),
    )(indices, *sources)


def chunk_kernel(first, in_ref, out_ref, held, in_sem, out_sem):
    height = out_ref.shape[2]

    def start(spot):
        pltpu.make_async_copy(
            in_ref.at[:, pl.ds(first + spot * height, height), :], held.at[spot], in_sem.at[spot]
        ).start()

    through_vmem(POOL, start, lambda spot: out_ref.at[spot], held, in_sem, out_sem)


def by_chunk(values, first, height):
    holding, _, hidden = values.shape
    anywhere = pl.BlockSpec(memory_space=pl.ANY)
    out = jax.ShapeDtypeStruct((POOL, holding, height, hidden), values.dtype)
    return pl.pallas_call(
        functools.partial(chunk_kernel, first),
        in_specs=[anywhere],
        out_specs=anywhere,
        out_shape=out,
        scratch_shapes=[
            pltpu.VMEM(out.shape, out.dtype),
            pltpu.SemaphoreType.DMA((POOL,)),
            pltpu.SemaphoreType.DMA((POOL,)),
        ],
        compiler_params=pltpu.CompilerParams(vmem_limit_bytes=VMEM_LIMIT),
        cost_estimate=pl.CostEstimate(
            flops=0, bytes_accessed=4 * out.size, transcendentals=0
        ),
    )(values)


def join_kernel(first, blocks_ref, *refs):
    out_ref, held, in_sem, out_sem = refs[-4:]
    count, height, _ = blocks_ref.shape

    def start(spot):
        pltpu.make_async_copy(blocks_ref.at[spot], held.at[spot], in_sem.at[spot]).start()

    def out_at(spot):
        return out_ref.at[0, pl.ds(first + spot * height, height), :]

    through_vmem(count, start, out_at, held, in_sem, out_sem)


def join(weights, blocks, first, width_in):
    count, _, hidden = blocks.shape
    anywhere = pl.BlockSpec(memory_space=pl.ANY)
    operands = (blocks,) if weights is None else (blocks, weights)
    return pl.pallas_call(
        functools.partial(join_kernel, first),
        in_specs=[anywhere] * len(operands),
        out_specs=anywhere,
        out_shape=jax.ShapeDtypeStruct((1, width_in, hidden), blocks.dtype),
        input_output_aliases={} if weights is None else {1: 0},
        scratch_shapes=[
            pltpu.VMEM(blocks.shape, blocks.dtype),
            pltpu.SemaphoreType.DMA((count,)),
            pltpu.SemaphoreType.DMA((count,)),
        ],
        compiler_params=pltpu.CompilerParams(vmem_limit_bytes=VMEM_LIMIT),
        cost_estimate=pl.CostEstimate(flops=0, bytes_accessed=4 * blocks.size, transcendentals=0),
    )(*operands)


def cross_over(count, leave_rows, give_rows, block, common, pairs):
    def branch_of(size):
        def branch(leave_rows, give_rows, block, common):
            if size == 0:
                return gather(give_rows, block, common)
            late = gather(leave_rows[COMMON : COMMON + size], block)
            return gather(give_rows, block, common, lax.ppermute(late, AXES, pairs))

        return branch

    branches = [branch_of(size) for size in range(POOL - COMMON + 1)]
    size = jnp.maximum(count - COMMON, 0)
    return lax.switch(size, branches, leave_rows, give_rows, block, common)


def route(experts, replica, place_all, holding):
    pair_count = experts.shape[1]
    device_ids = jnp.arange(place_all.shape[0], dtype=jnp.int32)
    matched = experts[:, :, None] == place_all[None, None, :]
    has_copy = jnp.any(matched, axis=2)
    holder = jnp.sum(jnp.where(matched, device_ids[None, None, :], 0), axis=2)
    use_copy = (replica == 1) & has_copy
    target = jnp.where(use_copy, holder, experts // holding)
    slot_id = jnp.where(use_copy, holding, experts % holding)
    pair_order = jnp.arange(pair_count)
    before = pair_order[:, None] < pair_order[None, :]
    position = jnp.sum((target[:, :, None] == target[:, None, :]) & before[None], axis=1)
    cell = experts % holding * (2 * CAP) + use_copy * CAP + position
    return target, slot_id, position < CAP, cell


def per_device(primary_q, primary_scales, new_place, tokens, experts, replica, route_num):
    holding, width_in, hidden = primary_q.shape
    dev_count = lax.axis_size("dev")
    group_count = lax.axis_size("group")
    device_count = dev_count * group_count
    half = dev_count // 2
    pooled = POOL // half
    my_dev = lax.axis_index("dev")
    my_group = lax.axis_index("group")
    first_dev = my_group * dev_count
    pools = [
        [(base + group) * dev_count + side * half + spot for group in range(pooled) for spot in range(half)]
        for base in range(0, group_count, pooled)
        for side in range(2)
    ]
    over = [
        (group * dev_count + spot, group * dev_count + (spot + half) % dev_count)
        for group in range(group_count)
        for spot in range(dev_count)
    ]

    device_ids = jnp.arange(device_count, dtype=jnp.int32)
    my_id = first_dev + my_dev

    place_all = lax.all_to_all(
        jnp.broadcast_to(new_place.astype(jnp.bfloat16), (device_count, TILE)),
        AXES,
        split_axis=0,
        concat_axis=0,
        tiled=True,
    )

    row_count, top_count = experts.shape
    pair_count = row_count * top_count
    scale_cols = primary_scales.size // row_count
    notice = jnp.concatenate(
        [
            experts.astype(jnp.bfloat16),
            replica.astype(jnp.bfloat16),
            primary_scales.reshape(row_count, scale_cols),
        ],
        axis=1,
    )
    notice = jnp.pad(notice, ((0, 0), (0, -notice.shape[1] % TILE)))
    held = jnp.concatenate([tokens, notice], axis=1)
    dev_bits = dev_count.bit_length() - 1
    all_bits = device_count.bit_length() - 1
    order = list(range(dev_bits))[::-1] + list(range(dev_bits, all_bits))[::-1]
    apart = device_ids ^ my_id
    spot_of = sum((apart >> bit & 1) << step for step, bit in enumerate(order))

    def double(held, bits):
        for bit in bits:
            pairs = [(device, device ^ 1 << bit) for device in range(device_count)]
            held = jnp.concatenate([held, lax.ppermute(held, AXES, pairs)], axis=0)
        return held

    first_height, second_height = PARTS
    held = double(held, order[:1])
    first, held = lax.optimization_barrier((by_chunk(primary_q, 0, first_height), held))
    held = double(held, order[1:dev_bits])

    place_all = place_all[:, 0].astype(jnp.int32)
    source = place_all // holding
    dest_side = device_ids % dev_count // half
    source_side = source % dev_count // half
    crossing = source_side != dest_side
    source_row = (source // dev_count % pooled * half + source % half) * holding + place_all % holding
    pool_of = device_ids // dev_count // pooled
    peers = (pool_of[:, None] == pool_of[None, :]) & (dest_side[:, None] == dest_side[None, :])
    ahead = peers & crossing[None, :] & (device_ids[None, :] < device_ids[:, None])
    rank = jnp.sum(ahead, axis=1)
    cross_count = jnp.max(jnp.where(crossing, rank + 1, 0))
    my_side = my_dev // half
    my_pool = my_group // pooled
    leaving = (pool_of == my_pool) & (dest_side != my_side) & crossing
    slots = jnp.arange(POOL)
    leave_rows = jnp.sum(
        jnp.where(leaving[None, :] & (rank[None, :] == slots[:, None]), source_row[None, :], 0), axis=1
    )
    staying = (pool_of == my_pool) & (dest_side == my_side)
    place_in_pool = device_ids // dev_count % pooled * half + device_ids % half
    give_rows = jnp.sum(
        jnp.where(
            staying[None, :] & (place_in_pool[None, :] == slots[:, None]),
            jnp.where(crossing, POOL * holding + rank, source_row)[None, :],
            0,
        ),
        axis=1,
    )

    def spread_over(block):
        block = lax.all_to_all(
            block, AXES, split_axis=0, concat_axis=0, tiled=True, axis_index_groups=pools
        )
        return block.reshape((POOL * holding,) + block.shape[2:])

    first, held, place_all, leave_rows, give_rows, cross_count = lax.optimization_barrier(
        (first, held, place_all, leave_rows, give_rows, cross_count)
    )
    first = spread_over(first)
    second = by_chunk(primary_q, POOL * first_height, second_height)
    held, second = lax.optimization_barrier((held, second))
    held = double(held, order[dev_bits:-1])
    held, second = lax.optimization_barrier((held, second))
    second = spread_over(second)

    cells = 2 * CAP
    cell_count = device_count * holding * cells

    def pairs_of(held):
        notices = held[:, width_in:].reshape(device_count, row_count, -1)[spot_of]
        experts_all = notices[:, :, :top_count].astype(jnp.int32)
        replica_all = notices[:, :, top_count : 2 * top_count].astype(jnp.int32)
        return [each.reshape(device_count, pair_count) for each in (experts_all, replica_all)]

    def work(held, place_all, values, scales):
        experts_all, replica_all = pairs_of(held)
        _, _, served, cell = route(experts_all, replica_all, place_all, holding)
        mine = served & (experts_all // holding == my_id)
        cell_ids = jnp.arange(holding * cells)
        hit = mine[:, None, :] & (cell[:, None, :] == cell_ids[None, :, None])
        row_at = spot_of[:, None] * row_count + jnp.sum(
            jnp.where(hit, jnp.arange(pair_count) // top_count, 0), axis=2
        )
        row_at = jnp.where(jnp.any(hit, axis=2), row_at, -1).reshape(cell_count)
        row_hits = row_at[:, None] == jnp.arange(device_count * row_count)[None, :]
        rows = jnp.dot(row_hits.astype(jnp.bfloat16), held, preferred_element_type=jnp.float32)
        return serve(rows.astype(jnp.bfloat16), values, scales)

    sent = gather(leave_rows[:COMMON], first)
    sent, held = lax.optimization_barrier((sent, held))
    common = lax.ppermute(sent, AXES, over)
    held = double(held, order[-1:])
    activated = work(held, place_all, primary_q, primary_scales)

    columns = dev_count // ROW_CHIPS

    def exchange(blocks, axis, mine, stride, within):
        got = [lax.dynamic_index_in_dim(blocks, mine, axis, keepdims=False)]
        for step in range(1, blocks.shape[axis]):
            pairs = [
                (device, device ^ step * stride) for device in range(device_count)
            ]
            block = lax.dynamic_index_in_dim(blocks, mine ^ step, axis, keepdims=False)
            got.append(lax.ppermute(block, AXES, pairs))
        return jnp.stack(got, axis=within)

    blocks = activated.reshape(group_count, ROW_CHIPS, columns, holding * cells, hidden)
    blocks = exchange(blocks, 1, my_dev // columns, columns, 1)
    common, blocks = lax.optimization_barrier((common, blocks))
    first = cross_over(cross_count, leave_rows, give_rows, first, common, over)
    first, leave_rows, blocks = lax.optimization_barrier((first, leave_rows, blocks))
    sent = gather(leave_rows[:COMMON], second)
    sent, blocks = lax.optimization_barrier((sent, blocks))
    common = lax.ppermute(sent, AXES, over)
    blocks = exchange(blocks, 2, my_dev % columns, 1, 1)
    returned = exchange(blocks, 0, my_group, dev_count, 0)
    first = lax.all_to_all(
        first, AXES, split_axis=0, concat_axis=0, tiled=True, axis_index_groups=pools
    )
    second = cross_over(cross_count, leave_rows, give_rows, second, common, over)
    second, held = lax.optimization_barrier((second, held))
    second = lax.all_to_all(
        second, AXES, split_axis=0, concat_axis=0, tiled=True, axis_index_groups=pools
    )
    new_weights = join(None, first, 0, width_in)
    new_weights = join(new_weights, second, first.shape[0] * first.shape[1], width_in)

    experts_all, replica_all = pairs_of(held)
    target, slot_id, served, _ = route(experts_all, replica_all, place_all, holding)
    arriving = served & (target == my_id)
    slot_load = jnp.stack(
        [jnp.sum((arriving & (slot_id == slot)).astype(jnp.int32)) for slot in range(holding + 1)]
    )[None]
    owner_notice = held[:, width_in:].reshape(device_count, row_count, -1)
    owner_notice = lax.dynamic_index_in_dim(
        owner_notice, spot_of[new_place[0] // holding], 0, keepdims=False
    )
    owner_scales = owner_notice[:, 2 * top_count : 2 * top_count + scale_cols]
    new_scales = lax.dynamic_index_in_dim(
        owner_scales.reshape(primary_scales.shape), new_place[0] % holding, 0
    )

    my_experts = experts.reshape(1, pair_count)
    _, _, my_served, my_cell = route(
        my_experts, replica.reshape(1, pair_count), place_all, holding
    )
    their_id = my_experts // holding
    apart = their_id ^ my_id
    block_at = apart // dev_count * columns + apart % columns
    block_at = block_at * ROW_CHIPS + apart % dev_count // columns
    my_cell = (block_at * (holding * cells) + my_cell)[0]
    placed = (my_cell[:, None] == jnp.arange(cell_count)[None, :]) & my_served[0][:, None]
    selected = jnp.dot(
        placed.astype(jnp.bfloat16),
        returned.reshape(cell_count, hidden),
        preferred_element_type=jnp.float32,
    )
    weight = route_num.reshape(pair_count).astype(jnp.float32) / 16.0
    hidden_out = (selected * weight[:, None]).astype(jnp.bfloat16)
    hidden_out = hidden_out.reshape(row_count, top_count, hidden)
    return (new_weights, new_scales, hidden_out, slot_load)


def solution(mesh):
    in_specs = (
        P(AXES, None, None),
        P(AXES, None, None),
        P(AXES),
        P(AXES, None),
        P(AXES, None),
        P(AXES, None),
        P(AXES, None),
    )
    out_specs = (
        P(AXES, None, None),
        P(AXES, None, None),
        P(AXES, None, None),
        P(AXES, None),
    )
    return jax.shard_map(
        per_device, mesh=mesh, in_specs=in_specs, out_specs=out_specs, check_vma=False
    )
```

```python
import functools

import jax
import jax.numpy as jnp
from jax import lax
from jax.experimental import pallas as pl
from jax.experimental.pallas import tpu as pltpu
from jax.sharding import PartitionSpec as P

TILE = 128
CAP = 2
POOL = 16
ROW_CHIPS = 4
COMMON = 8
VMEM_LIMIT = 60 * 1024 * 1024
AXES = ("group", "dev")
PARTS = (128, 96)


def expert_kernel(x_ref, q_ref, s_ref, o_ref, acc_ref):
    step = pl.program_id(0)

    @pl.when(step == 0)
    def _():
        acc_ref[...] = jnp.zeros_like(acc_ref)

    holding, depth, _ = q_ref.shape
    cells = 2 * CAP
    rows = x_ref.shape[0]
    member_of = lax.broadcasted_iota(jnp.int32, (rows, TILE), 0) // cells % holding
    total = acc_ref[...]
    for member in range(holding):
        for block in range(depth // TILE):
            span = slice(block * TILE, (block + 1) * TILE)
            scale = s_ref[member, 0, block : block + 1, :]
            weights = (q_ref[member, span, :].astype(jnp.float32) * scale).astype(jnp.bfloat16)
            rows_in = jnp.where(member_of == member, x_ref[:, span], jnp.zeros((), jnp.bfloat16))
            total = total + jnp.dot(rows_in, weights, preferred_element_type=jnp.float32)
    acc_ref[...] = total

    @pl.when(step == pl.num_programs(0) - 1)
    def _():
        value = acc_ref[...]
        o_ref[...] = (value / (1.0 + jnp.exp(-value))).astype(jnp.bfloat16)


def serve(rows, values, scales):
    holding, width_in, hidden = values.shape
    depth = 512
    steps = width_in // depth
    count = rows.shape[0]
    wide = jnp.repeat(scales.astype(jnp.float32), TILE, axis=2)
    wide = wide.reshape(holding, steps, depth // TILE, hidden)
    return pl.pallas_call(
        expert_kernel,
        grid=(steps,),
        in_specs=[
            pl.BlockSpec((count, depth), lambda k: (0, k)),
            pl.BlockSpec((holding, depth, hidden), lambda k: (0, k, 0)),
            pl.BlockSpec((holding, 1, depth // TILE, hidden), lambda k: (0, k, 0, 0)),
        ],
        out_specs=pl.BlockSpec((count, hidden), lambda k: (0, 0)),
        out_shape=jax.ShapeDtypeStruct((count, hidden), jnp.bfloat16),
        scratch_shapes=[pltpu.VMEM((count, hidden), jnp.float32)],
        compiler_params=pltpu.CompilerParams(vmem_limit_bytes=VMEM_LIMIT),
        cost_estimate=pl.CostEstimate(
            flops=2 * count * width_in * hidden * holding,
            bytes_accessed=2 * (values.size + count * (width_in + hidden)),
            transcendentals=count * hidden,
        ),
    )(rows, values, wide)


def through_vmem(count, sources, out_at, held, in_sem, out_sem):
    def leave(spot):
        pltpu.make_async_copy(held.at[spot], held.at[spot], in_sem.at[spot]).wait()
        pltpu.make_async_copy(held.at[spot], out_at(spot), out_sem.at[spot]).start()

    def finish(spot):
        pltpu.make_async_copy(held.at[spot], out_at(spot), out_sem.at[spot]).wait()

    for stage in (sources, leave, finish):
        pl.loop(0, count)(stage)


def gather_kernel(index_ref, *refs):
    *source_refs, out_ref, held, in_sem, out_sem = refs

    def start(spot):
        index = index_ref[spot]
        base = 0
        for source_ref in source_refs:
            count = source_ref.shape[0]
            inside = (index >= base) & (index < base + count)
            at = jnp.clip(index - base, 0, count - 1)

            @pl.when(inside)
            def _():
                pltpu.make_async_copy(
                    source_ref.at[at], held.at[spot], in_sem.at[spot]
                ).start()

            base += count

    through_vmem(out_ref.shape[0], start, lambda spot: out_ref.at[spot], held, in_sem, out_sem)


def gather(indices, *sources):
    count = indices.shape[0]
    indices = jnp.clip(indices, 0, sum(source.shape[0] for source in sources) - 1)
    anywhere = pl.BlockSpec(memory_space=pl.ANY)
    out = jax.ShapeDtypeStruct((count,) + sources[0].shape[1:], sources[0].dtype)
    return pl.pallas_call(
        gather_kernel,
        in_specs=[pl.BlockSpec(memory_space=pltpu.SMEM)] + [anywhere] * len(sources),
        out_specs=anywhere,
        out_shape=out,
        scratch_shapes=[
            pltpu.VMEM(out.shape, out.dtype),
            pltpu.SemaphoreType.DMA((count,)),
            pltpu.SemaphoreType.DMA((count,)),
        ],
        compiler_params=pltpu.CompilerParams(vmem_limit_bytes=VMEM_LIMIT),
        cost_estimate=pl.CostEstimate(flops=0, bytes_accessed=4 * out.size, transcendentals=0),
    )(indices, *sources)


def chunk_kernel(first, in_ref, out_ref, held, in_sem, out_sem):
    height = out_ref.shape[2]

    def start(spot):
        pltpu.make_async_copy(
            in_ref.at[:, pl.ds(first + spot * height, height), :], held.at[spot], in_sem.at[spot]
        ).start()

    through_vmem(POOL, start, lambda spot: out_ref.at[spot], held, in_sem, out_sem)


def by_chunk(values, first, height):
    holding, _, hidden = values.shape
    anywhere = pl.BlockSpec(memory_space=pl.ANY)
    out = jax.ShapeDtypeStruct((POOL, holding, height, hidden), values.dtype)
    return pl.pallas_call(
        functools.partial(chunk_kernel, first),
        in_specs=[anywhere],
        out_specs=anywhere,
        out_shape=out,
        scratch_shapes=[
            pltpu.VMEM(out.shape, out.dtype),
            pltpu.SemaphoreType.DMA((POOL,)),
            pltpu.SemaphoreType.DMA((POOL,)),
        ],
        compiler_params=pltpu.CompilerParams(vmem_limit_bytes=VMEM_LIMIT),
        cost_estimate=pl.CostEstimate(
            flops=0, bytes_accessed=4 * out.size, transcendentals=0
        ),
    )(values)


def join_kernel(first, blocks_ref, *refs):
    out_ref, held, in_sem, out_sem = refs[-4:]
    count, height, _ = blocks_ref.shape

    def start(spot):
        pltpu.make_async_copy(blocks_ref.at[spot], held.at[spot], in_sem.at[spot]).start()

    def out_at(spot):
        return out_ref.at[0, pl.ds(first + spot * height, height), :]

    through_vmem(count, start, out_at, held, in_sem, out_sem)


def join(weights, blocks, first, width_in):
    count, _, hidden = blocks.shape
    anywhere = pl.BlockSpec(memory_space=pl.ANY)
    operands = (blocks,) if weights is None else (blocks, weights)
    return pl.pallas_call(
        functools.partial(join_kernel, first),
        in_specs=[anywhere] * len(operands),
        out_specs=anywhere,
        out_shape=jax.ShapeDtypeStruct((1, width_in, hidden), blocks.dtype),
        input_output_aliases={} if weights is None else {1: 0},
        scratch_shapes=[
            pltpu.VMEM(blocks.shape, blocks.dtype),
            pltpu.SemaphoreType.DMA((count,)),
            pltpu.SemaphoreType.DMA((count,)),
        ],
        compiler_params=pltpu.CompilerParams(vmem_limit_bytes=VMEM_LIMIT),
        cost_estimate=pl.CostEstimate(flops=0, bytes_accessed=4 * blocks.size, transcendentals=0),
    )(*operands)


def cross_over(count, leave_rows, give_rows, block, common, pairs):
    def branch_of(size):
        def branch(leave_rows, give_rows, block, common):
            if size == 0:
                return gather(give_rows, block, common)
            late = gather(leave_rows[COMMON : COMMON + size], block)
            return gather(give_rows, block, common, lax.ppermute(late, AXES, pairs))

        return branch

    branches = [branch_of(size) for size in range(POOL - COMMON + 1)]
    size = jnp.maximum(count - COMMON, 0)
    return lax.switch(size, branches, leave_rows, give_rows, block, common)


def route(experts, replica, place_all, holding):
    pair_count = experts.shape[1]
    device_ids = jnp.arange(place_all.shape[0], dtype=jnp.int32)
    matched = experts[:, :, None] == place_all[None, None, :]
    has_copy = jnp.any(matched, axis=2)
    holder = jnp.sum(jnp.where(matched, device_ids[None, None, :], 0), axis=2)
    use_copy = (replica == 1) & has_copy
    target = jnp.where(use_copy, holder, experts // holding)
    slot_id = jnp.where(use_copy, holding, experts % holding)
    pair_order = jnp.arange(pair_count)
    before = pair_order[:, None] < pair_order[None, :]
    position = jnp.sum((target[:, :, None] == target[:, None, :]) & before[None], axis=1)
    cell = experts % holding * (2 * CAP) + use_copy * CAP + position
    return target, slot_id, position < CAP, cell


def per_device(primary_q, primary_scales, new_place, tokens, experts, replica, route_num):
    holding, width_in, hidden = primary_q.shape
    dev_count = lax.axis_size("dev")
    group_count = lax.axis_size("group")
    device_count = dev_count * group_count
    half = dev_count // 2
    pooled = POOL // half
    my_dev = lax.axis_index("dev")
    my_group = lax.axis_index("group")
    first_dev = my_group * dev_count
    pools = [
        [(base + group) * dev_count + side * half + spot for group in range(pooled) for spot in range(half)]
        for base in range(0, group_count, pooled)
        for side in range(2)
    ]
    over = [
        (group * dev_count + spot, group * dev_count + (spot + half) % dev_count)
        for group in range(group_count)
        for spot in range(dev_count)
    ]

    device_ids = jnp.arange(device_count, dtype=jnp.int32)
    my_id = first_dev + my_dev

    row_count, top_count = experts.shape
    pair_count = row_count * top_count
    scale_cols = primary_scales.size // row_count
    notice = jnp.concatenate(
        [
            experts.astype(jnp.bfloat16),
            replica.astype(jnp.bfloat16),
            primary_scales.reshape(row_count, scale_cols),
        ],
        axis=1,
    )
    notice = jnp.pad(notice, ((0, 0), (0, -notice.shape[1] % TILE)))
    held = jnp.concatenate([tokens, notice], axis=1)
    dev_bits = dev_count.bit_length() - 1
    all_bits = device_count.bit_length() - 1
    order = list(range(dev_bits))[::-1] + list(range(dev_bits, all_bits))[::-1]
    apart = device_ids ^ my_id
    spot_of = sum((apart >> bit & 1) << step for step, bit in enumerate(order))

    def double(held, bits):
        for bit in bits:
            pairs = [(device, device ^ 1 << bit) for device in range(device_count)]
            held = jnp.concatenate([held, lax.ppermute(held, AXES, pairs)], axis=0)
        return held

    first_height, second_height = PARTS
    held = double(held, order[:1])
    place_all = jnp.broadcast_to(new_place.astype(jnp.bfloat16), (device_count, TILE))
    first, place_all = lax.optimization_barrier(
        (by_chunk(primary_q, 0, first_height), place_all)
    )
    first, held = lax.optimization_barrier((first, held))
    held = double(held, order[1:dev_bits])

    place_all = lax.all_to_all(
        place_all,
        AXES,
        split_axis=0,
        concat_axis=0,
        tiled=True,
    )

    place_all = place_all[:, 0].astype(jnp.int32)
    source = place_all // holding
    dest_side = device_ids % dev_count // half
    source_side = source % dev_count // half
    crossing = source_side != dest_side
    source_row = (source // dev_count % pooled * half + source % half) * holding + place_all % holding
    pool_of = device_ids // dev_count // pooled
    peers = (pool_of[:, None] == pool_of[None, :]) & (dest_side[:, None] == dest_side[None, :])
    ahead = peers & crossing[None, :] & (device_ids[None, :] < device_ids[:, None])
    rank = jnp.sum(ahead, axis=1)
    cross_count = jnp.max(jnp.where(crossing, rank + 1, 0))
    my_side = my_dev // half
    my_pool = my_group // pooled
    leaving = (pool_of == my_pool) & (dest_side != my_side) & crossing
    slots = jnp.arange(POOL)
    leave_rows = jnp.sum(
        jnp.where(leaving[None, :] & (rank[None, :] == slots[:, None]), source_row[None, :], 0), axis=1
    )
    staying = (pool_of == my_pool) & (dest_side == my_side)
    place_in_pool = device_ids // dev_count % pooled * half + device_ids % half
    give_rows = jnp.sum(
        jnp.where(
            staying[None, :] & (place_in_pool[None, :] == slots[:, None]),
            jnp.where(crossing, POOL * holding + rank, source_row)[None, :],
            0,
        ),
        axis=1,
    )

    def spread_over(block):
        block = lax.all_to_all(
            block, AXES, split_axis=0, concat_axis=0, tiled=True, axis_index_groups=pools
        )
        return block.reshape((POOL * holding,) + block.shape[2:])

    first, held, place_all, leave_rows, give_rows, cross_count = lax.optimization_barrier(
        (first, held, place_all, leave_rows, give_rows, cross_count)
    )
    first = spread_over(first)
    second = by_chunk(primary_q, POOL * first_height, second_height)
    held, second = lax.optimization_barrier((held, second))
    held = double(held, order[dev_bits:-1])
    held, second = lax.optimization_barrier((held, second))
    second = spread_over(second)

    cells = 2 * CAP
    cell_count = device_count * holding * cells

    def pairs_of(held):
        notices = held[:, width_in:].reshape(device_count, row_count, -1)[spot_of]
        experts_all = notices[:, :, :top_count].astype(jnp.int32)
        replica_all = notices[:, :, top_count : 2 * top_count].astype(jnp.int32)
        return [each.reshape(device_count, pair_count) for each in (experts_all, replica_all)]

    def work(held, place_all, values, scales):
        experts_all, replica_all = pairs_of(held)
        _, _, served, cell = route(experts_all, replica_all, place_all, holding)
        mine = served & (experts_all // holding == my_id)
        cell_ids = jnp.arange(holding * cells)
        hit = mine[:, None, :] & (cell[:, None, :] == cell_ids[None, :, None])
        row_at = spot_of[:, None] * row_count + jnp.sum(
            jnp.where(hit, jnp.arange(pair_count) // top_count, 0), axis=2
        )
        row_at = jnp.where(jnp.any(hit, axis=2), row_at, -1).reshape(cell_count)
        row_hits = row_at[:, None] == jnp.arange(device_count * row_count)[None, :]
        rows = jnp.dot(row_hits.astype(jnp.bfloat16), held, preferred_element_type=jnp.float32)
        return serve(rows.astype(jnp.bfloat16), values, scales)

    sent = gather(leave_rows[:COMMON], first)
    sent, held = lax.optimization_barrier((sent, held))
    common = lax.ppermute(sent, AXES, over)
    held = double(held, order[-1:])
    activated = work(held, place_all, primary_q, primary_scales)

    columns = dev_count // ROW_CHIPS

    def exchange(blocks, axis, mine, stride, within):
        got = [lax.dynamic_index_in_dim(blocks, mine, axis, keepdims=False)]
        for step in range(1, blocks.shape[axis]):
            pairs = [
                (device, device ^ step * stride) for device in range(device_count)
            ]
            block = lax.dynamic_index_in_dim(blocks, mine ^ step, axis, keepdims=False)
            got.append(lax.ppermute(block, AXES, pairs))
        return jnp.stack(got, axis=within)

    blocks = activated.reshape(group_count, ROW_CHIPS, columns, holding * cells, hidden)
    blocks = exchange(blocks, 1, my_dev // columns, columns, 1)
    common, blocks = lax.optimization_barrier((common, blocks))
    first = cross_over(cross_count, leave_rows, give_rows, first, common, over)
    first, leave_rows, blocks = lax.optimization_barrier((first, leave_rows, blocks))
    sent = gather(leave_rows[:COMMON], second)
    sent, blocks = lax.optimization_barrier((sent, blocks))
    common = lax.ppermute(sent, AXES, over)
    blocks = exchange(blocks, 2, my_dev % columns, 1, 1)
    returned = exchange(blocks, 0, my_group, dev_count, 0)
    common, returned = lax.optimization_barrier((common, returned))
    first = lax.all_to_all(
        first, AXES, split_axis=0, concat_axis=0, tiled=True, axis_index_groups=pools
    )
    second = cross_over(cross_count, leave_rows, give_rows, second, common, over)
    second, held = lax.optimization_barrier((second, held))
    second = lax.all_to_all(
        second, AXES, split_axis=0, concat_axis=0, tiled=True, axis_index_groups=pools
    )
    new_weights = join(None, first, 0, width_in)
    new_weights = join(new_weights, second, first.shape[0] * first.shape[1], width_in)

    experts_all, replica_all = pairs_of(held)
    target, slot_id, served, _ = route(experts_all, replica_all, place_all, holding)
    arriving = served & (target == my_id)
    slot_load = jnp.stack(
        [jnp.sum((arriving & (slot_id == slot)).astype(jnp.int32)) for slot in range(holding + 1)]
    )[None]
    owner_notice = held[:, width_in:].reshape(device_count, row_count, -1)
    owner_notice = lax.dynamic_index_in_dim(
        owner_notice, spot_of[new_place[0] // holding], 0, keepdims=False
    )
    owner_scales = owner_notice[:, 2 * top_count : 2 * top_count + scale_cols]
    new_scales = lax.dynamic_index_in_dim(
        owner_scales.reshape(primary_scales.shape), new_place[0] % holding, 0
    )

    my_experts = experts.reshape(1, pair_count)
    _, _, my_served, my_cell = route(
        my_experts, replica.reshape(1, pair_count), place_all, holding
    )
    their_id = my_experts // holding
    apart = their_id ^ my_id
    block_at = apart // dev_count * columns + apart % columns
    block_at = block_at * ROW_CHIPS + apart % dev_count // columns
    my_cell = (block_at * (holding * cells) + my_cell)[0]
    placed = (my_cell[:, None] == jnp.arange(cell_count)[None, :]) & my_served[0][:, None]
    selected = jnp.dot(
        placed.astype(jnp.bfloat16),
        returned.reshape(cell_count, hidden),
        preferred_element_type=jnp.float32,
    )
    weight = route_num.reshape(pair_count).astype(jnp.float32) / 16.0
    hidden_out = (selected * weight[:, None]).astype(jnp.bfloat16)
    hidden_out = hidden_out.reshape(row_count, top_count, hidden)
    return (new_weights, new_scales, hidden_out, slot_load)


def solution(mesh):
    in_specs = (
        P(AXES, None, None),
        P(AXES, None, None),
        P(AXES),
        P(AXES, None),
        P(AXES, None),
        P(AXES, None),
        P(AXES, None),
    )
    out_specs = (
        P(AXES, None, None),
        P(AXES, None, None),
        P(AXES, None, None),
        P(AXES, None),
    )
    return jax.shard_map(
        per_device, mesh=mesh, in_specs=in_specs, out_specs=out_specs, check_vma=False
    )
```

```python
import functools

import jax
import jax.numpy as jnp
from jax import lax
from jax.experimental import pallas as pl
from jax.experimental.pallas import tpu as pltpu
from jax.sharding import PartitionSpec as P

TILE = 128
CAP = 2
POOL = 16
ROW_CHIPS = 4
COMMON = 8
VMEM_LIMIT = 60 * 1024 * 1024
AXES = ("group", "dev")
PARTS = (128, 96)


def expert_kernel(x_ref, q_ref, s_ref, o_ref, acc_ref):
    step = pl.program_id(0)

    @pl.when(step == 0)
    def _():
        acc_ref[...] = jnp.zeros_like(acc_ref)

    holding, depth, _ = q_ref.shape
    cells = 2 * CAP
    rows = x_ref.shape[0]
    member_of = lax.broadcasted_iota(jnp.int32, (rows, TILE), 0) // cells % holding
    total = acc_ref[...]
    for member in range(holding):
        for block in range(depth // TILE):
            span = slice(block * TILE, (block + 1) * TILE)
            scale = s_ref[member, 0, block : block + 1, :]
            weights = (q_ref[member, span, :].astype(jnp.float32) * scale).astype(jnp.bfloat16)
            rows_in = jnp.where(member_of == member, x_ref[:, span], jnp.zeros((), jnp.bfloat16))
            total = total + jnp.dot(rows_in, weights, preferred_element_type=jnp.float32)
    acc_ref[...] = total

    @pl.when(step == pl.num_programs(0) - 1)
    def _():
        value = acc_ref[...]
        o_ref[...] = (value / (1.0 + jnp.exp(-value))).astype(jnp.bfloat16)


def serve(rows, values, scales):
    holding, width_in, hidden = values.shape
    depth = 512
    steps = width_in // depth
    count = rows.shape[0]
    wide = jnp.repeat(scales.astype(jnp.float32), TILE, axis=2)
    wide = wide.reshape(holding, steps, depth // TILE, hidden)
    return pl.pallas_call(
        expert_kernel,
        grid=(steps,),
        in_specs=[
            pl.BlockSpec((count, depth), lambda k: (0, k)),
            pl.BlockSpec((holding, depth, hidden), lambda k: (0, k, 0)),
            pl.BlockSpec((holding, 1, depth // TILE, hidden), lambda k: (0, k, 0, 0)),
        ],
        out_specs=pl.BlockSpec((count, hidden), lambda k: (0, 0)),
        out_shape=jax.ShapeDtypeStruct((count, hidden), jnp.bfloat16),
        scratch_shapes=[pltpu.VMEM((count, hidden), jnp.float32)],
        compiler_params=pltpu.CompilerParams(vmem_limit_bytes=VMEM_LIMIT),
        cost_estimate=pl.CostEstimate(
            flops=2 * count * width_in * hidden * holding,
            bytes_accessed=2 * (values.size + count * (width_in + hidden)),
            transcendentals=count * hidden,
        ),
    )(rows, values, wide)


def through_vmem(count, sources, out_at, held, in_sem, out_sem):
    def leave(spot):
        pltpu.make_async_copy(held.at[spot], held.at[spot], in_sem.at[spot]).wait()
        pltpu.make_async_copy(held.at[spot], out_at(spot), out_sem.at[spot]).start()

    def finish(spot):
        pltpu.make_async_copy(held.at[spot], out_at(spot), out_sem.at[spot]).wait()

    for stage in (sources, leave, finish):
        pl.loop(0, count)(stage)


def gather_kernel(index_ref, *refs):
    *source_refs, out_ref, held, in_sem, out_sem = refs

    def start(spot):
        index = index_ref[spot]
        base = 0
        for source_ref in source_refs:
            count = source_ref.shape[0]
            inside = (index >= base) & (index < base + count)
            at = jnp.clip(index - base, 0, count - 1)

            @pl.when(inside)
            def _():
                pltpu.make_async_copy(
                    source_ref.at[at], held.at[spot], in_sem.at[spot]
                ).start()

            base += count

    through_vmem(out_ref.shape[0], start, lambda spot: out_ref.at[spot], held, in_sem, out_sem)


def gather(indices, *sources):
    count = indices.shape[0]
    indices = jnp.clip(indices, 0, sum(source.shape[0] for source in sources) - 1)
    anywhere = pl.BlockSpec(memory_space=pl.ANY)
    out = jax.ShapeDtypeStruct((count,) + sources[0].shape[1:], sources[0].dtype)
    return pl.pallas_call(
        gather_kernel,
        in_specs=[pl.BlockSpec(memory_space=pltpu.SMEM)] + [anywhere] * len(sources),
        out_specs=anywhere,
        out_shape=out,
        scratch_shapes=[
            pltpu.VMEM(out.shape, out.dtype),
            pltpu.SemaphoreType.DMA((count,)),
            pltpu.SemaphoreType.DMA((count,)),
        ],
        compiler_params=pltpu.CompilerParams(vmem_limit_bytes=VMEM_LIMIT),
        cost_estimate=pl.CostEstimate(flops=0, bytes_accessed=4 * out.size, transcendentals=0),
    )(indices, *sources)


def chunk_kernel(first, in_ref, out_ref, held, in_sem, out_sem):
    height = out_ref.shape[2]

    def start(spot):
        pltpu.make_async_copy(
            in_ref.at[:, pl.ds(first + spot * height, height), :], held.at[spot], in_sem.at[spot]
        ).start()

    through_vmem(POOL, start, lambda spot: out_ref.at[spot], held, in_sem, out_sem)


def by_chunk(values, first, height):
    holding, _, hidden = values.shape
    anywhere = pl.BlockSpec(memory_space=pl.ANY)
    out = jax.ShapeDtypeStruct((POOL, holding, height, hidden), values.dtype)
    return pl.pallas_call(
        functools.partial(chunk_kernel, first),
        in_specs=[anywhere],
        out_specs=anywhere,
        out_shape=out,
        scratch_shapes=[
            pltpu.VMEM(out.shape, out.dtype),
            pltpu.SemaphoreType.DMA((POOL,)),
            pltpu.SemaphoreType.DMA((POOL,)),
        ],
        compiler_params=pltpu.CompilerParams(vmem_limit_bytes=VMEM_LIMIT),
        cost_estimate=pl.CostEstimate(
            flops=0, bytes_accessed=4 * out.size, transcendentals=0
        ),
    )(values)


def join_kernel(first, blocks_ref, *refs):
    out_ref, held, in_sem, out_sem = refs[-4:]
    count, height, _ = blocks_ref.shape

    def start(spot):
        pltpu.make_async_copy(blocks_ref.at[spot], held.at[spot], in_sem.at[spot]).start()

    def out_at(spot):
        return out_ref.at[0, pl.ds(first + spot * height, height), :]

    through_vmem(count, start, out_at, held, in_sem, out_sem)


def join(weights, blocks, first, width_in):
    count, _, hidden = blocks.shape
    anywhere = pl.BlockSpec(memory_space=pl.ANY)
    operands = (blocks,) if weights is None else (blocks, weights)
    return pl.pallas_call(
        functools.partial(join_kernel, first),
        in_specs=[anywhere] * len(operands),
        out_specs=anywhere,
        out_shape=jax.ShapeDtypeStruct((1, width_in, hidden), blocks.dtype),
        input_output_aliases={} if weights is None else {1: 0},
        scratch_shapes=[
            pltpu.VMEM(blocks.shape, blocks.dtype),
            pltpu.SemaphoreType.DMA((count,)),
            pltpu.SemaphoreType.DMA((count,)),
        ],
        compiler_params=pltpu.CompilerParams(vmem_limit_bytes=VMEM_LIMIT),
        cost_estimate=pl.CostEstimate(flops=0, bytes_accessed=4 * blocks.size, transcendentals=0),
    )(*operands)


def cross_over(count, leave_rows, give_rows, block, common, pairs):
    def branch_of(size):
        def branch(leave_rows, give_rows, block, common):
            if size == 0:
                return gather(give_rows, block, common)
            late = gather(leave_rows[COMMON : COMMON + size], block)
            return gather(give_rows, block, common, lax.ppermute(late, AXES, pairs))

        return branch

    branches = [branch_of(size) for size in range(POOL - COMMON + 1)]
    size = jnp.maximum(count - COMMON, 0)
    return lax.switch(size, branches, leave_rows, give_rows, block, common)


def route(experts, replica, place_all, holding):
    pair_count = experts.shape[1]
    device_ids = jnp.arange(place_all.shape[0], dtype=jnp.int32)
    matched = experts[:, :, None] == place_all[None, None, :]
    has_copy = jnp.any(matched, axis=2)
    holder = jnp.sum(jnp.where(matched, device_ids[None, None, :], 0), axis=2)
    use_copy = (replica == 1) & has_copy
    target = jnp.where(use_copy, holder, experts // holding)
    slot_id = jnp.where(use_copy, holding, experts % holding)
    pair_order = jnp.arange(pair_count)
    before = pair_order[:, None] < pair_order[None, :]
    position = jnp.sum((target[:, :, None] == target[:, None, :]) & before[None], axis=1)
    cell = experts % holding * (2 * CAP) + use_copy * CAP + position
    return target, slot_id, position < CAP, cell


def per_device(primary_q, primary_scales, new_place, tokens, experts, replica, route_num):
    holding, width_in, hidden = primary_q.shape
    dev_count = lax.axis_size("dev")
    group_count = lax.axis_size("group")
    device_count = dev_count * group_count
    half = dev_count // 2
    pooled = POOL // half
    my_dev = lax.axis_index("dev")
    my_group = lax.axis_index("group")
    first_dev = my_group * dev_count
    pools = [
        [(base + group) * dev_count + side * half + spot for group in range(pooled) for spot in range(half)]
        for base in range(0, group_count, pooled)
        for side in range(2)
    ]
    over = [
        (group * dev_count + spot, group * dev_count + (spot + half) % dev_count)
        for group in range(group_count)
        for spot in range(dev_count)
    ]

    device_ids = jnp.arange(device_count, dtype=jnp.int32)
    my_id = first_dev + my_dev

    row_count, top_count = experts.shape
    pair_count = row_count * top_count
    scale_cols = primary_scales.size // row_count
    notice = jnp.concatenate(
        [
            experts.astype(jnp.bfloat16),
            replica.astype(jnp.bfloat16),
            primary_scales.reshape(row_count, scale_cols),
        ],
        axis=1,
    )
    notice = jnp.pad(notice, ((0, 0), (0, -notice.shape[1] % TILE)))
    held = jnp.concatenate([tokens, notice], axis=1)
    first_height, second_height = PARTS
    first = by_chunk(primary_q, 0, first_height)
    place_all = jnp.broadcast_to(new_place.astype(jnp.bfloat16), (device_count, TILE))

    place_all = lax.all_to_all(
        place_all,
        AXES,
        split_axis=0,
        concat_axis=0,
        tiled=True,
    )

    place_all = place_all[:, 0].astype(jnp.int32)
    source = place_all // holding
    dest_side = device_ids % dev_count // half
    source_side = source % dev_count // half
    crossing = source_side != dest_side
    source_row = (source // dev_count % pooled * half + source % half) * holding + place_all % holding
    pool_of = device_ids // dev_count // pooled
    peers = (pool_of[:, None] == pool_of[None, :]) & (dest_side[:, None] == dest_side[None, :])
    ahead = peers & crossing[None, :] & (device_ids[None, :] < device_ids[:, None])
    rank = jnp.sum(ahead, axis=1)
    cross_count = jnp.max(jnp.where(crossing, rank + 1, 0))
    my_side = my_dev // half
    my_pool = my_group // pooled
    leaving = (pool_of == my_pool) & (dest_side != my_side) & crossing
    slots = jnp.arange(POOL)
    leave_rows = jnp.sum(
        jnp.where(leaving[None, :] & (rank[None, :] == slots[:, None]), source_row[None, :], 0), axis=1
    )
    staying = (pool_of == my_pool) & (dest_side == my_side)
    place_in_pool = device_ids // dev_count % pooled * half + device_ids % half
    give_rows = jnp.sum(
        jnp.where(
            staying[None, :] & (place_in_pool[None, :] == slots[:, None]),
            jnp.where(crossing, POOL * holding + rank, source_row)[None, :],
            0,
        ),
        axis=1,
    )

    def spread_over(block):
        block = lax.all_to_all(
            block, AXES, split_axis=0, concat_axis=0, tiled=True, axis_index_groups=pools
        )
        return block.reshape((POOL * holding,) + block.shape[2:])

    first, held, place_all, leave_rows, give_rows, cross_count = lax.optimization_barrier(
        (first, held, place_all, leave_rows, give_rows, cross_count)
    )
    first = spread_over(first)
    held = lax.all_gather(held, AXES, axis=0, tiled=True)
    second = by_chunk(primary_q, POOL * first_height, second_height)
    sent = gather(leave_rows[:COMMON], first)
    common = lax.ppermute(sent, AXES, over)
    second, held, _ = lax.optimization_barrier((second, held, sent))
    second = spread_over(second)

    cells = 2 * CAP
    cell_count = device_count * holding * cells

    def pairs_of(held):
        notices = held[:, width_in:].reshape(device_count, row_count, -1)
        experts_all = notices[:, :, :top_count].astype(jnp.int32)
        replica_all = notices[:, :, top_count : 2 * top_count].astype(jnp.int32)
        return [each.reshape(device_count, pair_count) for each in (experts_all, replica_all)]

    def work(held, place_all, values, scales):
        experts_all, replica_all = pairs_of(held)
        _, _, served, cell = route(experts_all, replica_all, place_all, holding)
        mine = served & (experts_all // holding == my_id)
        cell_ids = jnp.arange(holding * cells)
        hit = mine[:, None, :] & (cell[:, None, :] == cell_ids[None, :, None])
        row_at = device_ids[:, None] * row_count + jnp.sum(
            jnp.where(hit, jnp.arange(pair_count) // top_count, 0), axis=2
        )
        row_at = jnp.where(jnp.any(hit, axis=2), row_at, -1).reshape(cell_count)
        row_hits = row_at[:, None] == jnp.arange(device_count * row_count)[None, :]
        rows = jnp.dot(row_hits.astype(jnp.bfloat16), held, preferred_element_type=jnp.float32)
        return serve(rows.astype(jnp.bfloat16), values, scales)

    activated = work(held, place_all, primary_q, primary_scales)

    columns = dev_count // ROW_CHIPS

    def exchange(blocks, axis, mine, stride, within):
        got = [lax.dynamic_index_in_dim(blocks, mine, axis, keepdims=False)]
        for step in range(1, blocks.shape[axis]):
            pairs = [
                (device, device ^ step * stride) for device in range(device_count)
            ]
            block = lax.dynamic_index_in_dim(blocks, mine ^ step, axis, keepdims=False)
            got.append(lax.ppermute(block, AXES, pairs))
        return jnp.stack(got, axis=within)

    blocks = activated.reshape(group_count, ROW_CHIPS, columns, holding * cells, hidden)
    blocks = exchange(blocks, 1, my_dev // columns, columns, 1)
    common, blocks = lax.optimization_barrier((common, blocks))
    first = cross_over(cross_count, leave_rows, give_rows, first, common, over)
    first, leave_rows, blocks = lax.optimization_barrier((first, leave_rows, blocks))
    sent = gather(leave_rows[:COMMON], second)
    sent, blocks = lax.optimization_barrier((sent, blocks))
    common = lax.ppermute(sent, AXES, over)
    blocks = exchange(blocks, 2, my_dev % columns, 1, 1)
    returned = exchange(blocks, 0, my_group, dev_count, 0)
    common, returned = lax.optimization_barrier((common, returned))
    first = lax.all_to_all(
        first, AXES, split_axis=0, concat_axis=0, tiled=True, axis_index_groups=pools
    )
    second = cross_over(cross_count, leave_rows, give_rows, second, common, over)
    second, held = lax.optimization_barrier((second, held))
    second = lax.all_to_all(
        second, AXES, split_axis=0, concat_axis=0, tiled=True, axis_index_groups=pools
    )
    new_weights = join(None, first, 0, width_in)
    new_weights = join(new_weights, second, first.shape[0] * first.shape[1], width_in)

    experts_all, replica_all = pairs_of(held)
    target, slot_id, served, _ = route(experts_all, replica_all, place_all, holding)
    arriving = served & (target == my_id)
    slot_load = jnp.stack(
        [jnp.sum((arriving & (slot_id == slot)).astype(jnp.int32)) for slot in range(holding + 1)]
    )[None]
    owner_notice = held[:, width_in:].reshape(device_count, row_count, -1)
    owner_notice = lax.dynamic_index_in_dim(
        owner_notice, new_place[0] // holding, 0, keepdims=False
    )
    owner_scales = owner_notice[:, 2 * top_count : 2 * top_count + scale_cols]
    new_scales = lax.dynamic_index_in_dim(
        owner_scales.reshape(primary_scales.shape), new_place[0] % holding, 0
    )

    my_experts = experts.reshape(1, pair_count)
    _, _, my_served, my_cell = route(
        my_experts, replica.reshape(1, pair_count), place_all, holding
    )
    their_id = my_experts // holding
    apart = their_id ^ my_id
    block_at = apart // dev_count * columns + apart % columns
    block_at = block_at * ROW_CHIPS + apart % dev_count // columns
    my_cell = (block_at * (holding * cells) + my_cell)[0]
    placed = (my_cell[:, None] == jnp.arange(cell_count)[None, :]) & my_served[0][:, None]
    selected = jnp.dot(
        placed.astype(jnp.bfloat16),
        returned.reshape(cell_count, hidden),
        preferred_element_type=jnp.float32,
    )
    weight = route_num.reshape(pair_count).astype(jnp.float32) / 16.0
    hidden_out = (selected * weight[:, None]).astype(jnp.bfloat16)
    hidden_out = hidden_out.reshape(row_count, top_count, hidden)
    return (new_weights, new_scales, hidden_out, slot_load)


def solution(mesh):
    in_specs = (
        P(AXES, None, None),
        P(AXES, None, None),
        P(AXES),
        P(AXES, None),
        P(AXES, None),
        P(AXES, None),
        P(AXES, None),
    )
    out_specs = (
        P(AXES, None, None),
        P(AXES, None, None),
        P(AXES, None, None),
        P(AXES, None),
    )
    return jax.shard_map(
        per_device, mesh=mesh, in_specs=in_specs, out_specs=out_specs, check_vma=False
    )
```

```python
import functools

import jax
import jax.numpy as jnp
from jax import lax
from jax.experimental import pallas as pl
from jax.experimental.pallas import tpu as pltpu
from jax.sharding import PartitionSpec as P

TILE = 128
CAP = 2
POOL = 16
ROW_CHIPS = 4
COMMON = 8
VMEM_LIMIT = 60 * 1024 * 1024
AXES = ("group", "dev")
PARTS = (112, 112)


def expert_kernel(x_ref, q_ref, s_ref, o_ref, acc_ref):
    step = pl.program_id(0)

    @pl.when(step == 0)
    def _():
        acc_ref[...] = jnp.zeros_like(acc_ref)

    holding, depth, _ = q_ref.shape
    cells = 2 * CAP
    rows = x_ref.shape[0]
    member_of = lax.broadcasted_iota(jnp.int32, (rows, TILE), 0) // cells % holding
    total = acc_ref[...]
    for member in range(holding):
        for block in range(depth // TILE):
            span = slice(block * TILE, (block + 1) * TILE)
            scale = s_ref[member, 0, block : block + 1, :]
            weights = (q_ref[member, span, :].astype(jnp.float32) * scale).astype(jnp.bfloat16)
            rows_in = jnp.where(member_of == member, x_ref[:, span], jnp.zeros((), jnp.bfloat16))
            total = total + jnp.dot(rows_in, weights, preferred_element_type=jnp.float32)
    acc_ref[...] = total

    @pl.when(step == pl.num_programs(0) - 1)
    def _():
        value = acc_ref[...]
        o_ref[...] = (value / (1.0 + jnp.exp(-value))).astype(jnp.bfloat16)


def serve(rows, values, scales):
    holding, width_in, hidden = values.shape
    depth = 512
    steps = width_in // depth
    count = rows.shape[0]
    wide = jnp.repeat(scales.astype(jnp.float32), TILE, axis=2)
    wide = wide.reshape(holding, steps, depth // TILE, hidden)
    return pl.pallas_call(
        expert_kernel,
        grid=(steps,),
        in_specs=[
            pl.BlockSpec((count, depth), lambda k: (0, k)),
            pl.BlockSpec((holding, depth, hidden), lambda k: (0, k, 0)),
            pl.BlockSpec((holding, 1, depth // TILE, hidden), lambda k: (0, k, 0, 0)),
        ],
        out_specs=pl.BlockSpec((count, hidden), lambda k: (0, 0)),
        out_shape=jax.ShapeDtypeStruct((count, hidden), jnp.bfloat16),
        scratch_shapes=[pltpu.VMEM((count, hidden), jnp.float32)],
        compiler_params=pltpu.CompilerParams(vmem_limit_bytes=VMEM_LIMIT),
        cost_estimate=pl.CostEstimate(
            flops=2 * count * width_in * hidden * holding,
            bytes_accessed=2 * (values.size + count * (width_in + hidden)),
            transcendentals=count * hidden,
        ),
    )(rows, values, wide)


def through_vmem(count, sources, out_at, held, in_sem, out_sem):
    def leave(spot):
        pltpu.make_async_copy(held.at[spot], held.at[spot], in_sem.at[spot]).wait()
        pltpu.make_async_copy(held.at[spot], out_at(spot), out_sem.at[spot]).start()

    def finish(spot):
        pltpu.make_async_copy(held.at[spot], out_at(spot), out_sem.at[spot]).wait()

    for stage in (sources, leave, finish):
        pl.loop(0, count)(stage)


def gather_kernel(index_ref, *refs):
    *source_refs, out_ref, held, in_sem, out_sem = refs

    def start(spot):
        index = index_ref[spot]
        base = 0
        for source_ref in source_refs:
            count = source_ref.shape[0]
            inside = (index >= base) & (index < base + count)
            at = jnp.clip(index - base, 0, count - 1)

            @pl.when(inside)
            def _():
                pltpu.make_async_copy(
                    source_ref.at[at], held.at[spot], in_sem.at[spot]
                ).start()

            base += count

    through_vmem(out_ref.shape[0], start, lambda spot: out_ref.at[spot], held, in_sem, out_sem)


def gather(indices, *sources):
    count = indices.shape[0]
    indices = jnp.clip(indices, 0, sum(source.shape[0] for source in sources) - 1)
    anywhere = pl.BlockSpec(memory_space=pl.ANY)
    out = jax.ShapeDtypeStruct((count,) + sources[0].shape[1:], sources[0].dtype)
    return pl.pallas_call(
        gather_kernel,
        in_specs=[pl.BlockSpec(memory_space=pltpu.SMEM)] + [anywhere] * len(sources),
        out_specs=anywhere,
        out_shape=out,
        scratch_shapes=[
            pltpu.VMEM(out.shape, out.dtype),
            pltpu.SemaphoreType.DMA((count,)),
            pltpu.SemaphoreType.DMA((count,)),
        ],
        compiler_params=pltpu.CompilerParams(vmem_limit_bytes=VMEM_LIMIT),
        cost_estimate=pl.CostEstimate(flops=0, bytes_accessed=4 * out.size, transcendentals=0),
    )(indices, *sources)


def chunk_kernel(first, in_ref, out_ref, held, in_sem, out_sem):
    height = out_ref.shape[2]

    def start(spot):
        pltpu.make_async_copy(
            in_ref.at[:, pl.ds(first + spot * height, height), :], held.at[spot], in_sem.at[spot]
        ).start()

    through_vmem(POOL, start, lambda spot: out_ref.at[spot], held, in_sem, out_sem)


def by_chunk(values, first, height):
    holding, _, hidden = values.shape
    anywhere = pl.BlockSpec(memory_space=pl.ANY)
    out = jax.ShapeDtypeStruct((POOL, holding, height, hidden), values.dtype)
    return pl.pallas_call(
        functools.partial(chunk_kernel, first),
        in_specs=[anywhere],
        out_specs=anywhere,
        out_shape=out,
        scratch_shapes=[
            pltpu.VMEM(out.shape, out.dtype),
            pltpu.SemaphoreType.DMA((POOL,)),
            pltpu.SemaphoreType.DMA((POOL,)),
        ],
        compiler_params=pltpu.CompilerParams(vmem_limit_bytes=VMEM_LIMIT),
        cost_estimate=pl.CostEstimate(
            flops=0, bytes_accessed=4 * out.size, transcendentals=0
        ),
    )(values)


def join_kernel(first, blocks_ref, *refs):
    out_ref, held, in_sem, out_sem = refs[-4:]
    count, height, _ = blocks_ref.shape

    def start(spot):
        pltpu.make_async_copy(blocks_ref.at[spot], held.at[spot], in_sem.at[spot]).start()

    def out_at(spot):
        return out_ref.at[0, pl.ds(first + spot * height, height), :]

    through_vmem(count, start, out_at, held, in_sem, out_sem)


def join(weights, blocks, first, width_in):
    count, _, hidden = blocks.shape
    anywhere = pl.BlockSpec(memory_space=pl.ANY)
    operands = (blocks,) if weights is None else (blocks, weights)
    return pl.pallas_call(
        functools.partial(join_kernel, first),
        in_specs=[anywhere] * len(operands),
        out_specs=anywhere,
        out_shape=jax.ShapeDtypeStruct((1, width_in, hidden), blocks.dtype),
        input_output_aliases={} if weights is None else {1: 0},
        scratch_shapes=[
            pltpu.VMEM(blocks.shape, blocks.dtype),
            pltpu.SemaphoreType.DMA((count,)),
            pltpu.SemaphoreType.DMA((count,)),
        ],
        compiler_params=pltpu.CompilerParams(vmem_limit_bytes=VMEM_LIMIT),
        cost_estimate=pl.CostEstimate(flops=0, bytes_accessed=4 * blocks.size, transcendentals=0),
    )(*operands)


def cross_over(count, leave_rows, give_rows, block, common, pairs):
    def branch_of(size):
        def branch(leave_rows, give_rows, block, common):
            if size == 0:
                return gather(give_rows, block, common)
            late = gather(leave_rows[COMMON : COMMON + size], block)
            return gather(give_rows, block, common, lax.ppermute(late, AXES, pairs))

        return branch

    branches = [branch_of(size) for size in range(POOL - COMMON + 1)]
    size = jnp.maximum(count - COMMON, 0)
    return lax.switch(size, branches, leave_rows, give_rows, block, common)


def route(experts, replica, place_all, holding):
    pair_count = experts.shape[1]
    device_ids = jnp.arange(place_all.shape[0], dtype=jnp.int32)
    matched = experts[:, :, None] == place_all[None, None, :]
    has_copy = jnp.any(matched, axis=2)
    holder = jnp.sum(jnp.where(matched, device_ids[None, None, :], 0), axis=2)
    use_copy = (replica == 1) & has_copy
    target = jnp.where(use_copy, holder, experts // holding)
    slot_id = jnp.where(use_copy, holding, experts % holding)
    pair_order = jnp.arange(pair_count)
    before = pair_order[:, None] < pair_order[None, :]
    position = jnp.sum((target[:, :, None] == target[:, None, :]) & before[None], axis=1)
    cell = experts % holding * (2 * CAP) + use_copy * CAP + position
    return target, slot_id, position < CAP, cell


def per_device(primary_q, primary_scales, new_place, tokens, experts, replica, route_num):
    holding, width_in, hidden = primary_q.shape
    dev_count = lax.axis_size("dev")
    group_count = lax.axis_size("group")
    device_count = dev_count * group_count
    half = dev_count // 2
    pooled = POOL // half
    my_dev = lax.axis_index("dev")
    my_group = lax.axis_index("group")
    first_dev = my_group * dev_count
    pools = [
        [(base + group) * dev_count + side * half + spot for group in range(pooled) for spot in range(half)]
        for base in range(0, group_count, pooled)
        for side in range(2)
    ]
    over = [
        (group * dev_count + spot, group * dev_count + (spot + half) % dev_count)
        for group in range(group_count)
        for spot in range(dev_count)
    ]

    device_ids = jnp.arange(device_count, dtype=jnp.int32)
    my_id = first_dev + my_dev

    row_count, top_count = experts.shape
    pair_count = row_count * top_count
    scale_cols = primary_scales.size // row_count
    notice = jnp.concatenate(
        [
            experts.astype(jnp.bfloat16),
            replica.astype(jnp.bfloat16),
            primary_scales.reshape(row_count, scale_cols),
        ],
        axis=1,
    )
    notice = jnp.pad(notice, ((0, 0), (0, -notice.shape[1] % TILE)))
    held = jnp.concatenate([tokens, notice], axis=1)
    dev_bits = dev_count.bit_length() - 1
    all_bits = device_count.bit_length() - 1
    order = list(range(dev_bits))[::-1] + list(range(dev_bits, all_bits))[::-1]
    apart = device_ids ^ my_id
    spot_of = sum((apart >> bit & 1) << step for step, bit in enumerate(order))

    def double(held, bits):
        for bit in bits:
            pairs = [(device, device ^ 1 << bit) for device in range(device_count)]
            held = jnp.concatenate([held, lax.ppermute(held, AXES, pairs)], axis=0)
        return held

    first_height, second_height = PARTS
    held = double(held, order[:1])
    first, held = lax.optimization_barrier((by_chunk(primary_q, 0, first_height), held))
    held = double(held, order[1:2])
    place_all = jnp.broadcast_to(new_place.astype(jnp.bfloat16), (device_count, TILE))
    place_all, held = lax.optimization_barrier((place_all, held))
    held = double(held, order[2:dev_bits])

    place_all = lax.all_to_all(
        place_all,
        AXES,
        split_axis=0,
        concat_axis=0,
        tiled=True,
    )

    place_all = place_all[:, 0].astype(jnp.int32)
    source = place_all // holding
    dest_side = device_ids % dev_count // half
    source_side = source % dev_count // half
    crossing = source_side != dest_side
    source_row = (source // dev_count % pooled * half + source % half) * holding + place_all % holding
    pool_of = device_ids // dev_count // pooled
    peers = (pool_of[:, None] == pool_of[None, :]) & (dest_side[:, None] == dest_side[None, :])
    ahead = peers & crossing[None, :] & (device_ids[None, :] < device_ids[:, None])
    rank = jnp.sum(ahead, axis=1)
    cross_count = jnp.max(jnp.where(crossing, rank + 1, 0))
    my_side = my_dev // half
    my_pool = my_group // pooled
    leaving = (pool_of == my_pool) & (dest_side != my_side) & crossing
    slots = jnp.arange(POOL)
    leave_rows = jnp.sum(
        jnp.where(leaving[None, :] & (rank[None, :] == slots[:, None]), source_row[None, :], 0), axis=1
    )
    staying = (pool_of == my_pool) & (dest_side == my_side)
    place_in_pool = device_ids // dev_count % pooled * half + device_ids % half
    give_rows = jnp.sum(
        jnp.where(
            staying[None, :] & (place_in_pool[None, :] == slots[:, None]),
            jnp.where(crossing, POOL * holding + rank, source_row)[None, :],
            0,
        ),
        axis=1,
    )

    def spread_over(block):
        block = lax.all_to_all(
            block, AXES, split_axis=0, concat_axis=0, tiled=True, axis_index_groups=pools
        )
        return block.reshape((POOL * holding,) + block.shape[2:])

    first, held, place_all, leave_rows, give_rows, cross_count = lax.optimization_barrier(
        (first, held, place_all, leave_rows, give_rows, cross_count)
    )
    first = spread_over(first)
    second = by_chunk(primary_q, POOL * first_height, second_height)
    held, second = lax.optimization_barrier((held, second))
    held = double(held, order[dev_bits:-1])
    held, second = lax.optimization_barrier((held, second))
    second = spread_over(second)

    cells = 2 * CAP
    cell_count = device_count * holding * cells

    def pairs_of(held):
        notices = held[:, width_in:].reshape(device_count, row_count, -1)[spot_of]
        experts_all = notices[:, :, :top_count].astype(jnp.int32)
        replica_all = notices[:, :, top_count : 2 * top_count].astype(jnp.int32)
        return [each.reshape(device_count, pair_count) for each in (experts_all, replica_all)]

    def work(held, place_all, values, scales):
        experts_all, replica_all = pairs_of(held)
        _, _, served, cell = route(experts_all, replica_all, place_all, holding)
        mine = served & (experts_all // holding == my_id)
        cell_ids = jnp.arange(holding * cells)
        hit = mine[:, None, :] & (cell[:, None, :] == cell_ids[None, :, None])
        row_at = spot_of[:, None] * row_count + jnp.sum(
            jnp.where(hit, jnp.arange(pair_count) // top_count, 0), axis=2
        )
        row_at = jnp.where(jnp.any(hit, axis=2), row_at, -1).reshape(cell_count)
        row_hits = row_at[:, None] == jnp.arange(device_count * row_count)[None, :]
        rows = jnp.dot(row_hits.astype(jnp.bfloat16), held, preferred_element_type=jnp.float32)
        return serve(rows.astype(jnp.bfloat16), values, scales)

    sent = gather(leave_rows[:COMMON], first)
    sent, held = lax.optimization_barrier((sent, held))
    common = lax.ppermute(sent, AXES, over)
    held = double(held, order[-1:])
    activated = work(held, place_all, primary_q, primary_scales)

    columns = dev_count // ROW_CHIPS

    def exchange(blocks, axis, mine, stride, within):
        got = [lax.dynamic_index_in_dim(blocks, mine, axis, keepdims=False)]
        for step in range(1, blocks.shape[axis]):
            pairs = [
                (device, device ^ step * stride) for device in range(device_count)
            ]
            block = lax.dynamic_index_in_dim(blocks, mine ^ step, axis, keepdims=False)
            got.append(lax.ppermute(block, AXES, pairs))
        return jnp.stack(got, axis=within)

    blocks = activated.reshape(group_count, ROW_CHIPS, columns, holding * cells, hidden)
    blocks = exchange(blocks, 1, my_dev // columns, columns, 1)
    common, blocks = lax.optimization_barrier((common, blocks))
    first = cross_over(cross_count, leave_rows, give_rows, first, common, over)
    first, leave_rows, blocks = lax.optimization_barrier((first, leave_rows, blocks))
    sent = gather(leave_rows[:COMMON], second)
    sent, blocks = lax.optimization_barrier((sent, blocks))
    common = lax.ppermute(sent, AXES, over)
    blocks = exchange(blocks, 2, my_dev % columns, 1, 1)
    returned = exchange(blocks, 0, my_group, dev_count, 0)
    common, returned = lax.optimization_barrier((common, returned))
    first = lax.all_to_all(
        first, AXES, split_axis=0, concat_axis=0, tiled=True, axis_index_groups=pools
    )
    second = cross_over(cross_count, leave_rows, give_rows, second, common, over)
    second, held = lax.optimization_barrier((second, held))
    second = lax.all_to_all(
        second, AXES, split_axis=0, concat_axis=0, tiled=True, axis_index_groups=pools
    )
    new_weights = join(None, first, 0, width_in)
    new_weights = join(new_weights, second, first.shape[0] * first.shape[1], width_in)

    experts_all, replica_all = pairs_of(held)
    target, slot_id, served, _ = route(experts_all, replica_all, place_all, holding)
    arriving = served & (target == my_id)
    slot_load = jnp.stack(
        [jnp.sum((arriving & (slot_id == slot)).astype(jnp.int32)) for slot in range(holding + 1)]
    )[None]
    owner_notice = held[:, width_in:].reshape(device_count, row_count, -1)
    owner_notice = lax.dynamic_index_in_dim(
        owner_notice, spot_of[new_place[0] // holding], 0, keepdims=False
    )
    owner_scales = owner_notice[:, 2 * top_count : 2 * top_count + scale_cols]
    new_scales = lax.dynamic_index_in_dim(
        owner_scales.reshape(primary_scales.shape), new_place[0] % holding, 0
    )

    my_experts = experts.reshape(1, pair_count)
    _, _, my_served, my_cell = route(
        my_experts, replica.reshape(1, pair_count), place_all, holding
    )
    their_id = my_experts // holding
    apart = their_id ^ my_id
    block_at = apart // dev_count * columns + apart % columns
    block_at = block_at * ROW_CHIPS + apart % dev_count // columns
    my_cell = (block_at * (holding * cells) + my_cell)[0]
    placed = (my_cell[:, None] == jnp.arange(cell_count)[None, :]) & my_served[0][:, None]
    selected = jnp.dot(
        placed.astype(jnp.bfloat16),
        returned.reshape(cell_count, hidden),
        preferred_element_type=jnp.float32,
    )
    weight = route_num.reshape(pair_count).astype(jnp.float32) / 16.0
    hidden_out = (selected * weight[:, None]).astype(jnp.bfloat16)
    hidden_out = hidden_out.reshape(row_count, top_count, hidden)
    return (new_weights, new_scales, hidden_out, slot_load)


def solution(mesh):
    in_specs = (
        P(AXES, None, None),
        P(AXES, None, None),
        P(AXES),
        P(AXES, None),
        P(AXES, None),
        P(AXES, None),
        P(AXES, None),
    )
    out_specs = (
        P(AXES, None, None),
        P(AXES, None, None),
        P(AXES, None, None),
        P(AXES, None),
    )
    return jax.shard_map(
        per_device, mesh=mesh, in_specs=in_specs, out_specs=out_specs, check_vma=False
    )
```

```python
import functools

import jax
import jax.numpy as jnp
from jax import lax
from jax.experimental import pallas as pl
from jax.experimental.pallas import tpu as pltpu
from jax.sharding import PartitionSpec as P

TILE = 128
CAP = 2
POOL = 16
ROW_CHIPS = 4
COMMON = 8
VMEM_LIMIT = 60 * 1024 * 1024
AXES = ("group", "dev")
PARTS = (112, 112)


def expert_kernel(x_ref, q_ref, s_ref, o_ref, acc_ref):
    step = pl.program_id(0)

    @pl.when(step == 0)
    def _():
        acc_ref[...] = jnp.zeros_like(acc_ref)

    holding, depth, _ = q_ref.shape
    cells = 2 * CAP
    rows = x_ref.shape[0]
    member_of = lax.broadcasted_iota(jnp.int32, (rows, TILE), 0) // cells % holding
    total = acc_ref[...]
    for member in range(holding):
        for block in range(depth // TILE):
            span = slice(block * TILE, (block + 1) * TILE)
            scale = s_ref[member, 0, block : block + 1, :]
            weights = (q_ref[member, span, :].astype(jnp.float32) * scale).astype(jnp.bfloat16)
            rows_in = jnp.where(member_of == member, x_ref[:, span], jnp.zeros((), jnp.bfloat16))
            total = total + jnp.dot(rows_in, weights, preferred_element_type=jnp.float32)
    acc_ref[...] = total

    @pl.when(step == pl.num_programs(0) - 1)
    def _():
        value = acc_ref[...]
        o_ref[...] = (value / (1.0 + jnp.exp(-value))).astype(jnp.bfloat16)


def serve(rows, values, scales):
    holding, width_in, hidden = values.shape
    depth = 512
    steps = width_in // depth
    count = rows.shape[0]
    wide = jnp.repeat(scales.astype(jnp.float32), TILE, axis=2)
    wide = wide.reshape(holding, steps, depth // TILE, hidden)
    return pl.pallas_call(
        expert_kernel,
        grid=(steps,),
        in_specs=[
            pl.BlockSpec((count, depth), lambda k: (0, k)),
            pl.BlockSpec((holding, depth, hidden), lambda k: (0, k, 0)),
            pl.BlockSpec((holding, 1, depth // TILE, hidden), lambda k: (0, k, 0, 0)),
        ],
        out_specs=pl.BlockSpec((count, hidden), lambda k: (0, 0)),
        out_shape=jax.ShapeDtypeStruct((count, hidden), jnp.bfloat16),
        scratch_shapes=[pltpu.VMEM((count, hidden), jnp.float32)],
        compiler_params=pltpu.CompilerParams(vmem_limit_bytes=VMEM_LIMIT),
        cost_estimate=pl.CostEstimate(
            flops=2 * count * width_in * hidden * holding,
            bytes_accessed=2 * (values.size + count * (width_in + hidden)),
            transcendentals=count * hidden,
        ),
    )(rows, values, wide)


def through_vmem(count, sources, out_at, held, in_sem, out_sem):
    def leave(spot):
        pltpu.make_async_copy(held.at[spot], held.at[spot], in_sem.at[spot]).wait()
        pltpu.make_async_copy(held.at[spot], out_at(spot), out_sem.at[spot]).start()

    def finish(spot):
        pltpu.make_async_copy(held.at[spot], out_at(spot), out_sem.at[spot]).wait()

    for stage in (sources, leave, finish):
        pl.loop(0, count)(stage)


def gather_kernel(index_ref, *refs):
    *source_refs, out_ref, held, in_sem, out_sem = refs

    def start(spot):
        index = index_ref[spot]
        base = 0
        for source_ref in source_refs:
            count = source_ref.shape[0]
            inside = (index >= base) & (index < base + count)
            at = jnp.clip(index - base, 0, count - 1)

            @pl.when(inside)
            def _():
                pltpu.make_async_copy(
                    source_ref.at[at], held.at[spot], in_sem.at[spot]
                ).start()

            base += count

    through_vmem(out_ref.shape[0], start, lambda spot: out_ref.at[spot], held, in_sem, out_sem)


def gather(indices, *sources):
    count = indices.shape[0]
    indices = jnp.clip(indices, 0, sum(source.shape[0] for source in sources) - 1)
    anywhere = pl.BlockSpec(memory_space=pl.ANY)
    out = jax.ShapeDtypeStruct((count,) + sources[0].shape[1:], sources[0].dtype)
    return pl.pallas_call(
        gather_kernel,
        in_specs=[pl.BlockSpec(memory_space=pltpu.SMEM)] + [anywhere] * len(sources),
        out_specs=anywhere,
        out_shape=out,
        scratch_shapes=[
            pltpu.VMEM(out.shape, out.dtype),
            pltpu.SemaphoreType.DMA((count,)),
            pltpu.SemaphoreType.DMA((count,)),
        ],
        compiler_params=pltpu.CompilerParams(vmem_limit_bytes=VMEM_LIMIT),
        cost_estimate=pl.CostEstimate(flops=0, bytes_accessed=4 * out.size, transcendentals=0),
    )(indices, *sources)


def chunk_kernel(first, in_ref, out_ref, held, in_sem, out_sem):
    height = out_ref.shape[2]

    def start(spot):
        pltpu.make_async_copy(
            in_ref.at[:, pl.ds(first + spot * height, height), :], held.at[spot], in_sem.at[spot]
        ).start()

    through_vmem(POOL, start, lambda spot: out_ref.at[spot], held, in_sem, out_sem)


def by_chunk(values, first, height):
    holding, _, hidden = values.shape
    anywhere = pl.BlockSpec(memory_space=pl.ANY)
    out = jax.ShapeDtypeStruct((POOL, holding, height, hidden), values.dtype)
    return pl.pallas_call(
        functools.partial(chunk_kernel, first),
        in_specs=[anywhere],
        out_specs=anywhere,
        out_shape=out,
        scratch_shapes=[
            pltpu.VMEM(out.shape, out.dtype),
            pltpu.SemaphoreType.DMA((POOL,)),
            pltpu.SemaphoreType.DMA((POOL,)),
        ],
        compiler_params=pltpu.CompilerParams(vmem_limit_bytes=VMEM_LIMIT),
        cost_estimate=pl.CostEstimate(
            flops=0, bytes_accessed=4 * out.size, transcendentals=0
        ),
    )(values)


def join_kernel(first, blocks_ref, *refs):
    out_ref, held, in_sem, out_sem = refs[-4:]
    count, height, _ = blocks_ref.shape

    def start(spot):
        pltpu.make_async_copy(blocks_ref.at[spot], held.at[spot], in_sem.at[spot]).start()

    def out_at(spot):
        return out_ref.at[0, pl.ds(first + spot * height, height), :]

    through_vmem(count, start, out_at, held, in_sem, out_sem)


def join(weights, blocks, first, width_in):
    count, _, hidden = blocks.shape
    anywhere = pl.BlockSpec(memory_space=pl.ANY)
    operands = (blocks,) if weights is None else (blocks, weights)
    return pl.pallas_call(
        functools.partial(join_kernel, first),
        in_specs=[anywhere] * len(operands),
        out_specs=anywhere,
        out_shape=jax.ShapeDtypeStruct((1, width_in, hidden), blocks.dtype),
        input_output_aliases={} if weights is None else {1: 0},
        scratch_shapes=[
            pltpu.VMEM(blocks.shape, blocks.dtype),
            pltpu.SemaphoreType.DMA((count,)),
            pltpu.SemaphoreType.DMA((count,)),
        ],
        compiler_params=pltpu.CompilerParams(vmem_limit_bytes=VMEM_LIMIT),
        cost_estimate=pl.CostEstimate(flops=0, bytes_accessed=4 * blocks.size, transcendentals=0),
    )(*operands)


def late_over(count, leave_rows, block, pairs):
    most = POOL - COMMON

    def branch_of(size):
        def branch(leave_rows, block):
            if size == 0:
                return jnp.zeros((most,) + block.shape[1:], block.dtype)
            late = gather(leave_rows[COMMON : COMMON + size], block)
            got = lax.ppermute(late, AXES, pairs)
            return jnp.pad(got, ((0, most - size), (0, 0), (0, 0)))

        return branch

    branches = [branch_of(size) for size in range(most + 1)]
    return lax.switch(jnp.maximum(count - COMMON, 0), branches, leave_rows, block)


def route(experts, replica, place_all, holding):
    pair_count = experts.shape[1]
    device_ids = jnp.arange(place_all.shape[0], dtype=jnp.int32)
    matched = experts[:, :, None] == place_all[None, None, :]
    has_copy = jnp.any(matched, axis=2)
    holder = jnp.sum(jnp.where(matched, device_ids[None, None, :], 0), axis=2)
    use_copy = (replica == 1) & has_copy
    target = jnp.where(use_copy, holder, experts // holding)
    slot_id = jnp.where(use_copy, holding, experts % holding)
    pair_order = jnp.arange(pair_count)
    before = pair_order[:, None] < pair_order[None, :]
    position = jnp.sum((target[:, :, None] == target[:, None, :]) & before[None], axis=1)
    cell = experts % holding * (2 * CAP) + use_copy * CAP + position
    return target, slot_id, position < CAP, cell


def per_device(primary_q, primary_scales, new_place, tokens, experts, replica, route_num):
    holding, width_in, hidden = primary_q.shape
    dev_count = lax.axis_size("dev")
    group_count = lax.axis_size("group")
    device_count = dev_count * group_count
    half = dev_count // 2
    pooled = POOL // half
    my_dev = lax.axis_index("dev")
    my_group = lax.axis_index("group")
    first_dev = my_group * dev_count
    pools = [
        [(base + group) * dev_count + side * half + spot for group in range(pooled) for spot in range(half)]
        for base in range(0, group_count, pooled)
        for side in range(2)
    ]
    over = [
        (group * dev_count + spot, group * dev_count + (spot + half) % dev_count)
        for group in range(group_count)
        for spot in range(dev_count)
    ]

    device_ids = jnp.arange(device_count, dtype=jnp.int32)
    my_id = first_dev + my_dev

    row_count, top_count = experts.shape
    pair_count = row_count * top_count
    scale_cols = primary_scales.size // row_count
    notice = jnp.concatenate(
        [
            experts.astype(jnp.bfloat16),
            replica.astype(jnp.bfloat16),
            primary_scales.reshape(row_count, scale_cols),
        ],
        axis=1,
    )
    notice = jnp.pad(notice, ((0, 0), (0, -notice.shape[1] % TILE)))
    held = jnp.concatenate([tokens, notice], axis=1)
    dev_bits = dev_count.bit_length() - 1
    all_bits = device_count.bit_length() - 1
    order = list(range(dev_bits))[::-1] + list(range(dev_bits, all_bits))[::-1]
    apart = device_ids ^ my_id
    spot_of = sum((apart >> bit & 1) << step for step, bit in enumerate(order))

    def double(held, bits):
        for bit in bits:
            pairs = [(device, device ^ 1 << bit) for device in range(device_count)]
            held = jnp.concatenate([held, lax.ppermute(held, AXES, pairs)], axis=0)
        return held

    first_height, second_height = PARTS
    held = double(held, order[:1])
    first, held = lax.optimization_barrier((by_chunk(primary_q, 0, first_height), held))
    held = double(held, order[1:2])
    place_all = jnp.broadcast_to(new_place.astype(jnp.bfloat16), (device_count, TILE))
    place_all, held = lax.optimization_barrier((place_all, held))
    held = double(held, order[2:dev_bits])

    place_all = lax.all_to_all(
        place_all,
        AXES,
        split_axis=0,
        concat_axis=0,
        tiled=True,
    )

    place_all = place_all[:, 0].astype(jnp.int32)
    source = place_all // holding
    dest_side = device_ids % dev_count // half
    source_side = source % dev_count // half
    crossing = source_side != dest_side
    source_row = (source // dev_count % pooled * half + source % half) * holding + place_all % holding
    pool_of = device_ids // dev_count // pooled
    peers = (pool_of[:, None] == pool_of[None, :]) & (dest_side[:, None] == dest_side[None, :])
    ahead = peers & crossing[None, :] & (device_ids[None, :] < device_ids[:, None])
    rank = jnp.sum(ahead, axis=1)
    cross_count = jnp.max(jnp.where(crossing, rank + 1, 0))
    my_side = my_dev // half
    my_pool = my_group // pooled
    leaving = (pool_of == my_pool) & (dest_side != my_side) & crossing
    slots = jnp.arange(POOL)
    leave_rows = jnp.sum(
        jnp.where(leaving[None, :] & (rank[None, :] == slots[:, None]), source_row[None, :], 0), axis=1
    )
    staying = (pool_of == my_pool) & (dest_side == my_side)
    place_in_pool = device_ids // dev_count % pooled * half + device_ids % half
    give_rows = jnp.sum(
        jnp.where(
            staying[None, :] & (place_in_pool[None, :] == slots[:, None]),
            jnp.where(crossing, POOL * holding + rank, source_row)[None, :],
            0,
        ),
        axis=1,
    )

    def spread_over(block):
        block = lax.all_to_all(
            block, AXES, split_axis=0, concat_axis=0, tiled=True, axis_index_groups=pools
        )
        return block.reshape((POOL * holding,) + block.shape[2:])

    first, held, place_all, leave_rows, give_rows, cross_count = lax.optimization_barrier(
        (first, held, place_all, leave_rows, give_rows, cross_count)
    )
    first = spread_over(first)
    second = by_chunk(primary_q, POOL * first_height, second_height)
    held, second = lax.optimization_barrier((held, second))
    held = double(held, order[dev_bits:-1])
    held, second = lax.optimization_barrier((held, second))
    second = spread_over(second)

    cells = 2 * CAP
    cell_count = device_count * holding * cells

    def pairs_of(held):
        notices = held[:, width_in:].reshape(device_count, row_count, -1)[spot_of]
        experts_all = notices[:, :, :top_count].astype(jnp.int32)
        replica_all = notices[:, :, top_count : 2 * top_count].astype(jnp.int32)
        return [each.reshape(device_count, pair_count) for each in (experts_all, replica_all)]

    def work(held, place_all, values, scales):
        experts_all, replica_all = pairs_of(held)
        _, _, served, cell = route(experts_all, replica_all, place_all, holding)
        mine = served & (experts_all // holding == my_id)
        cell_ids = jnp.arange(holding * cells)
        hit = mine[:, None, :] & (cell[:, None, :] == cell_ids[None, :, None])
        row_at = spot_of[:, None] * row_count + jnp.sum(
            jnp.where(hit, jnp.arange(pair_count) // top_count, 0), axis=2
        )
        row_at = jnp.where(jnp.any(hit, axis=2), row_at, -1).reshape(cell_count)
        row_hits = row_at[:, None] == jnp.arange(device_count * row_count)[None, :]
        rows = jnp.dot(row_hits.astype(jnp.bfloat16), held, preferred_element_type=jnp.float32)
        return serve(rows.astype(jnp.bfloat16), values, scales)

    sent = gather(leave_rows[:COMMON], first)
    sent, held = lax.optimization_barrier((sent, held))
    common = lax.ppermute(sent, AXES, over)
    held = double(held, order[-1:])
    activated = work(held, place_all, primary_q, primary_scales)

    columns = dev_count // ROW_CHIPS

    def exchange(blocks, axis, mine, stride, within):
        got = [lax.dynamic_index_in_dim(blocks, mine, axis, keepdims=False)]
        for step in range(1, blocks.shape[axis]):
            pairs = [
                (device, device ^ step * stride) for device in range(device_count)
            ]
            block = lax.dynamic_index_in_dim(blocks, mine ^ step, axis, keepdims=False)
            got.append(lax.ppermute(block, AXES, pairs))
        return jnp.stack(got, axis=within)

    blocks = activated.reshape(group_count, ROW_CHIPS, columns, holding * cells, hidden)
    blocks = exchange(blocks, 1, my_dev // columns, columns, 1)
    leave_rows, blocks = lax.optimization_barrier((leave_rows, blocks))
    late = late_over(cross_count, leave_rows, first, over)
    first = gather(give_rows, first, common, late)
    first, leave_rows, blocks = lax.optimization_barrier((first, leave_rows, blocks))
    sent = gather(leave_rows[:COMMON], second)
    sent, blocks = lax.optimization_barrier((sent, blocks))
    common = lax.ppermute(sent, AXES, over)
    blocks = exchange(blocks, 2, my_dev % columns, 1, 1)
    returned = exchange(blocks, 0, my_group, dev_count, 0)
    leave_rows, returned = lax.optimization_barrier((leave_rows, returned))
    first = lax.all_to_all(
        first, AXES, split_axis=0, concat_axis=0, tiled=True, axis_index_groups=pools
    )
    late = late_over(cross_count, leave_rows, second, over)
    second = gather(give_rows, second, common, late)
    second, held = lax.optimization_barrier((second, held))
    second = lax.all_to_all(
        second, AXES, split_axis=0, concat_axis=0, tiled=True, axis_index_groups=pools
    )
    new_weights = join(None, first, 0, width_in)
    new_weights = join(new_weights, second, first.shape[0] * first.shape[1], width_in)

    experts_all, replica_all = pairs_of(held)
    target, slot_id, served, _ = route(experts_all, replica_all, place_all, holding)
    arriving = served & (target == my_id)
    slot_load = jnp.stack(
        [jnp.sum((arriving & (slot_id == slot)).astype(jnp.int32)) for slot in range(holding + 1)]
    )[None]
    owner_notice = held[:, width_in:].reshape(device_count, row_count, -1)
    owner_notice = lax.dynamic_index_in_dim(
        owner_notice, spot_of[new_place[0] // holding], 0, keepdims=False
    )
    owner_scales = owner_notice[:, 2 * top_count : 2 * top_count + scale_cols]
    new_scales = lax.dynamic_index_in_dim(
        owner_scales.reshape(primary_scales.shape), new_place[0] % holding, 0
    )

    my_experts = experts.reshape(1, pair_count)
    _, _, my_served, my_cell = route(
        my_experts, replica.reshape(1, pair_count), place_all, holding
    )
    their_id = my_experts // holding
    apart = their_id ^ my_id
    block_at = apart // dev_count * columns + apart % columns
    block_at = block_at * ROW_CHIPS + apart % dev_count // columns
    my_cell = (block_at * (holding * cells) + my_cell)[0]
    placed = (my_cell[:, None] == jnp.arange(cell_count)[None, :]) & my_served[0][:, None]
    selected = jnp.dot(
        placed.astype(jnp.bfloat16),
        returned.reshape(cell_count, hidden),
        preferred_element_type=jnp.float32,
    )
    weight = route_num.reshape(pair_count).astype(jnp.float32) / 16.0
    hidden_out = (selected * weight[:, None]).astype(jnp.bfloat16)
    hidden_out = hidden_out.reshape(row_count, top_count, hidden)
    return (new_weights, new_scales, hidden_out, slot_load)


def solution(mesh):
    in_specs = (
        P(AXES, None, None),
        P(AXES, None, None),
        P(AXES),
        P(AXES, None),
        P(AXES, None),
        P(AXES, None),
        P(AXES, None),
    )
    out_specs = (
        P(AXES, None, None),
        P(AXES, None, None),
        P(AXES, None, None),
        P(AXES, None),
    )
    return jax.shard_map(
        per_device, mesh=mesh, in_specs=in_specs, out_specs=out_specs, check_vma=False
    )
```

```python
import functools

import jax
import jax.numpy as jnp
from jax import lax
from jax.experimental import pallas as pl
from jax.experimental.pallas import tpu as pltpu
from jax.sharding import PartitionSpec as P

TILE = 128
CAP = 2
POOL = 16
ROW_CHIPS = 4
COMMON = 8
VMEM_LIMIT = 60 * 1024 * 1024
AXES = ("group", "dev")
PARTS = (112, 112)


def expert_kernel(x_ref, q_ref, s_ref, o_ref, acc_ref):
    step = pl.program_id(0)

    @pl.when(step == 0)
    def _():
        acc_ref[...] = jnp.zeros_like(acc_ref)

    holding, depth, _ = q_ref.shape
    cells = 2 * CAP
    rows = x_ref.shape[0]
    member_of = lax.broadcasted_iota(jnp.int32, (rows, TILE), 0) // cells % holding
    total = acc_ref[...]
    for member in range(holding):
        for block in range(depth // TILE):
            span = slice(block * TILE, (block + 1) * TILE)
            scale = s_ref[member, 0, block : block + 1, :]
            weights = (q_ref[member, span, :].astype(jnp.float32) * scale).astype(jnp.bfloat16)
            rows_in = jnp.where(member_of == member, x_ref[:, span], jnp.zeros((), jnp.bfloat16))
            total = total + jnp.dot(rows_in, weights, preferred_element_type=jnp.float32)
    acc_ref[...] = total

    @pl.when(step == pl.num_programs(0) - 1)
    def _():
        value = acc_ref[...]
        o_ref[...] = (value / (1.0 + jnp.exp(-value))).astype(jnp.bfloat16)


def serve(rows, values, scales):
    holding, width_in, hidden = values.shape
    depth = 512
    steps = width_in // depth
    count = rows.shape[0]
    wide = jnp.repeat(scales.astype(jnp.float32), TILE, axis=2)
    wide = wide.reshape(holding, steps, depth // TILE, hidden)
    return pl.pallas_call(
        expert_kernel,
        grid=(steps,),
        in_specs=[
            pl.BlockSpec((count, depth), lambda k: (0, k)),
            pl.BlockSpec((holding, depth, hidden), lambda k: (0, k, 0)),
            pl.BlockSpec((holding, 1, depth // TILE, hidden), lambda k: (0, k, 0, 0)),
        ],
        out_specs=pl.BlockSpec((count, hidden), lambda k: (0, 0)),
        out_shape=jax.ShapeDtypeStruct((count, hidden), jnp.bfloat16),
        scratch_shapes=[pltpu.VMEM((count, hidden), jnp.float32)],
        compiler_params=pltpu.CompilerParams(vmem_limit_bytes=VMEM_LIMIT),
        cost_estimate=pl.CostEstimate(
            flops=2 * count * width_in * hidden * holding,
            bytes_accessed=2 * (values.size + count * (width_in + hidden)),
            transcendentals=count * hidden,
        ),
    )(rows, values, wide)


def through_vmem(count, sources, out_at, held, in_sem, out_sem):
    def leave(spot):
        pltpu.make_async_copy(held.at[spot], held.at[spot], in_sem.at[spot]).wait()
        pltpu.make_async_copy(held.at[spot], out_at(spot), out_sem.at[spot]).start()

    def finish(spot):
        pltpu.make_async_copy(held.at[spot], out_at(spot), out_sem.at[spot]).wait()

    for stage in (sources, leave, finish):
        pl.loop(0, count)(stage)


def gather_kernel(index_ref, *refs):
    *source_refs, out_ref, held, in_sem, out_sem = refs

    def start(spot):
        index = index_ref[spot]
        base = 0
        for source_ref in source_refs:
            count = source_ref.shape[0]
            inside = (index >= base) & (index < base + count)
            at = jnp.clip(index - base, 0, count - 1)

            @pl.when(inside)
            def _():
                pltpu.make_async_copy(
                    source_ref.at[at], held.at[spot], in_sem.at[spot]
                ).start()

            base += count

    through_vmem(out_ref.shape[0], start, lambda spot: out_ref.at[spot], held, in_sem, out_sem)


def gather(indices, *sources):
    count = indices.shape[0]
    indices = jnp.clip(indices, 0, sum(source.shape[0] for source in sources) - 1)
    anywhere = pl.BlockSpec(memory_space=pl.ANY)
    out = jax.ShapeDtypeStruct((count,) + sources[0].shape[1:], sources[0].dtype)
    return pl.pallas_call(
        gather_kernel,
        in_specs=[pl.BlockSpec(memory_space=pltpu.SMEM)] + [anywhere] * len(sources),
        out_specs=anywhere,
        out_shape=out,
        scratch_shapes=[
            pltpu.VMEM(out.shape, out.dtype),
            pltpu.SemaphoreType.DMA((count,)),
            pltpu.SemaphoreType.DMA((count,)),
        ],
        compiler_params=pltpu.CompilerParams(vmem_limit_bytes=VMEM_LIMIT),
        cost_estimate=pl.CostEstimate(flops=0, bytes_accessed=4 * out.size, transcendentals=0),
    )(indices, *sources)


def chunk_kernel(first, in_ref, out_ref, held, in_sem, out_sem):
    height = out_ref.shape[2]

    def start(spot):
        pltpu.make_async_copy(
            in_ref.at[:, pl.ds(first + spot * height, height), :], held.at[spot], in_sem.at[spot]
        ).start()

    through_vmem(POOL, start, lambda spot: out_ref.at[spot], held, in_sem, out_sem)


def by_chunk(values, first, height):
    holding, _, hidden = values.shape
    anywhere = pl.BlockSpec(memory_space=pl.ANY)
    out = jax.ShapeDtypeStruct((POOL, holding, height, hidden), values.dtype)
    return pl.pallas_call(
        functools.partial(chunk_kernel, first),
        in_specs=[anywhere],
        out_specs=anywhere,
        out_shape=out,
        scratch_shapes=[
            pltpu.VMEM(out.shape, out.dtype),
            pltpu.SemaphoreType.DMA((POOL,)),
            pltpu.SemaphoreType.DMA((POOL,)),
        ],
        compiler_params=pltpu.CompilerParams(vmem_limit_bytes=VMEM_LIMIT),
        cost_estimate=pl.CostEstimate(
            flops=0, bytes_accessed=4 * out.size, transcendentals=0
        ),
    )(values)


def join_kernel(first, blocks_ref, *refs):
    out_ref, held, in_sem, out_sem = refs[-4:]
    count, height, _ = blocks_ref.shape

    def start(spot):
        pltpu.make_async_copy(blocks_ref.at[spot], held.at[spot], in_sem.at[spot]).start()

    def out_at(spot):
        return out_ref.at[0, pl.ds(first + spot * height, height), :]

    through_vmem(count, start, out_at, held, in_sem, out_sem)


def join(weights, blocks, first, width_in):
    count, _, hidden = blocks.shape
    anywhere = pl.BlockSpec(memory_space=pl.ANY)
    operands = (blocks,) if weights is None else (blocks, weights)
    return pl.pallas_call(
        functools.partial(join_kernel, first),
        in_specs=[anywhere] * len(operands),
        out_specs=anywhere,
        out_shape=jax.ShapeDtypeStruct((1, width_in, hidden), blocks.dtype),
        input_output_aliases={} if weights is None else {1: 0},
        scratch_shapes=[
            pltpu.VMEM(blocks.shape, blocks.dtype),
            pltpu.SemaphoreType.DMA((count,)),
            pltpu.SemaphoreType.DMA((count,)),
        ],
        compiler_params=pltpu.CompilerParams(vmem_limit_bytes=VMEM_LIMIT),
        cost_estimate=pl.CostEstimate(flops=0, bytes_accessed=4 * blocks.size, transcendentals=0),
    )(*operands)


def late_over(count, leave_rows, block, pairs):
    most = POOL - COMMON

    def branch_of(size):
        def branch(leave_rows, block):
            if size == 0:
                return jnp.zeros((most,) + block.shape[1:], block.dtype)
            late = gather(leave_rows[COMMON : COMMON + size], block)
            got = lax.ppermute(late, AXES, pairs)
            return jnp.pad(got, ((0, most - size), (0, 0), (0, 0)))

        return branch

    branches = [branch_of(size) for size in range(most + 1)]
    return lax.switch(jnp.maximum(count - COMMON, 0), branches, leave_rows, block)


def route(experts, replica, place_all, holding):
    pair_count = experts.shape[1]
    device_ids = jnp.arange(place_all.shape[0], dtype=jnp.int32)
    matched = experts[:, :, None] == place_all[None, None, :]
    has_copy = jnp.any(matched, axis=2)
    holder = jnp.sum(jnp.where(matched, device_ids[None, None, :], 0), axis=2)
    use_copy = (replica == 1) & has_copy
    target = jnp.where(use_copy, holder, experts // holding)
    slot_id = jnp.where(use_copy, holding, experts % holding)
    pair_order = jnp.arange(pair_count)
    before = pair_order[:, None] < pair_order[None, :]
    position = jnp.sum((target[:, :, None] == target[:, None, :]) & before[None], axis=1)
    cell = experts % holding * (2 * CAP) + use_copy * CAP + position
    return target, slot_id, position < CAP, cell


def per_device(primary_q, primary_scales, new_place, tokens, experts, replica, route_num):
    holding, width_in, hidden = primary_q.shape
    dev_count = lax.axis_size("dev")
    group_count = lax.axis_size("group")
    device_count = dev_count * group_count
    half = dev_count // 2
    pooled = POOL // half
    my_dev = lax.axis_index("dev")
    my_group = lax.axis_index("group")
    first_dev = my_group * dev_count
    pools = [
        [(base + group) * dev_count + side * half + spot for group in range(pooled) for spot in range(half)]
        for base in range(0, group_count, pooled)
        for side in range(2)
    ]
    over = [
        (group * dev_count + spot, group * dev_count + (spot + half) % dev_count)
        for group in range(group_count)
        for spot in range(dev_count)
    ]

    device_ids = jnp.arange(device_count, dtype=jnp.int32)
    my_id = first_dev + my_dev

    row_count, top_count = experts.shape
    pair_count = row_count * top_count
    scale_cols = primary_scales.size // row_count
    notice = jnp.concatenate(
        [
            experts.astype(jnp.bfloat16),
            replica.astype(jnp.bfloat16),
            primary_scales.reshape(row_count, scale_cols),
        ],
        axis=1,
    )
    notice = jnp.pad(notice, ((0, 0), (0, -notice.shape[1] % TILE)))
    held = jnp.concatenate([tokens, notice], axis=1)
    dev_bits = dev_count.bit_length() - 1
    all_bits = device_count.bit_length() - 1
    order = list(range(dev_bits))[::-1] + list(range(dev_bits, all_bits))[::-1]
    apart = device_ids ^ my_id
    spot_of = sum((apart >> bit & 1) << step for step, bit in enumerate(order))

    def double(held, bits):
        for bit in bits:
            pairs = [(device, device ^ 1 << bit) for device in range(device_count)]
            held = jnp.concatenate([held, lax.ppermute(held, AXES, pairs)], axis=0)
        return held

    first_height, second_height = PARTS
    held = double(held, order[:1])
    first, held = lax.optimization_barrier((by_chunk(primary_q, 0, first_height), held))
    held = double(held, order[1:2])
    place_all = jnp.broadcast_to(new_place.astype(jnp.bfloat16), (device_count, TILE))
    place_all, held = lax.optimization_barrier((place_all, held))
    held = double(held, order[2:dev_bits])

    place_all = lax.all_to_all(
        place_all,
        AXES,
        split_axis=0,
        concat_axis=0,
        tiled=True,
    )

    place_all = place_all[:, 0].astype(jnp.int32)
    source = place_all // holding
    dest_side = device_ids % dev_count // half
    source_side = source % dev_count // half
    crossing = source_side != dest_side
    source_row = (source // dev_count % pooled * half + source % half) * holding + place_all % holding
    pool_of = device_ids // dev_count // pooled
    peers = (pool_of[:, None] == pool_of[None, :]) & (dest_side[:, None] == dest_side[None, :])
    ahead = peers & crossing[None, :] & (device_ids[None, :] < device_ids[:, None])
    rank = jnp.sum(ahead, axis=1)
    cross_count = jnp.max(jnp.where(crossing, rank + 1, 0))
    my_side = my_dev // half
    my_pool = my_group // pooled
    leaving = (pool_of == my_pool) & (dest_side != my_side) & crossing
    slots = jnp.arange(POOL)
    leave_rows = jnp.sum(
        jnp.where(leaving[None, :] & (rank[None, :] == slots[:, None]), source_row[None, :], 0), axis=1
    )
    staying = (pool_of == my_pool) & (dest_side == my_side)
    place_in_pool = device_ids // dev_count % pooled * half + device_ids % half
    give_rows = jnp.sum(
        jnp.where(
            staying[None, :] & (place_in_pool[None, :] == slots[:, None]),
            jnp.where(crossing, POOL * holding + rank, source_row)[None, :],
            0,
        ),
        axis=1,
    )

    def spread_over(block):
        block = lax.all_to_all(
            block, AXES, split_axis=0, concat_axis=0, tiled=True, axis_index_groups=pools
        )
        return block.reshape((POOL * holding,) + block.shape[2:])

    first, held, place_all, leave_rows, give_rows, cross_count = lax.optimization_barrier(
        (first, held, place_all, leave_rows, give_rows, cross_count)
    )
    first = spread_over(first)
    second = by_chunk(primary_q, POOL * first_height, second_height)
    held, second = lax.optimization_barrier((held, second))
    held = double(held, order[dev_bits:-1])
    held, second = lax.optimization_barrier((held, second))
    second = spread_over(second)

    cells = 2 * CAP
    cell_count = device_count * holding * cells

    def pairs_of(held):
        notices = held[:, width_in:].reshape(device_count, row_count, -1)[spot_of]
        experts_all = notices[:, :, :top_count].astype(jnp.int32)
        replica_all = notices[:, :, top_count : 2 * top_count].astype(jnp.int32)
        return [each.reshape(device_count, pair_count) for each in (experts_all, replica_all)]

    def work(held, place_all, values, scales):
        experts_all, replica_all = pairs_of(held)
        _, _, served, cell = route(experts_all, replica_all, place_all, holding)
        mine = served & (experts_all // holding == my_id)
        cell_ids = jnp.arange(holding * cells)
        hit = mine[:, None, :] & (cell[:, None, :] == cell_ids[None, :, None])
        row_at = spot_of[:, None] * row_count + jnp.sum(
            jnp.where(hit, jnp.arange(pair_count) // top_count, 0), axis=2
        )
        row_at = jnp.where(jnp.any(hit, axis=2), row_at, -1).reshape(cell_count)
        row_hits = row_at[:, None] == jnp.arange(device_count * row_count)[None, :]
        rows = jnp.dot(row_hits.astype(jnp.bfloat16), held, preferred_element_type=jnp.float32)
        return serve(rows.astype(jnp.bfloat16), values, scales)

    sent = gather(leave_rows[:COMMON], first)
    sent, held = lax.optimization_barrier((sent, held))
    common = lax.ppermute(sent, AXES, over)
    held = double(held, order[-1:])
    activated = work(held, place_all, primary_q, primary_scales)
    leave_rows, activated = lax.optimization_barrier((leave_rows, activated))

    columns = dev_count // ROW_CHIPS

    def exchange(blocks, axis, mine, stride, within):
        got = [lax.dynamic_index_in_dim(blocks, mine, axis, keepdims=False)]
        for step in range(1, blocks.shape[axis]):
            pairs = [
                (device, device ^ step * stride) for device in range(device_count)
            ]
            block = lax.dynamic_index_in_dim(blocks, mine ^ step, axis, keepdims=False)
            got.append(lax.ppermute(block, AXES, pairs))
        return jnp.stack(got, axis=within)

    blocks = activated.reshape(group_count, ROW_CHIPS, columns, holding * cells, hidden)
    blocks = exchange(blocks, 1, my_dev // columns, columns, 1)
    late = late_over(cross_count, leave_rows, first, over)
    leave_rows, late = lax.optimization_barrier((leave_rows, late))
    sent = gather(leave_rows[:COMMON], second)
    sent, blocks = lax.optimization_barrier((sent, blocks))
    give_rows, _ = lax.optimization_barrier((give_rows, sent))
    first = gather(give_rows, first, common, late)
    common = lax.ppermute(sent, AXES, over)
    blocks = exchange(blocks, 2, my_dev % columns, 1, 1)
    returned = exchange(blocks, 0, my_group, dev_count, 0)
    leave_rows, returned = lax.optimization_barrier((leave_rows, returned))
    first = lax.all_to_all(
        first, AXES, split_axis=0, concat_axis=0, tiled=True, axis_index_groups=pools
    )
    late = late_over(cross_count, leave_rows, second, over)
    second = gather(give_rows, second, common, late)
    second, held = lax.optimization_barrier((second, held))
    second = lax.all_to_all(
        second, AXES, split_axis=0, concat_axis=0, tiled=True, axis_index_groups=pools
    )
    new_weights = join(None, first, 0, width_in)
    new_weights = join(new_weights, second, first.shape[0] * first.shape[1], width_in)

    experts_all, replica_all = pairs_of(held)
    target, slot_id, served, _ = route(experts_all, replica_all, place_all, holding)
    arriving = served & (target == my_id)
    slot_load = jnp.stack(
        [jnp.sum((arriving & (slot_id == slot)).astype(jnp.int32)) for slot in range(holding + 1)]
    )[None]
    owner_notice = held[:, width_in:].reshape(device_count, row_count, -1)
    owner_notice = lax.dynamic_index_in_dim(
        owner_notice, spot_of[new_place[0] // holding], 0, keepdims=False
    )
    owner_scales = owner_notice[:, 2 * top_count : 2 * top_count + scale_cols]
    new_scales = lax.dynamic_index_in_dim(
        owner_scales.reshape(primary_scales.shape), new_place[0] % holding, 0
    )

    my_experts = experts.reshape(1, pair_count)
    _, _, my_served, my_cell = route(
        my_experts, replica.reshape(1, pair_count), place_all, holding
    )
    their_id = my_experts // holding
    apart = their_id ^ my_id
    block_at = apart // dev_count * columns + apart % columns
    block_at = block_at * ROW_CHIPS + apart % dev_count // columns
    my_cell = (block_at * (holding * cells) + my_cell)[0]
    placed = (my_cell[:, None] == jnp.arange(cell_count)[None, :]) & my_served[0][:, None]
    selected = jnp.dot(
        placed.astype(jnp.bfloat16),
        returned.reshape(cell_count, hidden),
        preferred_element_type=jnp.float32,
    )
    weight = route_num.reshape(pair_count).astype(jnp.float32) / 16.0
    hidden_out = (selected * weight[:, None]).astype(jnp.bfloat16)
    hidden_out = hidden_out.reshape(row_count, top_count, hidden)
    return (new_weights, new_scales, hidden_out, slot_load)


def solution(mesh):
    in_specs = (
        P(AXES, None, None),
        P(AXES, None, None),
        P(AXES),
        P(AXES, None),
        P(AXES, None),
        P(AXES, None),
        P(AXES, None),
    )
    out_specs = (
        P(AXES, None, None),
        P(AXES, None, None),
        P(AXES, None, None),
        P(AXES, None),
    )
    return jax.shard_map(
        per_device, mesh=mesh, in_specs=in_specs, out_specs=out_specs, check_vma=False
    )
```

```python
import functools

import jax
import jax.numpy as jnp
from jax import lax
from jax.experimental import pallas as pl
from jax.experimental.pallas import tpu as pltpu
from jax.sharding import PartitionSpec as P

TILE = 128
CAP = 2
POOL = 16
ROW_CHIPS = 4
COMMON = 8
VMEM_LIMIT = 60 * 1024 * 1024
AXES = ("group", "dev")
PARTS = (112, 112)


def expert_kernel(x_ref, q_ref, s_ref, o_ref, acc_ref):
    step = pl.program_id(0)

    @pl.when(step == 0)
    def _():
        acc_ref[...] = jnp.zeros_like(acc_ref)

    holding, depth, _ = q_ref.shape
    cells = 2 * CAP
    rows = x_ref.shape[0]
    member_of = lax.broadcasted_iota(jnp.int32, (rows, TILE), 0) // cells % holding
    total = acc_ref[...]
    for member in range(holding):
        for block in range(depth // TILE):
            span = slice(block * TILE, (block + 1) * TILE)
            scale = s_ref[member, 0, block : block + 1, :]
            weights = (q_ref[member, span, :].astype(jnp.float32) * scale).astype(jnp.bfloat16)
            rows_in = jnp.where(member_of == member, x_ref[:, span], jnp.zeros((), jnp.bfloat16))
            total = total + jnp.dot(rows_in, weights, preferred_element_type=jnp.float32)
    acc_ref[...] = total

    @pl.when(step == pl.num_programs(0) - 1)
    def _():
        value = acc_ref[...]
        o_ref[...] = (value / (1.0 + jnp.exp(-value))).astype(jnp.bfloat16)


def serve(rows, values, scales):
    holding, width_in, hidden = values.shape
    depth = 512
    steps = width_in // depth
    count = rows.shape[0]
    wide = jnp.repeat(scales.astype(jnp.float32), TILE, axis=2)
    wide = wide.reshape(holding, steps, depth // TILE, hidden)
    return pl.pallas_call(
        expert_kernel,
        grid=(steps,),
        in_specs=[
            pl.BlockSpec((count, depth), lambda k: (0, k)),
            pl.BlockSpec((holding, depth, hidden), lambda k: (0, k, 0)),
            pl.BlockSpec((holding, 1, depth // TILE, hidden), lambda k: (0, k, 0, 0)),
        ],
        out_specs=pl.BlockSpec((count, hidden), lambda k: (0, 0)),
        out_shape=jax.ShapeDtypeStruct((count, hidden), jnp.bfloat16),
        scratch_shapes=[pltpu.VMEM((count, hidden), jnp.float32)],
        compiler_params=pltpu.CompilerParams(vmem_limit_bytes=VMEM_LIMIT),
        cost_estimate=pl.CostEstimate(
            flops=2 * count * width_in * hidden * holding,
            bytes_accessed=2 * (values.size + count * (width_in + hidden)),
            transcendentals=count * hidden,
        ),
    )(rows, values, wide)


def through_vmem(count, sources, out_at, held, in_sem, out_sem):
    def leave(spot):
        pltpu.make_async_copy(held.at[spot], held.at[spot], in_sem.at[spot]).wait()
        pltpu.make_async_copy(held.at[spot], out_at(spot), out_sem.at[spot]).start()

    def finish(spot):
        pltpu.make_async_copy(held.at[spot], out_at(spot), out_sem.at[spot]).wait()

    for stage in (sources, leave, finish):
        pl.loop(0, count)(stage)


def gather_kernel(index_ref, *refs):
    *source_refs, out_ref, held, in_sem, out_sem = refs

    def start(spot):
        index = index_ref[spot]
        base = 0
        for source_ref in source_refs:
            count = source_ref.shape[0]
            inside = (index >= base) & (index < base + count)
            at = jnp.clip(index - base, 0, count - 1)

            @pl.when(inside)
            def _():
                pltpu.make_async_copy(
                    source_ref.at[at], held.at[spot], in_sem.at[spot]
                ).start()

            base += count

    through_vmem(out_ref.shape[0], start, lambda spot: out_ref.at[spot], held, in_sem, out_sem)


def gather(indices, *sources):
    count = indices.shape[0]
    indices = jnp.clip(indices, 0, sum(source.shape[0] for source in sources) - 1)
    anywhere = pl.BlockSpec(memory_space=pl.ANY)
    out = jax.ShapeDtypeStruct((count,) + sources[0].shape[1:], sources[0].dtype)
    return pl.pallas_call(
        gather_kernel,
        in_specs=[pl.BlockSpec(memory_space=pltpu.SMEM)] + [anywhere] * len(sources),
        out_specs=anywhere,
        out_shape=out,
        scratch_shapes=[
            pltpu.VMEM(out.shape, out.dtype),
            pltpu.SemaphoreType.DMA((count,)),
            pltpu.SemaphoreType.DMA((count,)),
        ],
        compiler_params=pltpu.CompilerParams(vmem_limit_bytes=VMEM_LIMIT),
        cost_estimate=pl.CostEstimate(flops=0, bytes_accessed=4 * out.size, transcendentals=0),
    )(indices, *sources)


def chunk_kernel(first, in_ref, out_ref, held, in_sem, out_sem):
    height = out_ref.shape[2]

    def start(spot):
        pltpu.make_async_copy(
            in_ref.at[:, pl.ds(first + spot * height, height), :], held.at[spot], in_sem.at[spot]
        ).start()

    through_vmem(POOL, start, lambda spot: out_ref.at[spot], held, in_sem, out_sem)


def by_chunk(values, first, height):
    holding, _, hidden = values.shape
    anywhere = pl.BlockSpec(memory_space=pl.ANY)
    out = jax.ShapeDtypeStruct((POOL, holding, height, hidden), values.dtype)
    return pl.pallas_call(
        functools.partial(chunk_kernel, first),
        in_specs=[anywhere],
        out_specs=anywhere,
        out_shape=out,
        scratch_shapes=[
            pltpu.VMEM(out.shape, out.dtype),
            pltpu.SemaphoreType.DMA((POOL,)),
            pltpu.SemaphoreType.DMA((POOL,)),
        ],
        compiler_params=pltpu.CompilerParams(vmem_limit_bytes=VMEM_LIMIT),
        cost_estimate=pl.CostEstimate(
            flops=0, bytes_accessed=4 * out.size, transcendentals=0
        ),
    )(values)


def join_kernel(first, blocks_ref, *refs):
    out_ref, held, in_sem, out_sem = refs[-4:]
    count, height, _ = blocks_ref.shape

    def start(spot):
        pltpu.make_async_copy(blocks_ref.at[spot], held.at[spot], in_sem.at[spot]).start()

    def out_at(spot):
        return out_ref.at[0, pl.ds(first + spot * height, height), :]

    through_vmem(count, start, out_at, held, in_sem, out_sem)


def join(weights, blocks, first, width_in):
    count, _, hidden = blocks.shape
    anywhere = pl.BlockSpec(memory_space=pl.ANY)
    operands = (blocks,) if weights is None else (blocks, weights)
    return pl.pallas_call(
        functools.partial(join_kernel, first),
        in_specs=[anywhere] * len(operands),
        out_specs=anywhere,
        out_shape=jax.ShapeDtypeStruct((1, width_in, hidden), blocks.dtype),
        input_output_aliases={} if weights is None else {1: 0},
        scratch_shapes=[
            pltpu.VMEM(blocks.shape, blocks.dtype),
            pltpu.SemaphoreType.DMA((count,)),
            pltpu.SemaphoreType.DMA((count,)),
        ],
        compiler_params=pltpu.CompilerParams(vmem_limit_bytes=VMEM_LIMIT),
        cost_estimate=pl.CostEstimate(flops=0, bytes_accessed=4 * blocks.size, transcendentals=0),
    )(*operands)


def late_over(count, leave_rows, block, pairs):
    most = POOL - COMMON

    def branch_of(size):
        def branch(leave_rows, block):
            if size == 0:
                return jnp.zeros((most,) + block.shape[1:], block.dtype)
            late = gather(leave_rows[COMMON : COMMON + size], block)
            got = lax.ppermute(late, AXES, pairs)
            return jnp.pad(got, ((0, most - size), (0, 0), (0, 0)))

        return branch

    branches = [branch_of(size) for size in range(most + 1)]
    return lax.switch(jnp.maximum(count - COMMON, 0), branches, leave_rows, block)


def route(experts, replica, place_all, holding):
    pair_count = experts.shape[1]
    device_ids = jnp.arange(place_all.shape[0], dtype=jnp.int32)
    matched = experts[:, :, None] == place_all[None, None, :]
    has_copy = jnp.any(matched, axis=2)
    holder = jnp.sum(jnp.where(matched, device_ids[None, None, :], 0), axis=2)
    use_copy = (replica == 1) & has_copy
    target = jnp.where(use_copy, holder, experts // holding)
    slot_id = jnp.where(use_copy, holding, experts % holding)
    pair_order = jnp.arange(pair_count)
    before = pair_order[:, None] < pair_order[None, :]
    position = jnp.sum((target[:, :, None] == target[:, None, :]) & before[None], axis=1)
    cell = experts % holding * (2 * CAP) + use_copy * CAP + position
    return target, slot_id, position < CAP, cell


def per_device(primary_q, primary_scales, new_place, tokens, experts, replica, route_num):
    holding, width_in, hidden = primary_q.shape
    dev_count = lax.axis_size("dev")
    group_count = lax.axis_size("group")
    device_count = dev_count * group_count
    half = dev_count // 2
    pooled = POOL // half
    my_dev = lax.axis_index("dev")
    my_group = lax.axis_index("group")
    first_dev = my_group * dev_count
    pools = [
        [(base + group) * dev_count + side * half + spot for group in range(pooled) for spot in range(half)]
        for base in range(0, group_count, pooled)
        for side in range(2)
    ]
    over = [
        (group * dev_count + spot, group * dev_count + (spot + half) % dev_count)
        for group in range(group_count)
        for spot in range(dev_count)
    ]

    device_ids = jnp.arange(device_count, dtype=jnp.int32)
    my_id = first_dev + my_dev

    row_count, top_count = experts.shape
    pair_count = row_count * top_count
    scale_cols = primary_scales.size // row_count
    notice = jnp.concatenate(
        [
            experts.astype(jnp.bfloat16),
            replica.astype(jnp.bfloat16),
            primary_scales.reshape(row_count, scale_cols),
        ],
        axis=1,
    )
    notice = jnp.pad(notice, ((0, 0), (0, -notice.shape[1] % TILE)))
    held = jnp.concatenate([tokens, notice], axis=1)
    dev_bits = dev_count.bit_length() - 1
    all_bits = device_count.bit_length() - 1
    order = list(range(dev_bits))[::-1] + list(range(dev_bits, all_bits))[::-1]
    apart = device_ids ^ my_id
    spot_of = sum((apart >> bit & 1) << step for step, bit in enumerate(order))

    def double(held, bits):
        for bit in bits:
            pairs = [(device, device ^ 1 << bit) for device in range(device_count)]
            held = jnp.concatenate([held, lax.ppermute(held, AXES, pairs)], axis=0)
        return held

    first_height, second_height = PARTS
    held = double(held, order[:1])
    first, held = lax.optimization_barrier((by_chunk(primary_q, 0, first_height), held))
    held = double(held, order[1:2])
    place_all = jnp.broadcast_to(new_place.astype(jnp.bfloat16), (device_count, TILE))
    place_all, _ = lax.optimization_barrier((place_all, held))
    held = double(held, order[2:dev_bits])

    place_all = lax.all_to_all(
        place_all,
        AXES,
        split_axis=0,
        concat_axis=0,
        tiled=True,
    )

    place_all = place_all[:, 0].astype(jnp.int32)
    source = place_all // holding
    dest_side = device_ids % dev_count // half
    source_side = source % dev_count // half
    crossing = source_side != dest_side
    source_row = (source // dev_count % pooled * half + source % half) * holding + place_all % holding
    pool_of = device_ids // dev_count // pooled
    peers = (pool_of[:, None] == pool_of[None, :]) & (dest_side[:, None] == dest_side[None, :])
    ahead = peers & crossing[None, :] & (device_ids[None, :] < device_ids[:, None])
    rank = jnp.sum(ahead, axis=1)
    cross_count = jnp.max(jnp.where(crossing, rank + 1, 0))
    my_side = my_dev // half
    my_pool = my_group // pooled
    leaving = (pool_of == my_pool) & (dest_side != my_side) & crossing
    slots = jnp.arange(POOL)
    leave_rows = jnp.sum(
        jnp.where(leaving[None, :] & (rank[None, :] == slots[:, None]), source_row[None, :], 0), axis=1
    )
    staying = (pool_of == my_pool) & (dest_side == my_side)
    place_in_pool = device_ids // dev_count % pooled * half + device_ids % half
    give_rows = jnp.sum(
        jnp.where(
            staying[None, :] & (place_in_pool[None, :] == slots[:, None]),
            jnp.where(crossing, POOL * holding + rank, source_row)[None, :],
            0,
        ),
        axis=1,
    )

    def spread_over(block):
        block = lax.all_to_all(
            block, AXES, split_axis=0, concat_axis=0, tiled=True, axis_index_groups=pools
        )
        return block.reshape((POOL * holding,) + block.shape[2:])

    first, held, place_all, leave_rows, give_rows, cross_count = lax.optimization_barrier(
        (first, held, place_all, leave_rows, give_rows, cross_count)
    )
    first = spread_over(first)
    second = by_chunk(primary_q, POOL * first_height, second_height)
    held, second = lax.optimization_barrier((held, second))
    held = double(held, order[dev_bits:-1])
    held, second = lax.optimization_barrier((held, second))
    second = spread_over(second)

    cells = 2 * CAP
    cell_count = device_count * holding * cells

    def pairs_of(held):
        notices = held[:, width_in:].reshape(device_count, row_count, -1)[spot_of]
        experts_all = notices[:, :, :top_count].astype(jnp.int32)
        replica_all = notices[:, :, top_count : 2 * top_count].astype(jnp.int32)
        return [each.reshape(device_count, pair_count) for each in (experts_all, replica_all)]

    def work(held, place_all, values, scales):
        experts_all, replica_all = pairs_of(held)
        _, _, served, cell = route(experts_all, replica_all, place_all, holding)
        mine = served & (experts_all // holding == my_id)
        cell_ids = jnp.arange(holding * cells)
        hit = mine[:, None, :] & (cell[:, None, :] == cell_ids[None, :, None])
        row_at = spot_of[:, None] * row_count + jnp.sum(
            jnp.where(hit, jnp.arange(pair_count) // top_count, 0), axis=2
        )
        row_at = jnp.where(jnp.any(hit, axis=2), row_at, -1).reshape(cell_count)
        row_hits = row_at[:, None] == jnp.arange(device_count * row_count)[None, :]
        rows = jnp.dot(row_hits.astype(jnp.bfloat16), held, preferred_element_type=jnp.float32)
        return serve(rows.astype(jnp.bfloat16), values, scales)

    sent = gather(leave_rows[:COMMON], first)
    sent, held = lax.optimization_barrier((sent, held))
    common = lax.ppermute(sent, AXES, over)
    held = double(held, order[-1:])
    activated = work(held, place_all, primary_q, primary_scales)
    leave_rows, activated = lax.optimization_barrier((leave_rows, activated))

    columns = dev_count // ROW_CHIPS

    def exchange(blocks, axis, mine, stride, within):
        got = [lax.dynamic_index_in_dim(blocks, mine, axis, keepdims=False)]
        for step in range(1, blocks.shape[axis]):
            pairs = [
                (device, device ^ step * stride) for device in range(device_count)
            ]
            block = lax.dynamic_index_in_dim(blocks, mine ^ step, axis, keepdims=False)
            got.append(lax.ppermute(block, AXES, pairs))
        return jnp.stack(got, axis=within)

    blocks = activated.reshape(group_count, ROW_CHIPS, columns, holding * cells, hidden)
    blocks = exchange(blocks, 1, my_dev // columns, columns, 1)
    late = late_over(cross_count, leave_rows, first, over)
    leave_rows, late = lax.optimization_barrier((leave_rows, late))
    sent = gather(leave_rows[:COMMON], second)
    sent, blocks = lax.optimization_barrier((sent, blocks))
    give_rows, _ = lax.optimization_barrier((give_rows, sent))
    first = gather(give_rows, first, common, late)
    common = lax.ppermute(sent, AXES, over)
    blocks = exchange(blocks, 2, my_dev % columns, 1, 1)
    returned = exchange(blocks, 0, my_group, dev_count, 0)
    leave_rows, returned = lax.optimization_barrier((leave_rows, returned))
    first = lax.all_to_all(
        first, AXES, split_axis=0, concat_axis=0, tiled=True, axis_index_groups=pools
    )
    late = late_over(cross_count, leave_rows, second, over)
    second = gather(give_rows, second, common, late)
    second, held = lax.optimization_barrier((second, held))
    second = lax.all_to_all(
        second, AXES, split_axis=0, concat_axis=0, tiled=True, axis_index_groups=pools
    )
    new_weights = join(None, first, 0, width_in)
    new_weights = join(new_weights, second, first.shape[0] * first.shape[1], width_in)

    experts_all, replica_all = pairs_of(held)
    target, slot_id, served, _ = route(experts_all, replica_all, place_all, holding)
    arriving = served & (target == my_id)
    slot_load = jnp.stack(
        [jnp.sum((arriving & (slot_id == slot)).astype(jnp.int32)) for slot in range(holding + 1)]
    )[None]
    owner_notice = held[:, width_in:].reshape(device_count, row_count, -1)
    owner_notice = lax.dynamic_index_in_dim(
        owner_notice, spot_of[new_place[0] // holding], 0, keepdims=False
    )
    owner_scales = owner_notice[:, 2 * top_count : 2 * top_count + scale_cols]
    new_scales = lax.dynamic_index_in_dim(
        owner_scales.reshape(primary_scales.shape), new_place[0] % holding, 0
    )

    my_experts = experts.reshape(1, pair_count)
    _, _, my_served, my_cell = route(
        my_experts, replica.reshape(1, pair_count), place_all, holding
    )
    their_id = my_experts // holding
    apart = their_id ^ my_id
    block_at = apart // dev_count * columns + apart % columns
    block_at = block_at * ROW_CHIPS + apart % dev_count // columns
    my_cell = (block_at * (holding * cells) + my_cell)[0]
    placed = (my_cell[:, None] == jnp.arange(cell_count)[None, :]) & my_served[0][:, None]
    selected = jnp.dot(
        placed.astype(jnp.bfloat16),
        returned.reshape(cell_count, hidden),
        preferred_element_type=jnp.float32,
    )
    weight = route_num.reshape(pair_count).astype(jnp.float32) / 16.0
    hidden_out = (selected * weight[:, None]).astype(jnp.bfloat16)
    hidden_out = hidden_out.reshape(row_count, top_count, hidden)
    return (new_weights, new_scales, hidden_out, slot_load)


def solution(mesh):
    in_specs = (
        P(AXES, None, None),
        P(AXES, None, None),
        P(AXES),
        P(AXES, None),
        P(AXES, None),
        P(AXES, None),
        P(AXES, None),
    )
    out_specs = (
        P(AXES, None, None),
        P(AXES, None, None),
        P(AXES, None, None),
        P(AXES, None),
    )
    return jax.shard_map(
        per_device, mesh=mesh, in_specs=in_specs, out_specs=out_specs, check_vma=False
    )
```
